32 devices in a mesh: dp: 4 (over z), fsdp: 8 (over y, x, core).
Axes of the slice: x: 2, y: 2, z: 4, core: 2. Of those that a mesh axis runs over, the one named last changes fastest.
Arguments:
- activations: bfloat16 [64, 256, 1024], P(('dp', 'fsdp')), may hold values from -6 to 6
- lengths: int32 [64, 4], P(('dp', 'fsdp')), may hold values from 1 to 128, 256 in all within a row
- cotangent: bfloat16 [64, 256, 1024], P(('dp', 'fsdp')), may hold values from -8 to 8
- gain_first: float32 [1024], replicated, may hold values from 0.5 to 1.5
- shift_first: float32 [1024], replicated, may hold values from -1 to 1
- triple_weight: bfloat16 [1024, 3072], P('fsdp', 'dp'), may hold values from -0.1875 to 0.1875
- output_weight: bfloat16 [1024, 1024], P('fsdp', 'dp'), may hold values from -0.5 to 0.5
- output_bias: float32 [1024], replicated, may hold values from -1.5 to 1.5
- gain_second: float32 [1024], replicated, may hold values from 0.5 to 1.5
- shift_second: float32 [1024], replicated, may hold values from -1 to 1
- upward_weight: bfloat16 [1024, 4096], P('fsdp', 'dp'), may hold values from -0.1875 to 0.1875
- upward_bias: float32 [4096], replicated, may hold values from -1.5 to 1.5
- downward_weight: bfloat16 [4096, 1024], P('fsdp', 'dp'), may hold values from -0.09375 to 0.09375
- downward_bias: float32 [1024], replicated, may hold values from -1.5 to 1.5
- prefix_table: bfloat16 [10, 1024], replicated, may hold values from -5 to 5
- inner_weight: bfloat16 [1024, 512], replicated, may hold values from -0.1875 to 0.1875
- inner_bias: float32 [512], replicated, may hold values from -1.5 to 1.5
- outer_weight: bfloat16 [512, 2048], replicated, may hold values from -0.25 to 0.25
- outer_bias: float32 [2048], replicated, may hold values from -1.5 to 1.5
Outputs:
- block_output: bfloat16 [64, 256, 1024], P(('dp', 'fsdp'))
- input_grad: bfloat16 [64, 256, 1024], P(('dp', 'fsdp'))
- table_grad: float32 [10, 1024], replicated
- inner_weight_grad: float32 [1024, 512], replicated
- inner_bias_grad: float32 [512], replicated
- outer_weight_grad: float32 [512, 2048], replicated
- outer_bias_grad: float32 [2048], replicated
The draws below stay inside these ranges and needn't reach their ends.
Inputs may be any that keep to these rules, and one draw needn't show every extreme that they name: The 4 lengths of a row sum to 256, and some row's longest document has exactly 128 tokens.
All inputs are finite; a program needn't handle non-finite values.
Results may differ from the reference program's by a relative error of at most 0.011.
Values may be sent and summed in bfloat16 or wider, within the bound.
No kernel may reach another device: no remote copies, remote signals or barrier semaphores. Data moves between devices by JAX's collectives and lax.ppermute only.
A program may use at most 192 MiB of HBM per device.

```python
import math
import jax
import jax.numpy as jnp
import numpy as np
from jax import lax

D = 1024
HEADS = 16
HEAD = 64
FF = 4096
MID = 512
PREFIX = 10
SEQ = 256
SEGS = 4
ROWS = 64


def draw_cotangent(key, part):
    key = jax.random.fold_in(key, 7)
    places = jnp.arange(ROWS, dtype=jnp.float32) / ROWS
    base = jnp.clip(jax.random.normal(key, (ROWS, SEQ, D), jnp.float32), -4.0, 4.0)
    rising = 0.6 * jnp.exp(places * math.log(3.0))
    return (base * rising[:, None, None]).astype(jnp.bfloat16)


def block_scale(own_key, shape, cuts, least, high):
    def one(dim, parts):
        draws = jax.random.uniform(jax.random.fold_in(jax.random.fold_in(own_key, 6), dim), (parts,), jnp.float32, least / len(cuts), high / len(cuts))
        return jnp.repeat(jnp.exp(draws), shape[dim] // parts).reshape((-1,) + (1,) * (len(shape) - dim - 1))

    level = one(*cuts[0])
    for cut in cuts[1:]:
        level = level * one(*cut)
    return level


def split_up(count, total, reach, slope):
    portions = [(1 << 20) // math.isqrt(grade ** slope) + 1 for grade in range(2, count + 1)]
    surplus, counts = total - reach - (count - 1), [1] * (count - 1)
    while surplus > 0:
        movable = [i for i in range(count - 1) if counts[i] < reach]
        pool, remaining = sum([portions[i] for i in movable]), surplus
        for i in movable:
            more = min(reach - counts[i], max(1, remaining * portions[i] // pool), surplus)
            counts[i] = counts[i] + more
            surplus = surplus - more
    return np.array([reach] + counts)


def uneven(key, number_of, total, limit, skew):
    if number_of == 2:
        one = jax.random.randint(key, (), max(1, total - limit), min(limit, total - 1) + 1)
        return jnp.stack([one, total - one])
    sizes = jnp.asarray(split_up(number_of, total, limit, skew), jnp.int32)
    twos = (number_of - 1) // 2
    giver, sink = sizes[1:1 + 2 * twos:2], sizes[2:2 + 2 * twos:2]
    margin = jnp.minimum(giver - 1, limit - sink)
    passed = jax.random.randint(jax.random.fold_in(key, 1), (twos,), 0, 1 << 20) % (margin + 1)
    sizes = sizes.at[1:1 + 2 * twos:2].set(giver - passed).at[2:2 + 2 * twos:2].set(sink + passed)
    return sizes[jax.random.permutation(jax.random.fold_in(key, 2), number_of)]


def gaussian(stream_key, extent, width, limit, cuts=(), kind=jnp.bfloat16):
    entries = jax.random.normal(stream_key, extent, jnp.float32) * width
    if len(cuts) > 0:
        entries = block_scale(stream_key, extent, cuts, -0.22, 0.18) * entries
    return jnp.clip(entries, min=-limit, max=limit).astype(kind)


def setup_inputs(seed: int = 0) -> dict:
    splits = jax.random.split(jax.random.key(seed), 20)
    activations = gaussian(splits[0], (ROWS, SEQ, D), 1.0, 6.0, ((0, 32),))
    lengths = jax.vmap(lambda own: uneven(own, SEGS, SEQ, SEQ // 2, 1))(jax.random.split(splits[1], ROWS)).reshape((ROWS, SEGS)).astype(jnp.int32)
    cotangent = draw_cotangent(jax.random.fold_in(splits[19], 71), 0)
    gain_first = jnp.clip(1.0 + 0.1 * jax.random.normal(splits[3], (D,), jnp.float32), 0.5, 1.5)
    shift_first = gaussian(splits[4], (D,), 0.2, 1.0, (), jnp.float32)
    triple_weight = gaussian(splits[5], (D, 3 * D), D ** -0.5, 0.1875, ((0, 8), (1, 4)))
    output_weight = gaussian(splits[6], (D, D), (D // 8) ** -0.5, 0.5, ((0, 8), (1, 4)))
    output_bias = gaussian(splits[7], (D,), 0.3, 1.5, (), jnp.float32)
    gain_second = jnp.clip(1.0 + 0.1 * jax.random.normal(splits[8], (D,), jnp.float32), 0.5, 1.5)
    shift_second = gaussian(splits[9], (D,), 0.2, 1.0, (), jnp.float32)
    upward_weight = gaussian(splits[10], (D, FF), D ** -0.5, 0.1875, ((0, 8), (1, 4)))
    upward_bias = gaussian(splits[11], (FF,), 0.3, 1.5, (), jnp.float32)
    downward_weight = gaussian(splits[12], (FF, D), FF ** -0.5, 0.09375, ((0, 8), (1, 4)))
    downward_bias = gaussian(splits[13], (D,), 0.3, 1.5, (), jnp.float32)
    prefix_table = gaussian(splits[14], (PREFIX, D), 1.0, 5.0)
    inner_weight = gaussian(splits[15], (D, MID), D ** -0.5, 0.1875)
    inner_bias = gaussian(splits[16], (MID,), 0.3, 1.5, (), jnp.float32)
    outer_weight = gaussian(splits[17], (MID, 2 * D), MID ** -0.5, 0.25)
    outer_bias = gaussian(splits[18], (2 * D,), 0.3, 1.5, (), jnp.float32)
    return {"activations": activations, "lengths": lengths, "cotangent": cotangent, "gain_first": gain_first, "shift_first": shift_first, "triple_weight": triple_weight, "output_weight": output_weight, "output_bias": output_bias, "gain_second": gain_second, "shift_second": shift_second, "upward_weight": upward_weight, "upward_bias": upward_bias, "downward_weight": downward_weight, "downward_bias": downward_bias, "prefix_table": prefix_table, "inner_weight": inner_weight, "inner_bias": inner_bias, "outer_weight": outer_weight, "outer_bias": outer_bias}


@jax.custom_vjp
def low(v):
    return lax.optimization_barrier(v.astype(jnp.bfloat16)).astype(jnp.float32)

@jax.custom_vjp
def low_back(v):
    return v

def low_keep(v):
    return (low(v), None)

def low_pass(kept, grad):
    return (grad,)

def back_keep(v):
    return (v, None)

def back_low(kept, grad):
    return (low(grad),)
low.defvjp(low_keep, low_pass)
low_back.defvjp(back_keep, back_low)
HIGHEST = lax.Precision.HIGHEST

def normalize(values, scaling, offset):
    center = values - lax.optimization_barrier(jnp.mean(values, axis=-1, keepdims=True))
    spread = lax.optimization_barrier(jnp.mean(center * center, axis=-1, keepdims=True))
    return center * lax.rsqrt(spread + 1e-05) * scaling + offset

def segment_of(lengths_row):
    bounds = jnp.cumsum(lengths_row)
    places = jnp.arange(SEQ, dtype=jnp.int32)
    return lax.optimization_barrier(jnp.sum((places[:, None] >= bounds[None, :]).astype(jnp.int32), axis=1))

def block_rows(packed, segment, prefix_keys, prefix_values, frozen):
    gain_one, shift_one, triple_w, output_w, output_b, gain_two, shift_two, upward_w, upward_b, downward_w, downward_b = frozen
    group_size = packed.shape[0]
    first_norm = low(normalize(packed, gain_one, shift_one))
    triple = low_back(low(jnp.einsum('gtd,de->gte', first_norm, triple_w, precision=HIGHEST)))
    queries = triple[..., :D].reshape(group_size, SEQ, HEADS, HEAD)
    keys_all = jnp.concatenate([jnp.broadcast_to(prefix_keys, (group_size, PREFIX, HEADS, HEAD)), triple[..., D:2 * D].reshape(group_size, SEQ, HEADS, HEAD)], axis=1)
    values_all = jnp.concatenate([jnp.broadcast_to(prefix_values, (group_size, PREFIX, HEADS, HEAD)), triple[..., 2 * D:].reshape(group_size, SEQ, HEADS, HEAD)], axis=1)
    scores = low_back(jnp.einsum('gqhe,gkhe->ghqk', queries, keys_all, precision=HIGHEST) * HEAD ** (-0.5))
    places = jnp.arange(SEQ, dtype=jnp.int32)
    causal = places[:, None] >= places[None, :]
    within = (segment[:, :, None] == segment[:, None, :]) & causal[None]
    visible = jnp.concatenate([jnp.ones((group_size, SEQ, PREFIX), jnp.int32) > 0, within], axis=2)
    scores = jnp.where(visible[:, None], scores, -1e+30)
    attention = low(jax.nn.softmax(scores, axis=-1))
    mixture = low_back(low(jnp.einsum('ghqk,gkhe->gqhe', attention, values_all, precision=HIGHEST)))
    mixture = mixture.reshape(group_size, SEQ, D)
    attended = low_back(jnp.einsum('gtd,de->gte', mixture, output_w, precision=HIGHEST) + output_b)
    middle = packed + attended
    second = low(normalize(middle, gain_two, shift_two))
    upward = low_back(jnp.einsum('gtd,df->gtf', second, upward_w, precision=HIGHEST) + upward_b)
    active = low(jax.nn.gelu(upward, approximate=True))
    lower_out = low_back(jnp.einsum('gtf,fd->gtd', active, downward_w, precision=HIGHEST) + downward_b)
    return middle + lower_out

def forward(packed, table_rows, first_weight, first_bias, second_weight, second_bias, segments, frozen):
    hidden = jnp.tanh(jnp.dot(table_rows, first_weight, precision=HIGHEST) + first_bias)
    prefix_pairs = low(jnp.dot(low(hidden), second_weight, precision=HIGHEST) + second_bias)
    prefix_keys = prefix_pairs[:, :D].reshape(PREFIX, HEADS, HEAD)
    prefix_values = prefix_pairs[:, D:].reshape(PREFIX, HEADS, HEAD)
    per_group = math.gcd(ROWS, 8)
    stacked = packed.reshape(ROWS // per_group, per_group, SEQ, D)
    segment_stack = segments.reshape(ROWS // per_group, per_group, SEQ)

    def apply_group(element):
        return block_rows(element[0], element[1], prefix_keys, prefix_values, frozen)
    results = lax.map(jax.checkpoint(apply_group), (stacked, segment_stack))
    return results.reshape(ROWS, SEQ, D)

def reference(activations, lengths, cotangent, gain_first, shift_first, triple_weight, output_weight, output_bias, gain_second, shift_second, upward_weight, upward_bias, downward_weight, downward_bias, prefix_table, inner_weight, inner_bias, outer_weight, outer_bias):
    frozen = tuple((member.astype(jnp.float32) for member in (gain_first, shift_first, triple_weight, output_weight, output_bias, gain_second, shift_second, upward_weight, upward_bias, downward_weight, downward_bias)))
    segments = jax.vmap(segment_of)(lengths)

    def whole_layer(packed, table_rows, first_weight, first_bias, second_weight, second_bias):
        return forward(packed, table_rows, first_weight, first_bias, second_weight, second_bias, segments, frozen)
    outputs, pullback = jax.vjp(whole_layer, activations.astype(jnp.float32), prefix_table.astype(jnp.float32), inner_weight.astype(jnp.float32), inner_bias.astype(jnp.float32), outer_weight.astype(jnp.float32), outer_bias.astype(jnp.float32))
    gradients = pullback(cotangent.astype(jnp.float32))
    return (outputs.astype(jnp.bfloat16), gradients[0].astype(jnp.bfloat16), gradients[1], gradients[2], gradients[3], gradients[4], gradients[5])
```

```python
from functools import partial

import jax
import jax.numpy as jnp
from jax import lax
from jax.experimental import pallas as pl
from jax.experimental.pallas import tpu as pltpu
from jax.sharding import PartitionSpec as P

HEAD = 64
PAD = 16
MASKED = -1e30
F32 = jnp.float32
BF16 = jnp.bfloat16
GELU_C = 0.7978845608028654
GELU_A = 0.044715

ANY = pl.BlockSpec(memory_space=pl.ANY)
VMEM = pl.BlockSpec(memory_space=pltpu.VMEM)
SMEM = pl.BlockSpec(memory_space=pltpu.SMEM)


def dot(a, b):
    return lax.dot_general(a, b, (((1,), (0,)), ((), ())), preferred_element_type=F32)


def dot_nt(a, b):
    return lax.dot_general(a, b, (((1,), (1,)), ((), ())), preferred_element_type=F32)


def dot_tn(a, b):
    return lax.dot_general(a, b, (((0,), (0,)), ((), ())), preferred_element_type=F32)


def unit(values):
    center = values - jnp.mean(values, axis=-1, keepdims=True)
    scaled = lax.rsqrt(jnp.mean(center * center, axis=-1, keepdims=True) + 1e-05)
    return center * scaled, scaled


def norm_back(upstream, unit_rows, scaled):
    return scaled * (
        upstream
        - jnp.mean(upstream, axis=-1, keepdims=True)
        - unit_rows * jnp.mean(upstream * unit_rows, axis=-1, keepdims=True)
    )


def call(body, name, outs, ins, scratch, flops, bytes_accessed, vmem=56):
    return pl.pallas_call(
        body,
        name=name,
        out_shape=[o[0] for o in outs],
        out_specs=[o[1] for o in outs],
        in_specs=ins,
        scratch_shapes=scratch,
        compiler_params=pltpu.CompilerParams(vmem_limit_bytes=vmem * 1024 * 1024),
        cost_estimate=pl.CostEstimate(
            flops=flops, bytes_accessed=bytes_accessed, transcendentals=0
        ),
    )


def shaped(shape, dtype):
    return jax.ShapeDtypeStruct(shape, dtype)


class Pieces:
    def __init__(self, fsdp, dp, shard_rows, shard_cols):
        self.fsdp, self.dp = fsdp, dp
        self.shard_rows, self.shard_cols = shard_rows, shard_cols
        self.parts = []

    def whole(self, key):
        self.parts.append((key, None, None, None, None, None, None))
        return self

    def add(self, key, first, count, flip, planes, col):
        rows = self.shard_rows
        for k, plane in enumerate(planes):
            low, high = max(first, k * rows), min(first + count, (k + 1) * rows)
            if low < high:
                self.parts.append((key, low - first, high - low, flip, plane, low - k * rows, col))

    def copies(self, refs, dst, sems, base, place, only=None):
        out = []
        for key, src_row, count, flip, plane, shard_row, col in self.parts:
            if flip is None:
                out.append(pltpu.make_async_copy(refs[key], dst, sems.at[base + len(out)]))
                continue
            if only is not None and flip >> 1 != only:
                continue
            owner = jnp.bitwise_xor(place[1], flip)
            if only is not None:
                owner = jnp.bitwise_and(owner, 1)
            row = pl.multiple_of(owner * self.shard_rows + shard_row, 16)
            across = lax.rem(place[0] + plane, self.dp)
            column = pl.multiple_of(across * self.shard_cols, 128)
            out.append(
                pltpu.make_async_copy(
                    refs[key].at[pl.ds(src_row, count), pl.ds(col, self.shard_cols)],
                    dst.at[pl.ds(row, count), pl.ds(column, self.shard_cols)],
                    sems.at[base + len(out)],
                )
            )
        return out


def start(copies):
    for c in copies:
        c.start()


def wait(copies):
    for c in copies:
        c.wait()


def flip(value, mask, size):
    return lax.ppermute(value, "fsdp", [(i, i ^ mask) for i in range(size)])


def spread(stack, size):
    half = stack.shape[0] // 2
    along_x = flip(stack, 2, size)
    along_y = flip(stack, 4, size)
    diag_x = flip(along_y[:half], 2, size)
    diag_y = flip(along_x[half:], 4, size)
    lane = [stack, along_x, along_y, diag_x, diag_y]
    return lane + [flip(a, 1, size) for a in lane]


def add_spread(pieces, keys, planes, col):
    total = pieces.shard_rows * len(planes)
    half = total // 2
    for core in (0, 1):
        own, along_x, along_y, diag_x, diag_y = keys[5 * core : 5 * core + 5]
        pieces.add(own, 0, total, core, planes, col)
        pieces.add(along_x, 0, total, 2 | core, planes, col)
        pieces.add(along_y, 0, total, 4 | core, planes, col)
        pieces.add(diag_x, 0, half, 6 | core, planes, col)
        pieces.add(diag_y, half, total - half, 6 | core, planes, col)


def foreign(value, dp, place_z):
    planes = lax.all_gather(value, "dp", axis=0, tiled=False)
    rows = [
        lax.dynamic_index_in_dim(planes, lax.rem(place_z + j, dp), 0, keepdims=False)
        for j in range(1, dp)
    ]
    return jnp.concatenate(rows, axis=0)


def collect(triple_w, output_w, upward_w, downward_w, fsdp, dp):
    if fsdp != 8 or dp < 2:
        out = []
        for w in (triple_w, output_w, upward_w, downward_w):
            rows = lax.all_gather(w, "fsdp", axis=0, tiled=True)
            full = lax.all_gather(rows, "dp", axis=1, tiled=True)
            pieces = Pieces(fsdp, dp, w.shape[0], w.shape[1]).whole(0)
            out.append(([full], pieces))
        (t, tp), (o, op), u, d = out
        op = Pieces(fsdp, dp, output_w.shape[0], output_w.shape[1]).whole(1)
        return ([t[0], o[0]], tp, op), u, d
    place_z = lax.axis_index("dp")
    triple_c, output_c, upward_c = (w.shape[1] for w in (triple_w, output_w, upward_w))
    first = jnp.concatenate([triple_w, output_w], axis=1)
    first_far = foreign(first, dp, place_z)
    upward_far = foreign(upward_w, dp, place_z)
    downward_far = foreign(downward_w, dp, place_z)
    near = jnp.concatenate([triple_w, output_w, upward_w], axis=1)
    near_all = spread(near, fsdp)
    down_near = spread(downward_w, fsdp)
    first_all = spread(first_far, fsdp)
    upward_all = spread(upward_far, fsdp)
    downward_all = spread(downward_far, fsdp)
    far = list(range(1, dp))

    def pieces(w, near_col, far_col):
        p = Pieces(fsdp, dp, w.shape[0], w.shape[1])
        add_spread(p, list(range(10)), [0], near_col)
        add_spread(p, list(range(10, 20)), far, far_col)
        return p

    return (
        (near_all + first_all, pieces(triple_w, 0, 0), pieces(output_w, triple_c, triple_c)),
        (near_all + upward_all, pieces(upward_w, triple_c + output_c, 0)),
        (down_near + downward_all, pieces(downward_w, 0, 0)),
    )


def prefix_body(prefix, table, inner_w, inner_b, outer_w, outer_b, hidden_o, keys_o, values_o, ones_o):
    width = keys_o.shape[1]
    hidden = jnp.tanh(dot(table[...], inner_w[...]) + inner_b[...])
    hidden_o[...] = hidden
    pairs = (dot(hidden.astype(BF16), outer_w[...]) + outer_b[...]).astype(BF16).astype(F32)
    shape = keys_o.shape
    row = lax.broadcasted_iota(jnp.int32, shape, 0)
    col = lax.broadcasted_iota(jnp.int32, shape, 1)
    inside = (row // PAD) == (col // HEAD)
    real = inside & (lax.rem(row, PAD) < prefix)
    heads = shape[0] // PAD
    keys_o[...] = jnp.where(real, jnp.tile(pairs[:, :width], (heads, 1)), 0.0).astype(BF16)
    values_o[...] = jnp.where(real, jnp.tile(pairs[:, width:], (heads, 1)), 0.0).astype(BF16)
    ones_o[...] = jnp.where(inside, 1.0, 0.0).astype(BF16)


def attend_body(rows, prefix, parts_t, parts_o, n_arrays, *refs):
    place, lengths, x, gain1, shift1, out_b, gain2, shift2, bdk, bdv = refs[:10]
    arrays = refs[10 : 10 + n_arrays]
    triple_o, prob_o, pre_o, mix_o, middle_o, norm_o, t_o, o_o = refs[10 + n_arrays : 18 + n_arrays]
    (tv, ov, normed, tri, prob, bias, spre, pre, main, mix, middle, sems, out_sems) = refs[
        18 + n_arrays :
    ]
    tokens, width = x.shape
    length = tokens // rows
    heads = width // HEAD
    scale = HEAD ** (-0.5)
    in_t = parts_t.copies(arrays, tv, sems, 0, place)
    in_o = parts_o.copies(arrays, ov, sems, len(in_t), place)
    start(in_t)
    start(in_o)
    step = 128
    for t in range(0, tokens, step):
        u, _ = unit(x[t : t + step, :].astype(F32))
        normed[t : t + step, :] = (u * gain1[...] + shift1[...]).astype(BF16)
    wait(in_t)
    outs = [pltpu.make_async_copy(tv, t_o, out_sems.at[0])]
    outs[0].start()

    def triple_block(n, carry):
        cols = pl.ds(pl.multiple_of(n * 512, 512), 512)
        tri[:, cols] = dot(normed[...], tv[:, cols]).astype(BF16)
        return carry

    lax.fori_loop(0, 3 * width // 512, triple_block, 0)
    outs.append(pltpu.make_async_copy(tri, triple_o, out_sems.at[1]))
    outs[1].start()

    lane = lax.broadcasted_iota(jnp.int32, (length, 2 * HEAD), 1)
    low_lane = lane < HEAD
    for row in range(rows):
        here = slice(row * length, (row + 1) * length)
        key = lax.broadcasted_iota(jnp.int32, (length, length), 0)
        query = lax.broadcasted_iota(jnp.int32, (length, length), 1)
        key_seg = jnp.zeros((length, length), jnp.int32)
        query_seg = jnp.zeros((length, length), jnp.int32)
        bound = 0
        for s in range(lengths.shape[1]):
            bound = bound + lengths[row, s]
            key_seg = key_seg + jnp.where(key >= bound, 1, 0)
            query_seg = query_seg + jnp.where(query >= bound, 1, 0)
        seen = (key_seg == query_seg) & (key <= query)
        bias[...] = jnp.where(seen, 0.0, MASKED)
        raw = dot_nt(bdk[...], tri[here, :width]) * scale
        pre_row = lax.broadcasted_iota(jnp.int32, raw.shape, 0)
        spre[...] = jnp.where(lax.rem(pre_row, PAD) < prefix, raw, MASKED)

        def pair(i, carry):
            cols = pl.multiple_of(i * 2 * HEAD, 2 * HEAD)
            q = tri[here, pl.ds(cols, 2 * HEAD)]
            k = tri[here, pl.ds(pl.multiple_of(width + cols, 2 * HEAD), 2 * HEAD)]
            v = tri[here, pl.ds(pl.multiple_of(2 * width + cols, 2 * HEAD), 2 * HEAD)]
            vt = v.T
            found = []
            for sub in (0, 1):
                qm = jnp.where(low_lane if sub == 0 else ~low_lane, q, jnp.zeros_like(q))
                s = dot_nt(k, qm) * scale + bias[...]
                at = pl.multiple_of((2 * i + sub) * PAD, PAD)
                sp = spre[pl.ds(at, PAD), :]
                top = jnp.maximum(
                    jnp.max(s, axis=0, keepdims=True), jnp.max(sp, axis=0, keepdims=True)
                )
                e = jnp.exp(s - top)
                ep = jnp.exp(sp - top)
                inverse = 1.0 / (
                    jnp.sum(e, axis=0, keepdims=True) + jnp.sum(ep, axis=0, keepdims=True)
                )
                p = (e * inverse).astype(BF16)
                prob[row * heads + 2 * i + sub] = p
                pre[row, pl.ds(at, PAD), :] = (ep * inverse).astype(BF16)
                found.append(dot(vt[sub * HEAD : (sub + 1) * HEAD, :], p))
            main[:, pl.ds(cols, 2 * HEAD)] = jnp.concatenate(found, axis=0).T
            return carry

        lax.fori_loop(0, heads // 2, pair, 0)
        outs.append(
            pltpu.make_async_copy(
                prob.at[pl.ds(row * heads, heads)],
                prob_o.at[pl.ds(row * heads, heads)],
                out_sems.at[len(outs)],
            )
        )
        outs[-1].start()
        mix[here, :] = (main[...] + dot_tn(pre[row], bdv[...])).astype(BF16)

    outs.append(pltpu.make_async_copy(pre, pre_o, out_sems.at[len(outs)]))
    outs[-1].start()
    outs.append(pltpu.make_async_copy(mix, mix_o, out_sems.at[len(outs)]))
    outs[-1].start()
    wait(in_o)
    outs.append(pltpu.make_async_copy(ov, o_o, out_sems.at[len(outs)]))
    outs[-1].start()

    def project(n, carry):
        cols = pl.ds(pl.multiple_of(n * 512, 512), 512)
        middle[:, cols] = (
            x[:, cols].astype(F32) + dot(mix[...], ov[:, cols]) + out_b[:, cols]
        )
        return carry

    lax.fori_loop(0, width // 512, project, 0)
    outs.append(pltpu.make_async_copy(middle, middle_o, out_sems.at[len(outs)]))
    outs[-1].start()
    for t in range(0, tokens, step):
        u, _ = unit(middle[t : t + step, :])
        normed[t : t + step, :] = (u * gain2[...] + shift2[...]).astype(BF16)
    outs.append(pltpu.make_async_copy(normed, norm_o, out_sems.at[len(outs)]))
    outs[-1].start()
    wait(outs)


def upward_body(parts, n_arrays, *refs):
    place, norm, bias = refs[:3]
    arrays = refs[3 : 3 + n_arrays]
    active_o, slope_o, up_o = refs[3 + n_arrays : 6 + n_arrays]
    uv, active, slope, sems, out_sems = refs[6 + n_arrays :]
    inward = parts.copies(arrays, uv, sems, 0, place)
    start(inward)
    wait(inward)
    out = pltpu.make_async_copy(uv, up_o, out_sems.at[0])
    out.start()
    block = 512

    def step(n, carry):
        cols = pl.ds(pl.multiple_of(n * block, block), block)
        u = dot(norm[...], uv[:, cols]) + bias[:, cols]
        square = u * u
        t = jnp.tanh(GELU_C * u * (1.0 + GELU_A * square))
        half = 0.5 * (1.0 + t)
        active[:, cols] = (u * half).astype(BF16)
        slope[:, cols] = (
            half + 0.5 * u * (1.0 - t * t) * (GELU_C + 3.0 * GELU_C * GELU_A * square)
        ).astype(BF16)
        return carry

    lax.fori_loop(0, uv.shape[1] // block, step, 0)
    done = [
        pltpu.make_async_copy(active, active_o, out_sems.at[1]),
        pltpu.make_async_copy(slope, slope_o, out_sems.at[2]),
    ]
    start(done)
    out.wait()
    wait(done)


def chunk_start(place, pick, parts, arrays, full, dv, uc, ac, sc, sems, base):
    active, slope, upward = full
    size = uc.shape[1]
    chunk = jnp.bitwise_xor(lax.shift_right_logical(place[1], 1), pick)
    cols = pl.ds(pl.multiple_of(chunk * size, size), size)
    if parts.parts[0][3] is None:
        down = [
            pltpu.make_async_copy(
                arrays[0].at[pl.ds(pl.multiple_of(chunk * size, size), size), :],
                dv,
                sems.at[base],
            )
        ]
    else:
        down = parts.copies(arrays, dv, sems, base, place, only=pick)
    base += len(down)
    rest = [
        pltpu.make_async_copy(slope.at[:, cols], sc, sems.at[base]),
        pltpu.make_async_copy(upward.at[:, cols], uc, sems.at[base + 1]),
        pltpu.make_async_copy(active.at[:, cols], ac, sems.at[base + 2]),
    ]
    start(rest[:1])
    start(down)
    start(rest[1:])
    return down, rest


def chunk_work(g, down, rest, dv, uc, ac, sc, gu, second, out, fresh):
    size = uc.shape[1]
    width = second.shape[1]
    wait(down)
    rest[0].wait()

    def upstream(n, carry):
        cols = pl.ds(pl.multiple_of(n * 512, 512), 512)
        gu[:, cols] = (dot_nt(g[...], dv[cols, :]) * sc[:, cols].astype(F32)).astype(BF16)
        return carry

    lax.fori_loop(0, size // 512, upstream, 0)
    rest[1].wait()

    def back(n, carry):
        cols = pl.ds(pl.multiple_of(n * 512, 512), 512)
        value = dot_nt(gu[...], uc[cols, :])
        second[:, cols] = value if fresh else second[:, cols] + value
        return carry

    lax.fori_loop(0, width // 512, back, 0)
    rest[2].wait()

    def ahead(n, carry):
        cols = pl.ds(pl.multiple_of(n * 512, 512), 512)
        value = dot(ac[...], dv[:, cols])
        out[:, cols] = value if fresh else out[:, cols] + value
        return carry

    lax.fori_loop(0, width // 512, ahead, 0)


def chunk_body(picks, first, parts, n_arrays, *refs):
    place, g, active, slope, upward = refs[:5]
    arrays = refs[5 : 5 + n_arrays]
    rest = refs[5 + n_arrays :]
    if not first:
        second_i, out_i = rest[:2]
        rest = rest[2:]
    second_o, out_o, dv, uc, ac, sc, gu, second, out, sems, io_sems = rest
    if not first:
        carried = [
            pltpu.make_async_copy(second_i, second, io_sems.at[0]),
            pltpu.make_async_copy(out_i, out, io_sems.at[1]),
        ]
        start(carried)
    for k, pick in enumerate(picks):
        down, more = chunk_start(
            place, pick, parts, arrays, (active, slope, upward), dv, uc, ac, sc, sems, 0
        )
        if not first and k == 0:
            wait(carried)
        chunk_work(g, down, more, dv, uc, ac, sc, gu, second, out, first and k == 0)
    done = [
        pltpu.make_async_copy(second, second_o, io_sems.at[2]),
        pltpu.make_async_copy(out, out_o, io_sems.at[3]),
    ]
    start(done)
    wait(done)


def middle_body(rows, picks, parts, n_arrays, *refs):
    place, g, active, slope, upward = refs[:5]
    arrays = refs[5 : 5 + n_arrays]
    second_i, out_i, middle_i, gain2, down_b, output_w, mix, triple, pre, bdv, ones = refs[
        5 + n_arrays : 16 + n_arrays
    ]
    result_o, gmid_o, gmix_o, delta_o, dspre_o, pairs_o = refs[16 + n_arrays : 22 + n_arrays]
    (dv, uc, ac, sc, gu, second, out, middle, ov, low, gmix, q, result, sems, io_sems) = refs[
        22 + n_arrays :
    ]
    tokens, width = g.shape
    length = tokens // rows
    heads = width // HEAD
    scale = HEAD ** (-0.5)
    carried = [
        pltpu.make_async_copy(second_i, second, io_sems.at[0]),
        pltpu.make_async_copy(out_i, out, io_sems.at[1]),
    ]
    later = [
        pltpu.make_async_copy(middle_i, middle, io_sems.at[2]),
        pltpu.make_async_copy(output_w, ov, io_sems.at[3]),
        pltpu.make_async_copy(triple.at[:, pl.ds(0, width)], q, io_sems.at[4]),
    ]
    for k, pick in enumerate(picks):
        down, more = chunk_start(
            place, pick, parts, arrays, (active, slope, upward), dv, uc, ac, sc, sems, 0
        )
        if k == 0:
            start(carried)
            start(later)
            wait(carried)
        chunk_work(g, down, more, dv, uc, ac, sc, gu, second, out, False)
    wait(later)
    step = 128
    for t in range(0, tokens, step):
        here = slice(t, t + step)
        mid = middle[here, :]
        u, scaled = unit(mid)
        gm = g[here, :].astype(F32) + norm_back(second[here, :] * gain2[...], u, scaled)
        second[here, :] = gm
        low[here, :] = gm.astype(BF16)
        result[here, :] = (mid + out[here, :] + down_b[...]).astype(BF16)
    done = [
        pltpu.make_async_copy(second, gmid_o, io_sems.at[5]),
        pltpu.make_async_copy(result, result_o, io_sems.at[6]),
    ]
    start(done)

    def back(n, carry):
        rows_n = pl.ds(pl.multiple_of(n * 512, 512), 512)
        gmix[:, rows_n] = dot_nt(low[...], ov[rows_n, :]).astype(BF16)
        return carry

    lax.fori_loop(0, width // 512, back, 0)
    done.append(pltpu.make_async_copy(gmix, gmix_o, io_sems.at[7]))
    done[-1].start()
    keys = jnp.zeros((heads * PAD, width), F32)
    values = jnp.zeros((heads * PAD, width), F32)
    for row in range(rows):
        here = slice(row * length, (row + 1) * length)
        up = gmix[here, :]
        product = up.astype(F32) * mix[here, :].astype(F32)
        high = product.astype(BF16)
        small = (product - high.astype(F32)).astype(BF16)
        delta = dot_nt(ones[...], high) + dot_nt(ones[...], small)
        delta_o[row] = delta
        p = pre[row]
        ds = (p.astype(F32) * (dot_nt(bdv[...], up) - delta)).astype(BF16)
        dspre_o[row] = ds
        keys = keys + dot(ds, q[here, :])
        values = values + dot(p, up)
    row = lax.broadcasted_iota(jnp.int32, keys.shape, 0)
    col = lax.broadcasted_iota(jnp.int32, keys.shape, 1)
    inside = (row // PAD) == (col // HEAD)
    keys = jnp.where(inside, keys * scale, 0.0).reshape(heads, PAD, width)
    values = jnp.where(inside, values, 0.0).reshape(heads, PAD, width)
    pairs_o[0] = jnp.sum(keys, axis=0)
    pairs_o[1] = jnp.sum(values, axis=0)
    wait(done)


def attend_back_body(row, length, heads, triple, gmix, prob, delta, dspre, bdk, out, tri, up, p, sems):
    width = heads * HEAD
    scale = HEAD ** (-0.5)
    here = pl.ds(row * length, length)
    inward = [
        pltpu.make_async_copy(triple.at[here, :], tri, sems.at[0]),
        pltpu.make_async_copy(gmix.at[here, :], up, sems.at[1]),
        pltpu.make_async_copy(prob.at[pl.ds(row * heads, heads)], p, sems.at[2]),
    ]
    start(inward)
    wait(inward)
    low_lane = lax.broadcasted_iota(jnp.int32, (length, 2 * HEAD), 1) < HEAD
    out[:, :width] = (dot_tn(dspre[row], bdk[...]) * scale).astype(BF16)

    def pair(i, carry):
        cols = pl.multiple_of(i * 2 * HEAD, 2 * HEAD)
        q = tri[:, pl.ds(cols, 2 * HEAD)]
        k = tri[:, pl.ds(pl.multiple_of(width + cols, 2 * HEAD), 2 * HEAD)]
        v = tri[:, pl.ds(pl.multiple_of(2 * width + cols, 2 * HEAD), 2 * HEAD)]
        g = up[:, pl.ds(cols, 2 * HEAD)]
        kt = k.T
        zero = jnp.zeros_like(q)
        queries, keys, values = [], 0.0, 0.0
        for sub in (0, 1):
            side = low_lane if sub == 0 else ~low_lane
            gm = jnp.where(side, g, zero)
            qm = jnp.where(side, q, zero)
            prob_here = p[2 * i + sub]
            at = pl.multiple_of((2 * i + sub) * PAD, PAD)
            d = delta[row, pl.ds(at, PAD), :][:1, :]
            ds = (prob_here.astype(F32) * (dot_nt(v, gm) - d)).astype(BF16)
            queries.append(dot(kt[sub * HEAD : (sub + 1) * HEAD, :], ds))
            keys = keys + dot(ds, qm)
            values = values + dot(prob_here, gm)
        before = dot_tn(dspre[row], bdk[:, pl.ds(cols, 2 * HEAD)])
        dq = jnp.concatenate(queries, axis=0).T + before
        out[:, pl.ds(cols, 2 * HEAD)] = (dq * scale).astype(BF16)
        out[:, pl.ds(pl.multiple_of(width + cols, 2 * HEAD), 2 * HEAD)] = (keys * scale).astype(
            BF16
        )
        out[:, pl.ds(pl.multiple_of(2 * width + cols, 2 * HEAD), 2 * HEAD)] = values.astype(BF16)
        return carry

    lax.fori_loop(0, heads // 2, pair, 0)


def input_body(rows, *refs):
    grads = refs[:rows]
    triple_w, x, gain1, gmid_i, result, tv, first, gmid, sems = refs[rows:]
    tokens, width = x.shape
    length = tokens // rows
    block = 256
    inward = [
        pltpu.make_async_copy(
            triple_w.at[pl.ds(n * block, block), :], tv.at[pl.ds(n * block, block), :], sems.at[n]
        )
        for n in range(width // block)
    ]
    start(inward)
    late = pltpu.make_async_copy(gmid_i, gmid, sems.at[len(inward)])
    late.start()
    for n in range(width // block):
        inward[n].wait()
        for row in range(rows):
            first[row * length : (row + 1) * length, n * block : (n + 1) * block] = dot_nt(
                grads[row][...], tv[n * block : (n + 1) * block, :]
            )
    late.wait()
    step = 128
    for t in range(0, tokens, step):
        here = slice(t, t + step)
        u, scaled = unit(x[here, :].astype(F32))
        back = norm_back(first[here, :] * gain1[...], u, scaled)
        result[here, :] = (gmid[here, :] + back).astype(BF16)


def split3(value):
    high = value.astype(BF16)
    rest = value - high.astype(F32)
    mid = rest.astype(BF16)
    return high, mid, (rest - mid.astype(F32)).astype(BF16)


def reparam_body(prefix, keys, values, hidden_r, table, inner_w, outer_w, *outs):
    table_o, inner_wo, inner_bo, outer_wo, outer_bo = outs
    width = keys.shape[1]
    hidden = hidden_r[...]
    low = hidden.astype(BF16)
    row = lax.broadcasted_iota(jnp.int32, (PAD, hidden.shape[1]), 0)
    grads = []
    for k, ref in enumerate((keys, values)):
        value = ref[...]
        parts = split3(value)
        cols = slice(k * width, (k + 1) * width)
        outer_wo[:, cols] = dot_tn(
            jnp.concatenate([low] * 3, axis=0), jnp.concatenate(parts, axis=0)
        )
        outer_bo[:, cols] = jnp.sum(value, axis=0, keepdims=True)
        grads.append(dot_nt(jnp.concatenate(parts, axis=0), outer_w[:, cols]))
    total = grads[0] + grads[1]
    hidden_grad = total[:PAD] + total[PAD : 2 * PAD] + total[2 * PAD :]
    before = jnp.where(row < prefix, hidden_grad * (1.0 - hidden * hidden), 0.0)
    inner_bo[...] = jnp.sum(before, axis=0, keepdims=True)
    stacked = jnp.concatenate(split3(before), axis=0)
    inner_wo[...] = dot_tn(jnp.concatenate([table[...]] * 3, axis=0), stacked)
    back = dot_nt(stacked, inner_w[...])
    table_o[...] = back[:PAD] + back[PAD : 2 * PAD] + back[2 * PAD :]


def add_over(value, axis, size, first):
    mask = first
    while mask < size:
        value = value + lax.ppermute(value, axis, [(i, i ^ mask) for i in range(size)])
        mask *= 2
    return value


def total_pairs(pairs, fsdp, dp):
    core = lax.rem(lax.axis_index("fsdp"), 2)
    kept = jnp.where(core == 0, pairs[0], pairs[1])
    sent = jnp.where(core == 0, pairs[1], pairs[0])
    value = kept + flip(sent, 1, fsdp)
    value = add_over(value, "fsdp", fsdp, 2)
    value = add_over(value, "dp", dp, 1)
    other = flip(value, 1, fsdp)
    return jnp.where(core == 0, value, other), jnp.where(core == 0, other, value)


def body(
    fsdp,
    dp,
    activations,
    lengths,
    cotangent,
    gain_first,
    shift_first,
    triple_weight,
    output_weight,
    output_bias,
    gain_second,
    shift_second,
    upward_weight,
    upward_bias,
    downward_weight,
    downward_bias,
    prefix_table,
    inner_weight,
    inner_bias,
    outer_weight,
    outer_bias,
):
    rows, length, width = activations.shape
    tokens = rows * length
    heads = width // HEAD
    wide = upward_bias.shape[0]
    prefix, _ = prefix_table.shape
    mid = inner_bias.shape[0]
    chunk = wide // 4
    place = jnp.stack([lax.axis_index("dp"), lax.axis_index("fsdp")]).astype(jnp.int32)
    x = activations.reshape(tokens, width)
    g = cotangent.reshape(tokens, width)
    flat = lambda v: v.reshape(1, -1)
    dma = lambda n: pltpu.SemaphoreType.DMA((n,))
    vm = pltpu.VMEM
    mm = tokens * width * width

    (first_arrays, triple_parts, output_parts), (up_arrays, up_parts), (down_arrays, down_parts) = (
        collect(triple_weight, output_weight, upward_weight, downward_weight, fsdp, dp)
    )

    table = jnp.pad(prefix_table, ((0, PAD - prefix), (0, 0)))
    hidden, bdk, bdv, ones = call(
        partial(prefix_body, prefix),
        "prefix",
        [(shaped((PAD, mid), F32), VMEM)] + [(shaped((heads * PAD, width), BF16), VMEM)] * 3,
        [VMEM] * 5,
        [],
        2 * PAD * mid * 3 * width,
        3 << 20,
    )(table, inner_weight, flat(inner_bias), outer_weight, flat(outer_bias))

    n = len(first_arrays)
    triple, prob, pre, mix, middle, norm_two, triple_full, output_full = call(
        partial(attend_body, rows, prefix, triple_parts, output_parts, n),
        "attend",
        [
            (shaped((tokens, 3 * width), BF16), ANY),
            (shaped((rows * heads, length, length), BF16), ANY),
            (shaped((rows, heads * PAD, length), BF16), ANY),
            (shaped((tokens, width), BF16), ANY),
            (shaped((tokens, width), F32), ANY),
            (shaped((tokens, width), BF16), ANY),
            (shaped((width, 3 * width), BF16), ANY),
            (shaped((width, width), BF16), ANY),
        ],
        [SMEM, SMEM] + [VMEM] * 8 + [ANY] * n,
        [
            vm((width, 3 * width), BF16),
            vm((width, width), BF16),
            vm((tokens, width), BF16),
            vm((tokens, 3 * width), BF16),
            vm((rows * heads, length, length), BF16),
            vm((length, length), F32),
            vm((heads * PAD, length), F32),
            vm((rows, heads * PAD, length), BF16),
            vm((length, width), F32),
            vm((tokens, width), BF16),
            vm((tokens, width), F32),
            dma(len(triple_parts.parts) + len(output_parts.parts)),
            dma(8 + rows),
        ],
        8 * mm + 4 * rows * heads * length * length * HEAD,
        30 << 20,
    )(
        place,
        lengths,
        x,
        flat(gain_first),
        flat(shift_first),
        flat(output_bias),
        flat(gain_second),
        flat(shift_second),
        bdk,
        bdv,
        *first_arrays,
    )

    n = len(up_arrays)
    active, slope, up_full = call(
        partial(upward_body, up_parts, n),
        "upward",
        [
            (shaped((tokens, wide), BF16), ANY),
            (shaped((tokens, wide), BF16), ANY),
            (shaped((width, wide), BF16), ANY),
        ],
        [SMEM] + [VMEM] * 2 + [ANY] * n,
        [
            vm((width, wide), BF16),
            vm((tokens, wide), BF16),
            vm((tokens, wide), BF16),
            dma(len(up_parts.parts)),
            dma(3),
        ],
        8 * mm,
        25 << 20,
    )(place, norm_two, flat(upward_bias), *up_arrays)

    n = len(down_arrays)
    chunk_scratch = [
        vm((chunk, width), BF16),
        vm((width, chunk), BF16),
        vm((tokens, chunk), BF16),
        vm((tokens, chunk), BF16),
        vm((tokens, chunk), BF16),
        vm((tokens, width), F32),
        vm((tokens, width), F32),
    ]
    sums = [(shaped((tokens, width), F32), ANY)] * 2
    n_sems = len(down_parts.parts) + 4
    second, out = call(
        partial(chunk_body, (0,), True, down_parts, n),
        "chunk_own",
        sums,
        [SMEM, VMEM] + [ANY] * (3 + n),
        chunk_scratch + [dma(n_sems), dma(4)],
        6 * mm,
        12 << 20,
    )(place, g, active, slope, up_full, *down_arrays)
    second, out = call(
        partial(chunk_body, (1, 2), False, down_parts, n),
        "chunk_near",
        sums,
        [SMEM, VMEM] + [ANY] * (5 + n),
        chunk_scratch + [dma(n_sems), dma(4)],
        12 * mm,
        24 << 20,
    )(place, g, active, slope, up_full, *down_arrays, second, out)
    result, g_middle, g_mix, delta, d_pre, pairs = call(
        partial(middle_body, rows, (3,), down_parts, n),
        "middle",
        [
            (shaped((tokens, width), BF16), ANY),
            (shaped((tokens, width), F32), ANY),
            (shaped((tokens, width), BF16), ANY),
            (shaped((rows, heads * PAD, length), F32), VMEM),
            (shaped((rows, heads * PAD, length), BF16), VMEM),
            (shaped((2, PAD, width), F32), VMEM),
        ],
        [SMEM, VMEM]
        + [ANY] * (3 + n)
        + [ANY] * 3
        + [VMEM] * 2
        + [ANY]
        + [VMEM]
        + [ANY]
        + [VMEM] * 3,
        chunk_scratch
        + [
            vm((tokens, width), F32),
            vm((width, width), BF16),
            vm((tokens, width), BF16),
            vm((tokens, width), BF16),
            vm((tokens, width), BF16),
            vm((tokens, width), BF16),
            dma(n_sems),
            dma(8),
        ],
        9 * mm,
        24 << 20,
    )(
        place,
        g,
        active,
        slope,
        up_full,
        *down_arrays,
        second,
        out,
        middle,
        flat(gain_second),
        flat(downward_bias),
        output_full,
        mix,
        triple,
        pre,
        bdv,
        ones,
    )

    grads = []
    for row in range(rows):
        grads += call(
            partial(attend_back_body, row, length, heads),
            "attend_back_%d" % row,
            [(shaped((length, 3 * width), BF16), VMEM)],
            [ANY] * 3 + [VMEM] * 3,
            [
                vm((length, 3 * width), BF16),
                vm((length, width), BF16),
                vm((heads, length, length), BF16),
                dma(3),
            ],
            16 * heads * length * length * HEAD,
            8 << 20,
        )(triple, g_mix, prob, delta, d_pre, bdk)

    (input_grad,) = call(
        partial(input_body, rows),
        "input",
        [(shaped((tokens, width), BF16), VMEM)],
        [VMEM] * rows + [ANY] + [VMEM] * 2 + [ANY],
        [
            vm((width, 3 * width), BF16),
            vm((tokens, width), F32),
            vm((tokens, width), F32),
            dma(width // 256 + 1),
        ],
        6 * mm,
        13 << 20,
    )(*grads, triple_full, x, flat(gain_first), g_middle)

    pair_keys, pair_values = total_pairs(pairs, fsdp, dp)
    table_grad, inner_w_grad, inner_b_grad, outer_w_grad, outer_b_grad = call(
        partial(reparam_body, prefix),
        "reparam",
        [
            (shaped((PAD, width), F32), VMEM),
            (shaped((width, mid), F32), VMEM),
            (shaped((1, mid), F32), VMEM),
            (shaped((mid, 2 * width), F32), VMEM),
            (shaped((1, 2 * width), F32), VMEM),
        ],
        [VMEM] * 6,
        [],
        2 * PAD * mid * 6 * width,
        9 << 20,
    )(pair_keys, pair_values, hidden, table, inner_weight, outer_weight)
    return (
        result.reshape(rows, length, width),
        input_grad.reshape(rows, length, width),
        table_grad[:prefix],
        inner_w_grad,
        inner_b_grad.reshape(-1),
        outer_w_grad,
        outer_b_grad.reshape(-1),
    )


def solution(mesh):
    in_specs = (
        P(("dp", "fsdp"), None, None),
        P(("dp", "fsdp"), None),
        P(("dp", "fsdp"), None, None),
        P(),
        P(),
        P("fsdp", "dp"),
        P("fsdp", "dp"),
        P(),
        P(),
        P(),
        P("fsdp", "dp"),
        P(),
        P("fsdp", "dp"),
        P(),
        P(),
        P(),
        P(),
        P(),
        P(),
    )
    out_specs = (
        P(("dp", "fsdp"), None, None),
        P(("dp", "fsdp"), None, None),
        P(),
        P(),
        P(),
        P(),
        P(),
    )
    return jax.shard_map(
        partial(body, mesh.shape["fsdp"], mesh.shape["dp"]),
        mesh=mesh,
        in_specs=in_specs,
        out_specs=out_specs,
        check_vma=False,
    )
```

```python
import math
from functools import partial

import jax
import jax.numpy as jnp
from jax import lax
from jax.experimental import pallas as pl
from jax.experimental.pallas import tpu as pltpu
from jax.sharding import PartitionSpec as P

HEAD = 64
PAD = 16
MASKED = -1e30
F32 = jnp.float32
BF16 = jnp.bfloat16
GELU_C = 0.7978845608028654
GELU_A = 0.044715
PEAK = 1.15e9

ANY = pl.BlockSpec(memory_space=pl.ANY)
VMEM = pl.BlockSpec(memory_space=pltpu.VMEM)
SMEM = pl.BlockSpec(memory_space=pltpu.SMEM)


def dot(a, b):
    return lax.dot_general(a, b, (((1,), (0,)), ((), ())), preferred_element_type=F32)


def dot_nt(a, b):
    return lax.dot_general(a, b, (((1,), (1,)), ((), ())), preferred_element_type=F32)


def dot_tn(a, b):
    return lax.dot_general(a, b, (((0,), (0,)), ((), ())), preferred_element_type=F32)


def unit(values):
    center = values - jnp.mean(values, axis=-1, keepdims=True)
    scaled = lax.rsqrt(jnp.mean(center * center, axis=-1, keepdims=True) + 1e-05)
    return center * scaled, scaled


def norm_back(upstream, unit_rows, scaled):
    return scaled * (
        upstream
        - jnp.mean(upstream, axis=-1, keepdims=True)
        - unit_rows * jnp.mean(upstream * unit_rows, axis=-1, keepdims=True)
    )


def call(body, name, outs, ins, scratch, micros, room=None, aliases={}):
    held = sum(
        math.prod(s.shape) * jnp.dtype(s.dtype).itemsize
        for s in scratch
        if jnp.issubdtype(s.dtype, jnp.floating)
    )
    limit = 56 * 1024 * 1024 if room is None else held + room * 1024 * 1024
    return pl.pallas_call(
        body,
        name=name,
        out_shape=[o[0] for o in outs],
        out_specs=[o[1] for o in outs],
        in_specs=ins,
        scratch_shapes=scratch,
        input_output_aliases=aliases,
        compiler_params=pltpu.CompilerParams(vmem_limit_bytes=limit),
        cost_estimate=pl.CostEstimate(
            flops=int(micros * PEAK), bytes_accessed=0, transcendentals=0
        ),
    )


def shaped(shape, dtype):
    return jax.ShapeDtypeStruct(shape, dtype)


class Pieces:
    def __init__(self, dp, shard):
        self.dp = dp
        self.shard_rows, self.shard_cols = shard.shape
        self.parts = []
        self.split = True

    def whole(self, key):
        self.split = False
        self.parts.append((key, None, None, None, 0, None, None))
        return self

    def add(self, stage, layout, rows):
        where = {(0, 0): (0, 0), (1, 0): (0, 1), (0, 1): (1, 0), (2, 1): (1, 1)}
        where.update({(2, 0): (2, 0), (3, 0): (2, 1), (1, 1): (3, 0), (3, 1): (3, 1)})
        for core in (0, 1):
            for way in range(4):
                for side, src_row, low, count, plane, col in layout:
                    array, second = where[way, side]
                    key = (stage, array, core)
                    src = src_row + second * rows
                    self.parts.append((key, src, low, count, plane, 2 * way | core, col))
        return self

    def of(self, picks):
        out = Pieces.__new__(Pieces)
        out.__dict__.update(self.__dict__)
        out.parts = [p for p in self.parts if not self.split or p[5] >> 1 in picks]
        return out

    def keys(self):
        return sorted({part[0] for part in self.parts})

    def planes(self):
        return sorted({part[4] for part in self.parts})

    def columns(self, place, plane):
        if not self.split:
            return 0, self.shard_cols * self.dp
        across = lax.rem(place[0] + plane, self.dp)
        return pl.multiple_of(across * self.shard_cols, 128), self.shard_cols

    def copies(self, refs, dst, sems, base, place, plane=None, paired=False):
        out = []
        for key, src_row, low, count, at, flip, col in self.parts:
            if plane is not None and at != plane:
                continue
            if not self.split:
                out.append(pltpu.make_async_copy(refs[key], dst, sems.at[base + len(out)]))
                continue
            owner = jnp.bitwise_xor(place[1], flip)
            if paired:
                owner = jnp.bitwise_and(owner, 1)
            row = pl.multiple_of(owner * self.shard_rows + low, 16)
            column, cols = self.columns(place, at)
            out.append(
                pltpu.make_async_copy(
                    refs[key].at[pl.ds(src_row, count), pl.ds(col, cols)],
                    dst.at[pl.ds(row, count), pl.ds(column, cols)],
                    sems.at[base + len(out)],
                )
            )
        return out


def start(copies):
    for c in copies:
        c.start()


def wait(copies):
    for c in copies:
        c.wait()


def after(value, *others):
    return lax.optimization_barrier((value, *others))[0]


def flip(value, mask, size):
    return lax.ppermute(value, "fsdp", [(i, i ^ mask) for i in range(size)])


class Spread:
    def __init__(self, low, high, size):
        self.size = size
        self.halves = low, high
        self.first = flip(low, 2, size), flip(high, 4, size)

    def second(self, *others):
        self.arrays = [
            jnp.concatenate([half, after(came, *others)], axis=0)
            for half, came in zip(self.halves, self.first)
        ]
        self.arrays.append(flip(self.arrays[0], 4, self.size))
        self.arrays.append(flip(self.arrays[1], 2, self.size))

    def put(self, arrays, stage, which, *others):
        for k in which:
            arrays[stage, k, 0] = self.arrays[k]
            arrays[stage, k, 1] = flip(after(self.arrays[k], *others), 1, self.size)


def packed(value, rows):
    return jnp.concatenate(
        [value[k : k + rows] for k in range(0, value.shape[0], rows)], axis=1
    )


def halves(planes, shard_rows):
    total = shard_rows * len(planes)
    middle = total // 2
    out = []
    for k, plane in enumerate(planes):
        for side, (first, last) in enumerate(((0, middle), (middle, total))):
            low, high = max(first, k * shard_rows), min(last, (k + 1) * shard_rows)
            if low < high:
                out.append((side, low - first, low - k * shard_rows, high - low, plane))
    return out


def cut(shards, layout):
    return [
        jnp.concatenate(
            [shards[p][low : low + count] for s, _, low, count, p in layout if s == side], axis=0
        )
        for side in (0, 1)
    ]


def from_planes(value, dp, *others):
    planes = after(lax.all_gather(value, "dp", axis=0, tiled=False), *others)
    here = lax.axis_index("dp")
    return {
        j: lax.dynamic_index_in_dim(planes, lax.rem(here + j, dp), 0, keepdims=False)
        for j in range(1, dp)
    }


def prefix_body(
    prefix, place, table, inner_w, inner_b, outer_w, outer_b, place_o, hidden_o, keys_o, values_o, ones_o
):
    place_o[0] = place[0]
    place_o[1] = place[1]
    width = keys_o.shape[1]
    hidden = jnp.tanh(dot(table[...], inner_w[...]) + inner_b[...])
    hidden_o[...] = hidden
    pairs = (dot(hidden.astype(BF16), outer_w[...]) + outer_b[...]).astype(BF16).astype(F32)
    shape = keys_o.shape
    row = lax.broadcasted_iota(jnp.int32, shape, 0)
    col = lax.broadcasted_iota(jnp.int32, shape, 1)
    inside = (row // PAD) == (col // HEAD)
    real = inside & (lax.rem(row, PAD) < prefix)
    heads = shape[0] // PAD
    keys_o[...] = jnp.where(real, jnp.tile(pairs[:, :width], (heads, 1)), 0.0).astype(BF16)
    values_o[...] = jnp.where(real, jnp.tile(pairs[:, width:], (heads, 1)), 0.0).astype(BF16)
    ones_o[...] = jnp.where(inside, 1.0, 0.0).astype(BF16)


def triple_body(parts, keys, *refs):
    n_arrays = len(keys)
    place, x, gain, shift = refs[:4]
    arrays = dict(zip(keys, refs[4 : 4 + n_arrays]))
    triple_o, t_o, tv, normed, tri, sems, out_sems = refs[4 + n_arrays :]
    tokens, _ = x.shape
    inward = []
    base = 0
    for plane in parts.planes():
        inward.append((plane, parts.copies(arrays, tv, sems, base, place, plane)))
        base += len(inward[-1][1])
        start(inward[-1][1])
    outs = []

    def send(src, dst):
        outs.append(pltpu.make_async_copy(src, dst, out_sems.at[len(outs)]))
        outs[-1].start()

    step = 128
    for t in range(0, tokens, step):
        u, _ = unit(x[t : t + step, :].astype(F32))
        normed[t : t + step, :] = (u * gain[...] + shift[...]).astype(BF16)
    for plane, copies in inward:
        wait(copies)
        column, count = parts.columns(place, plane)
        block = count if count <= 1024 else 1024
        for n in range(0, count, block):
            cols = pl.ds(column + n, block)
            if not isinstance(column, int):
                cols = pl.ds(pl.multiple_of(column + n, 128), block)
            tri[:, cols] = dot(normed[...], tv[:, cols]).astype(BF16)
            send(tri.at[:, cols], triple_o.at[:, cols])
            send(tv.at[:, cols], t_o.at[:, cols])
    wait(outs)


def attend_body(rows, prefix, parts, keys, *refs):
    n_arrays = len(keys)
    place, lengths, x, out_b, gain, shift, bdk, bdv, triple = refs[:9]
    arrays = dict(zip(keys, refs[9 : 9 + n_arrays]))
    prob_o, pre_o, mix_o, middle_o, norm_o, o_o = refs[9 + n_arrays : 15 + n_arrays]
    (tri, ov, normed, prob, bias, spre, pre, main, mix, middle, sems, out_sems) = refs[
        15 + n_arrays :
    ]
    tokens, width = x.shape
    length = tokens // rows
    heads = width // HEAD
    scale = HEAD ** (-0.5)
    step = 128
    inward = [
        pltpu.make_async_copy(
            triple.at[pl.ds(row * length, length), :],
            tri.at[pl.ds(row * length, length), :],
            sems.at[row],
        )
        for row in range(rows)
    ]
    start(inward)
    in_o = parts.copies(arrays, ov, sems, rows, place)
    start(in_o)
    outs = []

    def send(src, dst):
        outs.append(pltpu.make_async_copy(src, dst, out_sems.at[len(outs)]))
        outs[-1].start()

    lane = lax.broadcasted_iota(jnp.int32, (length, 2 * HEAD), 1)
    low_lane = lane < HEAD
    for row in range(rows):
        here = slice(row * length, (row + 1) * length)
        key = lax.broadcasted_iota(jnp.int32, (length, length), 0)
        query = lax.broadcasted_iota(jnp.int32, (length, length), 1)
        key_seg = jnp.zeros((length, length), jnp.int32)
        query_seg = jnp.zeros((length, length), jnp.int32)
        bound = 0
        for s in range(lengths.shape[1]):
            bound = bound + lengths[row, s]
            key_seg = key_seg + jnp.where(key >= bound, 1, 0)
            query_seg = query_seg + jnp.where(query >= bound, 1, 0)
        seen = (key_seg == query_seg) & (key <= query)
        bias[...] = jnp.where(seen, 0.0, MASKED)
        inward[row].wait()
        raw = dot_nt(bdk[...], tri[here, :width]) * scale
        pre_row = lax.broadcasted_iota(jnp.int32, raw.shape, 0)
        spre[...] = jnp.where(lax.rem(pre_row, PAD) < prefix, raw, MASKED)
        for i in range(heads // 2):
            cols = i * 2 * HEAD
            q = tri[here, cols : cols + 2 * HEAD]
            k = tri[here, width + cols : width + cols + 2 * HEAD]
            v = tri[here, 2 * width + cols : 2 * width + cols + 2 * HEAD]
            found = []
            for sub in (0, 1):
                qm = jnp.where(low_lane if sub == 0 else ~low_lane, q, jnp.zeros_like(q))
                s = dot_nt(k, qm) * scale + bias[...]
                at = (2 * i + sub) * PAD
                sp = spre[at : at + PAD, :]
                top = jnp.maximum(
                    jnp.max(s, axis=0, keepdims=True), jnp.max(sp, axis=0, keepdims=True)
                )
                e = jnp.exp(s - top)
                ep = jnp.exp(sp - top)
                inverse = 1.0 / (
                    jnp.sum(e, axis=0, keepdims=True) + jnp.sum(ep, axis=0, keepdims=True)
                )
                p = (e * inverse).astype(BF16)
                prob[row * heads + 2 * i + sub] = p
                pre[row, at : at + PAD, :] = (ep * inverse).astype(BF16)
                found.append(dot_tn(p, v))
            main[:, cols : cols + 2 * HEAD] = jnp.where(low_lane, found[0], found[1])
        send(prob.at[pl.ds(row * heads, heads)], prob_o.at[pl.ds(row * heads, heads)])
        mix[here, :] = (main[...] + dot_tn(pre[row], bdv[...])).astype(BF16)
        if row == 0:
            wait(in_o)
            send(ov, o_o)
        middle[here, :] = x[here, :].astype(F32) + dot(mix[here, :], ov[...]) + out_b[...]
        for t in range(row * length, (row + 1) * length, step):
            u, _ = unit(middle[t : t + step, :])
            normed[t : t + step, :] = (u * gain[...] + shift[...]).astype(BF16)
        send(middle.at[pl.ds(row * length, length), :], middle_o.at[pl.ds(row * length, length), :])
        send(normed.at[pl.ds(row * length, length), :], norm_o.at[pl.ds(row * length, length), :])
    send(pre, pre_o)
    send(mix, mix_o)
    wait(outs)


def upward_body(planes, parts, keys, carried, *refs):
    n_arrays = len(keys)
    place, norm, bias = refs[:3]
    arrays = dict(zip(keys, refs[3 : 3 + n_arrays]))
    n_arrays += carried
    active_o, slope_o, up_o = refs[3 + n_arrays : 6 + n_arrays]
    uv, active, slope, sems, out_sems = refs[6 + n_arrays :]
    inward = []
    base = 0
    for plane in planes:
        inward.append((plane, parts.copies(arrays, uv, sems, base, place, plane)))
        base += len(inward[-1][1])
        start(inward[-1][1])
    outs = []

    def send(src, dst):
        outs.append(pltpu.make_async_copy(src, dst, out_sems.at[len(outs)]))
        outs[-1].start()

    for plane, copies in inward:
        wait(copies)
        column, count = parts.columns(place, plane)
        block = 512
        for n in range(0, count, block):
            cols = pl.ds(column + n, block)
            if not isinstance(column, int):
                cols = pl.ds(pl.multiple_of(column + n, 128), block)
            u = dot(norm[...], uv[:, cols]) + bias[:, cols]
            square = u * u
            half = 0.5 + 0.5 * jnp.tanh(u * (GELU_C + GELU_C * GELU_A * square))
            active[:, cols] = (u * half).astype(BF16)
            slope[:, cols] = (
                half
                + (u * (half - half * half)) * (2.0 * GELU_C + 6.0 * GELU_C * GELU_A * square)
            ).astype(BF16)
            send(active.at[:, cols], active_o.at[:, cols])
            send(slope.at[:, cols], slope_o.at[:, cols])
            send(uv.at[:, cols], up_o.at[:, cols])
    wait(outs)


class Chunk:
    def __init__(self, place, pick, parts, arrays, full, held, slot, sems, base):
        active, slope, upward = full
        self.dv, self.uc, self.ac, self.sc, self.gu = (h.at[slot] for h in held)
        size = self.uc.shape[1]
        self.split = parts.split
        if not parts.split:
            cols = rows = pl.ds(pick * size, size)
            (whole,) = arrays.values()
            self.down = [pltpu.make_async_copy(whole.at[rows, :], self.dv, sems.at[base])]
        else:
            at = jnp.bitwise_xor(lax.shift_right_logical(place[1], 1), pick)
            self.down = parts.of((pick,)).copies(
                arrays, self.dv, sems, base, place, paired=True
            )
            self.planes, self.shard_rows = parts.dp, parts.shard_rows
            cols = pl.ds(pl.multiple_of(at * size, size), size)
        base += len(self.down)
        self.sems = len(self.down) + 3
        self.rest = [
            pltpu.make_async_copy(slope.at[:, cols], self.sc, sems.at[base]),
            pltpu.make_async_copy(upward.at[:, cols], self.uc, sems.at[base + 1]),
            pltpu.make_async_copy(active.at[:, cols], self.ac, sems.at[base + 2]),
        ]
        start(self.down)
        start(self.rest)

    def blocks(self):
        rows = self.shard_rows
        size = self.uc.shape[1]
        count = size // (2 * rows)
        return [(k, (k * rows, size // 2 + k * rows)) for k in range(count)]

    def upstream(self, g):
        wait(self.down)
        self.rest[0].wait()
        size = self.uc.shape[1]
        if not self.split:
            for n in range(0, size, 512):
                cols = slice(n, n + 512)
                value = dot_nt(g[...], self.dv[cols, :])
                self.gu[:, cols] = (value * self.sc[:, cols].astype(F32)).astype(BF16)
            return
        width = g.shape[1] // self.planes
        rows = self.shard_rows
        for k, places in self.blocks():
            value = 0.0
            for z in range(self.planes):
                at = z * self.dv.shape[1] // self.planes + k * width
                value = value + dot_nt(g[:, z * width : (z + 1) * width], self.dv[:, at : at + width])
            for n, low in enumerate(places):
                cols = slice(low, low + rows)
                part = value[:, n * rows : (n + 1) * rows]
                self.gu[:, cols] = (part * self.sc[:, cols].astype(F32)).astype(BF16)

    def back(self):
        self.rest[1].wait()
        return lambda cols: dot_nt(self.gu[...], self.uc[cols, :])

    def ahead(self):
        self.rest[2].wait()
        if not self.split:
            return lambda cols: dot(self.ac[...], self.dv[:, cols])
        rows = self.shard_rows

        def term(cols):
            width = self.uc.shape[0] // self.planes
            found = []
            for z in range(cols.start // width, cols.stop // width):
                value = 0.0
                for k, places in self.blocks():
                    at = z * self.dv.shape[1] // self.planes + k * width
                    left = jnp.concatenate([self.ac[:, low : low + rows] for low in places], axis=1)
                    value = value + dot(left, self.dv[:, at : at + width])
                found.append(value)
            return jnp.concatenate(found, axis=1)

        return term


def chunk_body(picks, parts, keys, *refs):
    n_arrays = len(keys)
    place, g, active, slope, upward = refs[:5]
    arrays = dict(zip(keys, refs[5 : 5 + n_arrays]))
    rest = refs[5 + n_arrays :]
    second_o, out_o, dv, uc, ac, sc, gu, second, out, g_v, sems, io_sems = rest
    width = second.shape[1]
    g_copy = pltpu.make_async_copy(g, g_v, io_sems.at[0])
    g_copy.start()
    g = g_v
    chunks = []
    base = 0
    for k, pick in enumerate(picks):
        chunks.append(
            Chunk(
                place, pick, parts, arrays, (active, slope, upward), (dv, uc, ac, sc, gu), k, sems, base
            )
        )
        base += chunks[-1].sems
    g_copy.wait()
    for chunk in chunks:
        chunk.upstream(g)
    done = []
    for k, (total, total_o) in enumerate(((second, second_o), (out, out_o))):
        terms = [chunk.back() if k == 0 else chunk.ahead() for chunk in chunks]
        for n in range(0, width, 512):
            cols = slice(n, n + 512)
            value = terms[0](cols)
            for term in terms[1:]:
                value = value + term(cols)
            total[:, cols] = value
            at = pl.ds(n, 512)
            done.append(
                pltpu.make_async_copy(
                    total.at[:, at], total_o.at[:, at], io_sems.at[2 + len(done)]
                )
            )
            done[-1].start()
    wait(done)


def middle_body(rows, picks, parts, keys, *refs):
    n_arrays = len(keys)
    place, g, active, slope, upward = refs[:5]
    arrays = dict(zip(keys, refs[5 : 5 + n_arrays]))
    second_i, out_i, middle_i, gain2, down_b, output_w, mix, triple, pre, bdv, ones = refs[
        5 + n_arrays : 16 + n_arrays
    ]
    result_o, gmid_o, gmix_o, delta_o, dspre_o, pairs_o = refs[16 + n_arrays : 22 + n_arrays]
    mix_i, pre_i, bdv_i, ones_i, g_i = mix, pre, bdv, ones, g
    (dv, uc, ac, sc, gu, second, out, middle, ov, low, gmix, q, result) = refs[
        22 + n_arrays : 35 + n_arrays
    ]
    mix, pre, bdv, ones, g, sems, io_sems = refs[35 + n_arrays :]
    tokens, width = g.shape
    g_copy = pltpu.make_async_copy(g_i, g, io_sems.at[12])
    g_copy.start()
    length = tokens // rows
    heads = width // HEAD
    scale = HEAD ** (-0.5)
    chunks = []
    base = 0
    for k, pick in enumerate(picks):
        chunks.append(
            Chunk(
                place, pick, parts, arrays, (active, slope, upward), (dv, uc, ac, sc, gu), k, sems, base
            )
        )
        base += chunks[-1].sems
    carried = [
        pltpu.make_async_copy(second_i, second, io_sems.at[0]),
        pltpu.make_async_copy(out_i, out, io_sems.at[1]),
        pltpu.make_async_copy(middle_i, middle, io_sems.at[2]),
        pltpu.make_async_copy(output_w, ov, io_sems.at[3]),
        pltpu.make_async_copy(triple.at[:, pl.ds(0, width)], q, io_sems.at[4]),
        pltpu.make_async_copy(mix_i, mix, io_sems.at[8]),
        pltpu.make_async_copy(pre_i, pre, io_sems.at[9]),
        pltpu.make_async_copy(bdv_i, bdv, io_sems.at[10]),
        pltpu.make_async_copy(ones_i, ones, io_sems.at[11]),
    ]
    start(carried)
    g_copy.wait()
    for chunk in chunks:
        chunk.upstream(g)
    back = [chunk.back() for chunk in chunks]
    ahead = [chunk.ahead() for chunk in chunks]
    wait(carried)
    for n in range(0, width, 512):
        cols = slice(n, n + 512)
        value = second[:, cols]
        for term in back:
            value = value + term(cols)
        second[:, cols] = value
    step = 128
    for t in range(0, tokens, step):
        here = slice(t, t + step)
        u, scaled = unit(middle[here, :])
        gm = g[here, :].astype(F32) + norm_back(second[here, :] * gain2[...], u, scaled)
        second[here, :] = gm
        low[here, :] = gm.astype(BF16)
    done = [pltpu.make_async_copy(second, gmid_o, io_sems.at[5])]
    done[-1].start()
    for row in range(rows):
        here = slice(row * length, (row + 1) * length)
        gmix[here, :] = dot_nt(low[here, :], ov[...]).astype(BF16)
    done.append(pltpu.make_async_copy(gmix, gmix_o, io_sems.at[6]))
    done[-1].start()
    for n in range(0, width, 512):
        cols = slice(n, n + 512)
        value = middle[:, cols] + out[:, cols] + down_b[:, cols]
        for term in ahead:
            value = value + term(cols)
        result[:, cols] = value.astype(BF16)
    done.append(pltpu.make_async_copy(result, result_o, io_sems.at[7]))
    done[-1].start()
    keys = 0.0
    values = 0.0
    for row in range(rows):
        here = slice(row * length, (row + 1) * length)
        up = gmix[here, :]
        product = up.astype(F32) * mix[here, :].astype(F32)
        high = product.astype(BF16)
        small = (product - high.astype(F32)).astype(BF16)
        delta = dot_nt(ones[...], high) + dot_nt(ones[...], small)
        delta_o[row] = delta
        p = pre[row]
        ds = (p.astype(F32) * (dot_nt(bdv[...], up) - delta)).astype(BF16)
        dspre_o[row] = ds
        keys = keys + dot(ds, q[here, :])
        values = values + dot(p, up)
    row = lax.broadcasted_iota(jnp.int32, keys.shape, 0)
    col = lax.broadcasted_iota(jnp.int32, keys.shape, 1)
    inside = (row // PAD) == (col // HEAD)
    keys = jnp.where(inside, keys * scale, 0.0).reshape(heads, PAD, width)
    values = jnp.where(inside, values, 0.0).reshape(heads, PAD, width)
    pairs_o[0] = jnp.sum(keys, axis=0)
    pairs_o[1] = jnp.sum(values, axis=0)
    wait(done)


def attend_back_body(row, length, heads, triple, gmix, prob, delta, dspre, bdk, out_o, tri, up, p, before, out, sems):
    width = heads * HEAD
    scale = HEAD ** (-0.5)
    here = pl.ds(row * length, length)
    groups = 4
    span = heads // groups
    inward = []
    for n in range(groups):
        cols = pl.ds(n * span * HEAD, span * HEAD)
        copies = [
            pltpu.make_async_copy(
                triple.at[here, pl.ds(m * width + n * span * HEAD, span * HEAD)],
                tri.at[:, pl.ds(m * width + n * span * HEAD, span * HEAD)],
                sems.at[5 * n + m],
            )
            for m in range(3)
        ]
        copies.append(pltpu.make_async_copy(gmix.at[here, cols], up.at[:, cols], sems.at[5 * n + 3]))
        copies.append(
            pltpu.make_async_copy(
                prob.at[pl.ds(row * heads + n * span, span)],
                p.at[pl.ds(n * span, span)],
                sems.at[5 * n + 4],
            )
        )
        start(copies)
        inward.append(copies)
    low_lane = lax.broadcasted_iota(jnp.int32, (length, 2 * HEAD), 1) < HEAD
    before[...] = dot_tn(dspre[row], bdk[...])
    done = []
    for i in range(heads // 2):
        if 2 * i % span == 0:
            wait(inward[2 * i // span])
        cols = i * 2 * HEAD
        now = slice(cols, cols + 2 * HEAD)
        q = tri[:, now]
        k = tri[:, width + cols : width + cols + 2 * HEAD]
        v = tri[:, 2 * width + cols : 2 * width + cols + 2 * HEAD]
        g = up[:, now]
        kt = k.T
        zero = jnp.zeros_like(q)
        queries, keys, values = [], 0.0, 0.0
        for sub in (0, 1):
            side = low_lane if sub == 0 else ~low_lane
            gm = jnp.where(side, g, zero)
            qm = jnp.where(side, q, zero)
            prob_here = p[2 * i + sub]
            at = (2 * i + sub) * PAD
            d = delta[row, at : at + 1, :]
            ds = (prob_here.astype(F32) * (dot_nt(v, gm) - d)).astype(BF16)
            queries.append(dot(kt[sub * HEAD : (sub + 1) * HEAD, :], ds))
            keys = keys + dot(ds, qm)
            values = values + dot(prob_here, gm)
        dq = jnp.concatenate(queries, axis=0).T + before[:, now]
        out[:, now] = (dq * scale).astype(BF16)
        out[:, width + cols : width + cols + 2 * HEAD] = (keys * scale).astype(BF16)
        out[:, 2 * width + cols : 2 * width + cols + 2 * HEAD] = values.astype(BF16)
        if (2 * i + 2) % span == 0:
            for m in range(3):
                at = pl.ds(m * width + (2 * i + 2 - span) * HEAD, span * HEAD)
                done.append(
                    pltpu.make_async_copy(
                        out.at[:, at], out_o.at[:, at], sems.at[5 * groups + len(done)]
                    )
                )
                done[-1].start()
    wait(done)


def input_body(rows, *refs):
    grads = refs[:rows]
    triple_w, x_i, gain1, gmid_i, result_o, tv, gv, first, gmid, x, result, sems = refs[rows:]
    tokens, width = x.shape
    length = tokens // rows
    inward = []
    for n in range(3):
        cols = pl.ds(n * width, width)
        copies = [pltpu.make_async_copy(triple_w.at[:, cols], tv.at[:, cols], sems.at[4 * n])]
        for row in range(rows):
            copies.append(
                pltpu.make_async_copy(
                    grads[row].at[:, cols],
                    gv.at[pl.ds(row * length, length), cols],
                    sems.at[4 * n + 1 + row],
                )
            )
        start(copies)
        inward.append(copies)
    late = [
        pltpu.make_async_copy(x_i, x, sems.at[12]),
        pltpu.make_async_copy(gmid_i, gmid, sems.at[13]),
    ]
    start(late)
    for n in range(2):
        wait(inward[n])
        cols = slice(n * width, (n + 1) * width)
        for m in range(0, width, 512):
            value = dot_nt(gv[:, cols], tv[m : m + 512, cols])
            first[:, m : m + 512] = value if n == 0 else first[:, m : m + 512] + value
    wait(inward[2])
    wait(late)
    step = 128
    done = []
    last = slice(2 * width, 3 * width)
    for row in range(rows):
        here = slice(row * length, (row + 1) * length)
        first[here, :] = first[here, :] + dot_nt(gv[here, last], tv[:, last])
        for t in range(row * length, (row + 1) * length, step):
            now = slice(t, t + step)
            u, scaled = unit(x[now, :].astype(F32))
            back = norm_back(first[now, :] * gain1[...], u, scaled)
            result[now, :] = (gmid[now, :] + back).astype(BF16)
        at = pl.ds(row * length, length)
        done.append(pltpu.make_async_copy(result.at[at, :], result_o.at[at, :], sems.at[14 + row]))
        done[-1].start()
    wait(done)


def split3(value):
    high = value.astype(BF16)
    rest = value - high.astype(F32)
    mid = rest.astype(BF16)
    return high, mid, (rest - mid.astype(F32)).astype(BF16)


def reparam_body(prefix, pairs, hidden_r, table, inner_w, outer_w, *refs):
    table_o, inner_wo, inner_bo, outer_wo, outer_bo, outer_g, inner_g, sems = refs
    width = pairs.shape[2]
    hidden = hidden_r[...]
    low = jnp.concatenate([hidden.astype(BF16)] * 3, axis=0)
    row = lax.broadcasted_iota(jnp.int32, (PAD, hidden.shape[1]), 0)
    grads = []
    done = []
    for k in (0, 1):
        value = pairs[k]
        parts = jnp.concatenate(split3(value), axis=0)
        cols = slice(k * width, (k + 1) * width)
        outer_g[:, cols] = dot_tn(low, parts)
        at = pl.ds(k * width, width)
        done.append(pltpu.make_async_copy(outer_g.at[:, at], outer_wo.at[:, at], sems.at[k]))
        done[-1].start()
        outer_bo[:, cols] = jnp.sum(value, axis=0, keepdims=True)
        grads.append(dot_nt(parts, outer_w[:, cols]))
    total = grads[0] + grads[1]
    hidden_grad = total[:PAD] + total[PAD : 2 * PAD] + total[2 * PAD :]
    before = jnp.where(row < prefix, hidden_grad * (1.0 - hidden * hidden), 0.0)
    inner_bo[...] = jnp.sum(before, axis=0, keepdims=True)
    stacked = jnp.concatenate(split3(before), axis=0)
    inner_g[...] = dot_tn(jnp.concatenate([table[...]] * 3, axis=0), stacked)
    done.append(pltpu.make_async_copy(inner_g, inner_wo, sems.at[2]))
    done[-1].start()
    back = dot_nt(stacked, inner_w[...])
    table_o[...] = back[:PAD] + back[PAD : 2 * PAD] + back[2 * PAD :]
    wait(done)


def total_pairs(pairs, fsdp, dp):
    if fsdp == 8 and dp == 4:
        rounds = [("fsdp", (1,)), ("fsdp", (2, 4, 6)), ("dp", (1, 2, 3))]
    else:
        rounds = [("fsdp", (1 << k,)) for k in range(fsdp.bit_length() - 1)]
        rounds += [("dp", (1 << k,)) for k in range(dp.bit_length() - 1)]
    sizes = {"fsdp": fsdp, "dp": dp}
    for axis, masks in rounds:
        size = sizes[axis]
        terms = {0: pairs}
        for mask in masks:
            terms[mask] = lax.ppermute(pairs, axis, [(i, i ^ mask) for i in range(size)])
        if len(masks) == 1:
            pairs = terms[0] + terms[masks[0]]
        else:
            low = min(masks)
            pairs = (terms[0] + terms[low]) + (terms[2 * low] + terms[3 * low])
    return pairs


def body(
    fsdp,
    dp,
    activations,
    lengths,
    cotangent,
    gain_first,
    shift_first,
    triple_weight,
    output_weight,
    output_bias,
    gain_second,
    shift_second,
    upward_weight,
    upward_bias,
    downward_weight,
    downward_bias,
    prefix_table,
    inner_weight,
    inner_bias,
    outer_weight,
    outer_bias,
):
    rows, length, width = activations.shape
    tokens = rows * length
    heads = width // HEAD
    wide = upward_bias.shape[0]
    prefix, _ = prefix_table.shape
    mid = inner_bias.shape[0]
    chunk = wide // 4
    place = jnp.stack([lax.axis_index("dp"), lax.axis_index("fsdp")]).astype(jnp.int32)
    x = activations.reshape(tokens, width)
    g = cotangent.reshape(tokens, width)
    flat = lambda v: v.reshape(1, -1)
    dma = lambda n: pltpu.SemaphoreType.DMA((n,))
    vm = pltpu.VMEM

    table = jnp.pad(prefix_table, ((0, PAD - prefix), (0, 0)))
    place, hidden, bdk, bdv, ones = call(
        partial(prefix_body, prefix),
        "prefix",
        [(shaped((2,), jnp.int32), SMEM), (shaped((PAD, mid), F32), VMEM)]
        + [(shaped((heads * PAD, width), BF16), VMEM)] * 3,
        [SMEM] + [VMEM] * 5,
        [],
        3.7,
    )(place, table, inner_weight, flat(inner_bias), outer_weight, flat(outer_bias))

    arrays = {}
    quick = fsdp == 8 and dp > 1
    triple_parts = Pieces(dp, triple_weight)
    output_parts = Pieces(dp, output_weight)
    up_parts = Pieces(dp, upward_weight)
    down_parts = Pieces(dp, packed(downward_weight, triple_weight.shape[0]))
    if quick:
        cut_rows, triple_c = triple_weight.shape
        blocks = downward_weight.shape[0] // cut_rows
        far = list(range(1, dp))
        layout = halves(far, cut_rows)
        near_rows = cut_rows + cut_rows // 2
        far_rows = cut_rows * (dp - 1) // 2
        half = cut_rows // 2
        triple_parts.add("near", [(0, 0, 0, cut_rows, 0, 0)], near_rows)
        triple_parts.add("first", [part + (0,) for part in layout], far_rows)
        output_parts.add("near", [(0, 0, 0, cut_rows, 0, triple_c)], near_rows)
        output_parts.add("first", [part + (triple_c,) for part in layout], far_rows)
        up_parts.add("near", [(1, 0, 0, cut_rows, 0, 0)], near_rows)
        up_parts.add("up", [part + (0,) for part in layout], far_rows)
        down_parts.add("near", [(side, cut_rows, side * half, half, 0, 0) for side in (0, 1)], near_rows)
        down_parts.add("down", [part + (0,) for part in layout], far_rows)

        head = jnp.concatenate([triple_weight, output_weight], axis=1)
        beside = packed(downward_weight, cut_rows)
        near = Spread(
            jnp.concatenate([head, beside[:half]], axis=0),
            jnp.concatenate([upward_weight, beside[half:]], axis=0),
            fsdp,
        )
        near.second(bdk)
        near.put(arrays, "near", range(4))
        first = Spread(*cut(from_planes(head, dp, *near.arrays[2:]), layout), fsdp)
        first.second()
        first.put(arrays, "first", (0, 1))
        up_far = from_planes(after(upward_weight, head), dp, *first.arrays[:2])
        up = Spread(*cut(up_far, layout), fsdp)
        first.put(arrays, "first", (2, 3), *up.first)
        up.second()
        up.put(arrays, "up", (0, 1))
        x = after(x, *up.arrays[:2])
    else:
        whole = (
            (triple_weight, triple_parts),
            (output_weight, output_parts),
            (upward_weight, up_parts),
            (downward_weight, down_parts),
        )
        for k, (weight, parts) in enumerate(whole):
            gathered = lax.all_gather(weight, "fsdp", axis=0, tiled=True)
            arrays["whole", k] = lax.all_gather(gathered, "dp", axis=1, tiled=True)
            parts.whole(("whole", k))

    keys = triple_parts.keys()
    triple, triple_full = call(
        partial(triple_body, triple_parts, keys),
        "triple",
        [(shaped((tokens, 3 * width), BF16), ANY), (shaped((width, 3 * width), BF16), ANY)],
        [SMEM] + [VMEM] * 3 + [ANY] * len(keys),
        [
            vm((width, 3 * width), BF16),
            vm((tokens, width), BF16),
            vm((tokens, 3 * width), BF16),
            dma(len(triple_parts.parts)),
            dma(2 * len(triple_parts.planes()) + 4),
        ],
        0.1,
    )(place, x, flat(gain_first), flat(shift_first), *[arrays[key] for key in keys])
    if quick:
        down_far = from_planes(after(beside, upward_weight), dp, triple)
        down = Spread(*cut(down_far, layout), fsdp)
        triple = after(triple, *down.halves)
    keys = output_parts.keys()
    prob, pre, mix, middle, norm_two, output_full = call(
        partial(attend_body, rows, prefix, output_parts, keys),
        "attend",
        [
            (shaped((rows * heads, length, length), BF16), ANY),
            (shaped((rows, heads * PAD, length), BF16), ANY),
            (shaped((tokens, width), BF16), ANY),
            (shaped((tokens, width), F32), ANY),
            (shaped((tokens, width), BF16), ANY),
            (shaped((width, width), BF16), ANY),
        ],
        [SMEM, SMEM] + [VMEM] * 6 + [ANY] * (1 + len(keys)),
        [
            vm((tokens, 3 * width), BF16),
            vm((width, width), BF16),
            vm((tokens, width), BF16),
            vm((rows * heads, length, length), BF16),
            vm((length, length), F32),
            vm((heads * PAD, length), F32),
            vm((rows, heads * PAD, length), BF16),
            vm((length, width), F32),
            vm((tokens, width), BF16),
            vm((tokens, width), F32),
            dma(rows + len(output_parts.parts)),
            dma(3 + 3 * rows),
        ],
        10,
    )(
        place,
        lengths,
        x,
        flat(output_bias),
        flat(gain_second),
        flat(shift_second),
        bdk,
        bdv,
        triple,
        *[arrays[key] for key in keys],
    )

    if quick:
        up.put(arrays, "up", (2, 3), norm_two)
        down.second(norm_two)
        down.put(arrays, "down", (0, 1))
        norm_two = after(norm_two, *down.arrays[:2])
    keys = up_parts.keys()
    state = []
    planes = up_parts.planes()
    cuts = [planes]
    for k, some in enumerate(cuts):
        state = call(
            partial(upward_body, some, up_parts, keys, len(state)),
            "upward_%d" % k,
            [
                (shaped((tokens, wide), BF16), ANY),
                (shaped((tokens, wide), BF16), ANY),
                (shaped((width, wide), BF16), ANY),
            ],
            [SMEM] + [VMEM] * 2 + [ANY] * (len(keys) + len(state)),
            [
                vm((width, wide), BF16),
                vm((tokens, wide), BF16),
                vm((tokens, wide), BF16),
                dma(len(up_parts.parts)),
                dma(3 * wide // 512),
            ],
            16 / len(cuts),
            aliases={3 + len(keys) + n: n for n in range(len(state))},
        )(place, norm_two, flat(upward_bias), *[arrays[key] for key in keys], *state)
    active, slope, up_full = state

    down_shape = (chunk, width)
    if quick:
        down_shape = (2 * cut_rows, dp * blocks * width // dp)

    def chunk_scratch(count):
        return [
            vm((count, *down_shape), BF16),
            vm((count, width, chunk), BF16),
            vm((count, tokens, chunk), BF16),
            vm((count, tokens, chunk), BF16),
            vm((count, tokens, chunk), BF16),
            vm((tokens, width), F32),
            vm((tokens, width), F32),
        ]

    sums = [(shaped((tokens, width), F32), ANY)] * 2
    n_sems = len(down_parts.parts) + 8
    n_io = 2 + 2 * width // 512
    keys = down_parts.of((0,)).keys()
    second, out = call(
        partial(chunk_body, (0,), down_parts.of((0,)), keys),
        "chunk_own",
        sums,
        [SMEM] + [ANY] * (4 + len(keys)),
        chunk_scratch(1) + [vm((tokens, width), BF16), dma(n_sems), dma(n_io)],
        8,
    )(place, g, active, slope, up_full, *[arrays[key] for key in keys])
    if quick:
        down.put(arrays, "down", (2, 3), second)
    keys = down_parts.of((1, 2, 3)).keys()
    result, g_middle, g_mix, delta, d_pre, pairs = call(
        partial(middle_body, rows, (1, 2, 3), down_parts.of((1, 2, 3)), keys),
        "middle",
        [
            (shaped((tokens, width), BF16), ANY),
            (shaped((tokens, width), F32), ANY),
            (shaped((tokens, width), BF16), ANY),
            (shaped((rows, heads * PAD, length), F32), VMEM),
            (shaped((rows, heads * PAD, length), BF16), VMEM),
            (shaped((2, PAD, width), F32), VMEM),
        ],
        [SMEM] + [ANY] * (4 + len(keys)) + [ANY] * 3 + [VMEM] * 2 + [ANY] * 6,
        chunk_scratch(3)
        + [
            vm((tokens, width), F32),
            vm((width, width), BF16),
            vm((tokens, width), BF16),
            vm((tokens, width), BF16),
            vm((tokens, width), BF16),
            vm((tokens, width), BF16),
            vm((tokens, width), BF16),
            vm((rows, heads * PAD, length), BF16),
            vm((heads * PAD, width), BF16),
            vm((heads * PAD, width), BF16),
            vm((tokens, width), BF16),
            dma(n_sems),
            dma(13),
        ],
        23,
    )(
        place,
        g,
        active,
        slope,
        up_full,
        *[arrays[key] for key in keys],
        second,
        out,
        middle,
        flat(gain_second),
        flat(downward_bias),
        output_full,
        mix,
        triple,
        pre,
        bdv,
        ones,
    )

    grads = []
    for row in range(rows):
        grads += call(
            partial(attend_back_body, row, length, heads),
            "attend_back_%d" % row,
            [(shaped((length, 3 * width), BF16), ANY)],
            [ANY] * 3 + [VMEM] * 3,
            [
                vm((length, 3 * width), BF16),
                vm((length, width), BF16),
                vm((heads, length, length), BF16),
                vm((length, width), F32),
                vm((length, 3 * width), BF16),
                dma(32),
            ],
            8.5,
        )(triple, g_mix, prob, delta, d_pre, bdk)

    (input_grad,) = call(
        partial(input_body, rows),
        "input",
        [(shaped((tokens, width), BF16), ANY)],
        [ANY] * rows + [ANY] * 2 + [VMEM] + [ANY],
        [
            vm((width, 3 * width), BF16),
            vm((tokens, 3 * width), BF16),
            vm((tokens, width), F32),
            vm((tokens, width), F32),
            vm((tokens, width), BF16),
            vm((tokens, width), BF16),
            dma(14 + rows),
        ],
        9,
    )(*grads, triple_full, x, flat(gain_first), g_middle)

    pairs = total_pairs(pairs, fsdp, dp)
    table_grad, inner_w_grad, inner_b_grad, outer_w_grad, outer_b_grad = call(
        partial(reparam_body, prefix),
        "reparam",
        [
            (shaped((PAD, width), F32), VMEM),
            (shaped((width, mid), F32), ANY),
            (shaped((1, mid), F32), VMEM),
            (shaped((mid, 2 * width), F32), ANY),
            (shaped((1, 2 * width), F32), VMEM),
        ],
        [VMEM] * 5,
        [vm((mid, 2 * width), F32), vm((width, mid), F32), dma(3)],
        6,
        room=10,
    )(pairs, hidden, table, inner_weight, outer_weight)
    return (
        result.reshape(rows, length, width),
        input_grad.reshape(rows, length, width),
        table_grad[:prefix],
        inner_w_grad,
        inner_b_grad.reshape(-1),
        outer_w_grad,
        outer_b_grad.reshape(-1),
    )


def solution(mesh):
    in_specs = (
        P(("dp", "fsdp"), None, None),
        P(("dp", "fsdp"), None),
        P(("dp", "fsdp"), None, None),
        P(),
        P(),
        P("fsdp", "dp"),
        P("fsdp", "dp"),
        P(),
        P(),
        P(),
        P("fsdp", "dp"),
        P(),
        P("fsdp", "dp"),
        P(),
        P(),
        P(),
        P(),
        P(),
        P(),
    )
    out_specs = (
        P(("dp", "fsdp"), None, None),
        P(("dp", "fsdp"), None, None),
        P(),
        P(),
        P(),
        P(),
        P(),
    )
    return jax.shard_map(
        partial(body, mesh.shape["fsdp"], mesh.shape["dp"]),
        mesh=mesh,
        in_specs=in_specs,
        out_specs=out_specs,
        check_vma=False,
    )
```

```python
import math
from functools import partial

import jax
import jax.numpy as jnp
from jax import lax
from jax.experimental import pallas as pl
from jax.experimental.pallas import tpu as pltpu
from jax.sharding import PartitionSpec as P

HEAD = 64
PAD = 16
MASKED = -1e30
F32 = jnp.float32
BF16 = jnp.bfloat16
GELU_C = 0.7978845608028654
GELU_A = 0.044715
PEAK = 1.15e9

ANY = pl.BlockSpec(memory_space=pl.ANY)
VMEM = pl.BlockSpec(memory_space=pltpu.VMEM)
SMEM = pl.BlockSpec(memory_space=pltpu.SMEM)


def dot(a, b):
    return lax.dot_general(a, b, (((1,), (0,)), ((), ())), preferred_element_type=F32)


def dot_nt(a, b):
    return lax.dot_general(a, b, (((1,), (1,)), ((), ())), preferred_element_type=F32)


def dot_tn(a, b):
    return lax.dot_general(a, b, (((0,), (0,)), ((), ())), preferred_element_type=F32)


def unit(values):
    center = values - jnp.mean(values, axis=-1, keepdims=True)
    scaled = lax.rsqrt(jnp.mean(center * center, axis=-1, keepdims=True) + 1e-05)
    return center * scaled, scaled


def norm_back(upstream, unit_rows, scaled):
    return scaled * (
        upstream
        - jnp.mean(upstream, axis=-1, keepdims=True)
        - unit_rows * jnp.mean(upstream * unit_rows, axis=-1, keepdims=True)
    )


def call(body, name, outs, ins, scratch, micros, room=None, aliases={}):
    held = sum(
        math.prod(s.shape) * jnp.dtype(s.dtype).itemsize
        for s in scratch
        if jnp.issubdtype(s.dtype, jnp.floating)
    )
    limit = 50 * 1024 * 1024 if room is None else held + room * 1024 * 1024
    return pl.pallas_call(
        body,
        name=name,
        out_shape=[o[0] for o in outs],
        out_specs=[o[1] for o in outs],
        in_specs=ins,
        scratch_shapes=scratch,
        input_output_aliases=aliases,
        compiler_params=pltpu.CompilerParams(vmem_limit_bytes=limit),
        cost_estimate=pl.CostEstimate(
            flops=int(micros * PEAK), bytes_accessed=0, transcendentals=0
        ),
    )


def shaped(shape, dtype):
    return jax.ShapeDtypeStruct(shape, dtype)


class Pieces:
    def __init__(self, dp, shard):
        self.dp = dp
        self.shard_rows, self.shard_cols = shard.shape
        self.parts = []
        self.split = True

    def whole(self, key):
        self.split = False
        self.parts.append((key, None, None, None, 0, None, None))
        return self

    def add(self, stage, layout, rows):
        where = {(0, 0): (0, 0), (1, 0): (0, 1), (0, 1): (1, 0), (2, 1): (1, 1)}
        where.update({(2, 0): (2, 0), (3, 0): (2, 1), (1, 1): (3, 0), (3, 1): (3, 1)})
        for core in (0, 1):
            for way in range(4):
                for side, src_row, low, count, plane, col in layout:
                    array, second = where[way, side]
                    key = (stage, array, core)
                    src = src_row + second * rows
                    self.parts.append((key, src, low, count, plane, 2 * way | core, col))
        return self

    def of(self, picks):
        out = Pieces.__new__(Pieces)
        out.__dict__.update(self.__dict__)
        out.parts = [p for p in self.parts if not self.split or p[5] >> 1 in picks]
        return out

    def keys(self):
        return sorted({part[0] for part in self.parts})

    def planes(self):
        return sorted({part[4] for part in self.parts})

    def columns(self, place, plane):
        if not self.split:
            return 0, self.shard_cols * self.dp
        across = lax.rem(place[0] + plane, self.dp)
        return pl.multiple_of(across * self.shard_cols, 128), self.shard_cols

    def copies(self, refs, dst, sems, base, place, plane=None, paired=False):
        out = []
        for key, src_row, low, count, at, flip, col in self.parts:
            if plane is not None and at != plane:
                continue
            if not self.split:
                out.append(pltpu.make_async_copy(refs[key], dst, sems.at[base + len(out)]))
                continue
            owner = jnp.bitwise_xor(place[1], flip)
            if paired:
                owner = jnp.bitwise_and(owner, 1)
            row = pl.multiple_of(owner * self.shard_rows + low, 16)
            column, cols = self.columns(place, at)
            out.append(
                pltpu.make_async_copy(
                    refs[key].at[pl.ds(src_row, count), pl.ds(col, cols)],
                    dst.at[pl.ds(row, count), pl.ds(column, cols)],
                    sems.at[base + len(out)],
                )
            )
        return out


def position():
    return lax.axis_index("dp"), lax.axis_index("fsdp")


def start(copies):
    for c in copies:
        c.start()


def wait(copies):
    for c in copies:
        c.wait()


def after(value, *others):
    return lax.optimization_barrier((value, *others))[0]


def flip(value, mask, size):
    return lax.ppermute(value, "fsdp", [(i, i ^ mask) for i in range(size)])


class Spread:
    def __init__(self, low, high, size):
        self.size = size
        self.halves = low, high
        self.first = flip(low, 2, size), flip(high, 4, size)

    def second(self, *others):
        self.arrays = [
            jnp.concatenate([half, after(came, *others)], axis=0)
            for half, came in zip(self.halves, self.first)
        ]
        self.arrays.append(flip(self.arrays[0], 4, self.size))
        self.arrays.append(flip(self.arrays[1], 2, self.size))

    def put(self, arrays, stage, which, *others):
        for k in which:
            arrays[stage, k, 0] = self.arrays[k]
            arrays[stage, k, 1] = flip(after(self.arrays[k], *others), 1, self.size)


def packed(value, rows):
    return jnp.concatenate(
        [value[k : k + rows] for k in range(0, value.shape[0], rows)], axis=1
    )


def halves(planes, shard_rows):
    total = shard_rows * len(planes)
    middle = total // 2
    out = []
    for k, plane in enumerate(planes):
        for side, (first, last) in enumerate(((0, middle), (middle, total))):
            low, high = max(first, k * shard_rows), min(last, (k + 1) * shard_rows)
            if low < high:
                out.append((side, low - first, low - k * shard_rows, high - low, plane))
    return out


def cut(shards, layout):
    return [
        jnp.concatenate(
            [shards[p][low : low + count] for s, _, low, count, p in layout if s == side], axis=0
        )
        for side in (0, 1)
    ]


def from_planes(value, dp, *others):
    planes = after(lax.all_gather(value, "dp", axis=0, tiled=False), *others)
    here = lax.axis_index("dp")
    return {
        j: lax.dynamic_index_in_dim(planes, lax.rem(here + j, dp), 0, keepdims=False)
        for j in range(1, dp)
    }


def prefix_body(
    prefix, lengths, table, inner_w, inner_b, outer_w, outer_b, bias_o, hidden_o, keys_o, values_o, ones_o
):
    rows, length, _ = bias_o.shape
    for row in range(rows):
        key = lax.broadcasted_iota(jnp.int32, (length, length), 0)
        query = lax.broadcasted_iota(jnp.int32, (length, length), 1)
        key_seg = jnp.zeros((length, length), jnp.int32)
        query_seg = jnp.zeros((length, length), jnp.int32)
        bound = 0
        for s in range(lengths.shape[1]):
            bound = bound + lengths[row, s]
            key_seg = key_seg + jnp.where(key >= bound, 1, 0)
            query_seg = query_seg + jnp.where(query >= bound, 1, 0)
        seen = (key_seg == query_seg) & (key <= query)
        bias_o[row] = jnp.where(seen, 0.0, MASKED)
    width = keys_o.shape[1]
    hidden = jnp.tanh(dot(table[...], inner_w[...]) + inner_b[...])
    hidden_o[...] = hidden
    pairs = (dot(hidden.astype(BF16), outer_w[...]) + outer_b[...]).astype(BF16).astype(F32)
    shape = keys_o.shape
    row = lax.broadcasted_iota(jnp.int32, shape, 0)
    col = lax.broadcasted_iota(jnp.int32, shape, 1)
    inside = (row // PAD) == (col // HEAD)
    real = inside & (lax.rem(row, PAD) < prefix)
    heads = shape[0] // PAD
    keys_o[...] = jnp.where(real, jnp.tile(pairs[:, :width], (heads, 1)), 0.0).astype(BF16)
    values_o[...] = jnp.where(real, jnp.tile(pairs[:, width:], (heads, 1)), 0.0).astype(BF16)
    head = lax.broadcasted_iota(jnp.int32, ones_o.shape, 0)
    lane = lax.broadcasted_iota(jnp.int32, ones_o.shape, 1)
    ones_o[...] = jnp.where(head == lane // HEAD, 1.0, 0.0).astype(BF16)


def triple_body(parts, keys, *refs):
    n_arrays = len(keys)
    place = position()
    x, gain, shift = refs[:3]
    arrays = dict(zip(keys, refs[3 : 3 + n_arrays]))
    triple_o, t_o, tv, normed, tri, sems, out_sems = refs[3 + n_arrays :]
    tokens, _ = x.shape
    inward = []
    base = 0
    for plane in parts.planes():
        inward.append((plane, parts.copies(arrays, tv, sems, base, place, plane)))
        base += len(inward[-1][1])
        start(inward[-1][1])
    outs = []

    def send(src, dst):
        outs.append(pltpu.make_async_copy(src, dst, out_sems.at[len(outs)]))
        outs[-1].start()

    step = 128
    for t in range(0, tokens, step):
        u, _ = unit(x[t : t + step, :].astype(F32))
        normed[t : t + step, :] = (u * gain[...] + shift[...]).astype(BF16)
    for plane, copies in inward:
        wait(copies)
        column, count = parts.columns(place, plane)
        block = count if count <= 1024 else 1024
        for n in range(0, count, block):
            cols = pl.ds(column + n, block)
            if not isinstance(column, int):
                cols = pl.ds(pl.multiple_of(column + n, 128), block)
            tri[:, cols] = dot(normed[...], tv[:, cols]).astype(BF16)
            send(tri.at[:, cols], triple_o.at[:, cols])
            send(tv.at[:, cols], t_o.at[:, cols])
    wait(outs)


def attend_body(rows, prefix, parts, keys, *refs):
    n_arrays = len(keys)
    place = position()
    bias, x, out_b, gain, shift, bdk, bdv, triple = refs[:8]
    arrays = dict(zip(keys, refs[8 : 8 + n_arrays]))
    prob_o, pre_o, mix_o, middle_o, norm_o, o_o = refs[8 + n_arrays : 14 + n_arrays]
    (tri, ov, normed, prob, spre, pre, main, mix, middle, sems, out_sems) = refs[14 + n_arrays :]
    tokens, width = x.shape
    length = tokens // rows
    heads = width // HEAD
    scale = HEAD ** (-0.5)
    step = 128
    inward = [
        pltpu.make_async_copy(
            triple.at[pl.ds(row * length, length), :],
            tri.at[pl.ds(row * length, length), :],
            sems.at[row],
        )
        for row in range(rows)
    ]
    start(inward)
    in_o = parts.copies(arrays, ov, sems, rows, place)
    start(in_o)
    outs = []

    def send(src, dst):
        outs.append(pltpu.make_async_copy(src, dst, out_sems.at[len(outs)]))
        outs[-1].start()

    lane = lax.broadcasted_iota(jnp.int32, (length, 2 * HEAD), 1)
    low_lane = lane < HEAD
    for row in range(rows):
        here = slice(row * length, (row + 1) * length)
        inward[row].wait()
        raw = dot_nt(bdk[...], tri[here, :width]) * scale
        pre_row = lax.broadcasted_iota(jnp.int32, raw.shape, 0)
        spre[...] = jnp.where(lax.rem(pre_row, PAD) < prefix, raw, MASKED)
        for i in range(heads // 2):
            cols = i * 2 * HEAD
            q = tri[here, cols : cols + 2 * HEAD]
            k = tri[here, width + cols : width + cols + 2 * HEAD]
            v = tri[here, 2 * width + cols : 2 * width + cols + 2 * HEAD]
            found = []
            for sub in (0, 1):
                qm = jnp.where(low_lane if sub == 0 else ~low_lane, q, jnp.zeros_like(q))
                s = dot_nt(k, qm) * scale + bias[row]
                at = (2 * i + sub) * PAD
                sp = spre[at : at + PAD, :]
                top = jnp.maximum(
                    jnp.max(s, axis=0, keepdims=True), jnp.max(sp, axis=0, keepdims=True)
                )
                e = jnp.exp(s - top)
                ep = jnp.exp(sp - top)
                inverse = 1.0 / (
                    jnp.sum(e, axis=0, keepdims=True) + jnp.sum(ep, axis=0, keepdims=True)
                )
                p = (e * inverse).astype(BF16)
                prob[row * heads + 2 * i + sub] = p
                pre[row, at : at + PAD, :] = (ep * inverse).astype(BF16)
                found.append(dot_tn(p, v))
            main[:, cols : cols + 2 * HEAD] = jnp.where(low_lane, found[0], found[1])
        send(prob.at[pl.ds(row * heads, heads)], prob_o.at[pl.ds(row * heads, heads)])
        if row == 0:
            wait(in_o)
            send(ov, o_o)
        mix[here, :] = (main[...] + dot_tn(pre[row], bdv[...])).astype(BF16)
        middle[here, :] = x[here, :].astype(F32) + dot(mix[here, :], ov[...]) + out_b[...]
        for t in range(row * length, (row + 1) * length, step):
            u, _ = unit(middle[t : t + step, :])
            normed[t : t + step, :] = (u * gain[...] + shift[...]).astype(BF16)
        send(middle.at[pl.ds(row * length, length), :], middle_o.at[pl.ds(row * length, length), :])
        send(normed.at[pl.ds(row * length, length), :], norm_o.at[pl.ds(row * length, length), :])
    send(pre, pre_o)
    send(mix, mix_o)
    wait(outs)


def upward_body(planes, parts, keys, carried, *refs):
    n_arrays = len(keys)
    place = position()
    norm, bias = refs[:2]
    arrays = dict(zip(keys, refs[2 : 2 + n_arrays]))
    n_arrays += carried
    active_o, slope_o, up_o = refs[2 + n_arrays : 5 + n_arrays]
    uv, active, slope, sems, out_sems = refs[5 + n_arrays :]
    inward = []
    base = 0
    for plane in planes:
        inward.append((plane, parts.copies(arrays, uv, sems, base, place, plane)))
        base += len(inward[-1][1])
        start(inward[-1][1])
    outs = []

    def send(src, dst):
        outs.append(pltpu.make_async_copy(src, dst, out_sems.at[len(outs)]))
        outs[-1].start()

    for plane, copies in inward:
        wait(copies)
        column, count = parts.columns(place, plane)
        block = 512
        for n in range(0, count, block):
            cols = pl.ds(column + n, block)
            if not isinstance(column, int):
                cols = pl.ds(pl.multiple_of(column + n, 128), block)
            u = dot(norm[...], uv[:, cols]) + bias[:, cols]
            square = u * u
            half = 0.5 + 0.5 * jnp.tanh(u * (GELU_C + GELU_C * GELU_A * square))
            active[:, cols] = (u * half).astype(BF16)
            slope[:, cols] = (
                half
                + (u * (half - half * half)) * (2.0 * GELU_C + 6.0 * GELU_C * GELU_A * square)
            ).astype(BF16)
            send(active.at[:, cols], active_o.at[:, cols])
            send(slope.at[:, cols], slope_o.at[:, cols])
            send(uv.at[:, cols], up_o.at[:, cols])
    wait(outs)


class Chunk:
    def __init__(self, place, pick, parts, arrays, full, held, slot, sems, base):
        active, slope, upward = full
        self.dv, self.uc, self.ac, self.sc, self.gu = (h.at[slot] for h in held)
        size = self.uc.shape[1]
        self.split = parts.split
        if not parts.split:
            cols = rows = pl.ds(pick * size, size)
            (whole,) = arrays.values()
            self.down = [pltpu.make_async_copy(whole.at[rows, :], self.dv, sems.at[base])]
        else:
            at = jnp.bitwise_xor(lax.shift_right_logical(place[1], 1), pick)
            self.down = parts.of((pick,)).copies(
                arrays, self.dv, sems, base, place, paired=True
            )
            self.planes, self.shard_rows = parts.dp, parts.shard_rows
            cols = pl.ds(pl.multiple_of(at * size, size), size)
        base += len(self.down)
        self.sems = len(self.down) + 3
        self.rest = [
            pltpu.make_async_copy(slope.at[:, cols], self.sc, sems.at[base]),
            pltpu.make_async_copy(upward.at[:, cols], self.uc, sems.at[base + 1]),
            pltpu.make_async_copy(active.at[:, cols], self.ac, sems.at[base + 2]),
        ]

    def blocks(self):
        rows = self.shard_rows
        size = self.uc.shape[1]
        count = size // (2 * rows)
        return [(k, (k * rows, size // 2 + k * rows)) for k in range(count)]

    def upstream(self, g):
        wait(self.down)
        self.rest[0].wait()
        size = self.uc.shape[1]
        if not self.split:
            for n in range(0, size, 512):
                cols = slice(n, n + 512)
                value = dot_nt(g[...], self.dv[cols, :])
                self.gu[:, cols] = (value * self.sc[:, cols].astype(F32)).astype(BF16)
            return
        width = g.shape[1] // self.planes
        rows = self.shard_rows
        for k, places in self.blocks():
            value = 0.0
            for z in range(self.planes):
                at = z * self.dv.shape[1] // self.planes + k * width
                value = value + dot_nt(g[:, z * width : (z + 1) * width], self.dv[:, at : at + width])
            for n, low in enumerate(places):
                cols = slice(low, low + rows)
                part = value[:, n * rows : (n + 1) * rows]
                self.gu[:, cols] = (part * self.sc[:, cols].astype(F32)).astype(BF16)

    def back(self):
        self.rest[1].wait()
        return lambda cols: dot_nt(self.gu[...], self.uc[cols, :])

    def ahead(self):
        self.rest[2].wait()
        if not self.split:
            return lambda cols: dot(self.ac[...], self.dv[:, cols])
        rows = self.shard_rows

        def term(cols):
            width = self.uc.shape[0] // self.planes
            found = []
            for z in range(cols.start // width, cols.stop // width):
                value = 0.0
                for k, places in self.blocks():
                    at = z * self.dv.shape[1] // self.planes + k * width
                    left = jnp.concatenate([self.ac[:, low : low + rows] for low in places], axis=1)
                    value = value + dot(left, self.dv[:, at : at + width])
                found.append(value)
            return jnp.concatenate(found, axis=1)

        return term


def middle_body(rows, picks, parts, keys, *refs):
    n_arrays = len(keys)
    place = position()
    g, active, slope, upward = refs[:4]
    arrays = dict(zip(keys, refs[4 : 4 + n_arrays]))
    middle_i, gain2, down_b, output_w, mix, triple, pre, bdv, ones = refs[
        4 + n_arrays : 13 + n_arrays
    ]
    result_o, gmid_o, gmix_o, delta_o, dspre_o, pairs_o = refs[13 + n_arrays : 19 + n_arrays]
    mix_i, pre_i, bdv_i, ones_i, g_i = mix, pre, bdv, ones, g
    (dv, uc, ac, sc, gu, second, middle, ov, low, gmix, q, result) = refs[
        19 + n_arrays : 31 + n_arrays
    ]
    mix, pre, bdv, ones, g, sems, io_sems = refs[31 + n_arrays :]
    tokens, width = g.shape
    g_copy = pltpu.make_async_copy(g_i, g, io_sems.at[12])
    g_copy.start()
    length = tokens // rows
    heads = width // HEAD
    scale = HEAD ** (-0.5)
    chunks = []
    base = 0
    for k, pick in enumerate(picks):
        chunks.append(
            Chunk(
                place, pick, parts, arrays, (active, slope, upward), (dv, uc, ac, sc, gu), k, sems, base
            )
        )
        base += chunks[-1].sems
    for chunk in chunks:
        start(chunk.down)
        start(chunk.rest[:1])
    for k in (1, 2):
        for chunk in chunks:
            start(chunk.rest[k : k + 1])
    carried = [
        pltpu.make_async_copy(middle_i, middle, io_sems.at[2]),
        pltpu.make_async_copy(output_w, ov, io_sems.at[3]),
        pltpu.make_async_copy(triple.at[:, pl.ds(0, width)], q, io_sems.at[4]),
        pltpu.make_async_copy(mix_i, mix, io_sems.at[8]),
        pltpu.make_async_copy(pre_i, pre, io_sems.at[9]),
        pltpu.make_async_copy(bdv_i, bdv, io_sems.at[10]),
        pltpu.make_async_copy(ones_i, ones, io_sems.at[11]),
    ]
    start(carried)
    g_copy.wait()
    for chunk in chunks:
        chunk.upstream(g)
    back = [chunk.back() for chunk in chunks]
    ahead = [chunk.ahead() for chunk in chunks]
    wait(carried)
    for n in range(0, width, 512):
        cols = slice(n, n + 512)
        value = back[0](cols)
        for term in back[1:]:
            value = value + term(cols)
        second[:, cols] = value
    step = 128
    for t in range(0, tokens, step):
        here = slice(t, t + step)
        u, scaled = unit(middle[here, :])
        gm = g[here, :].astype(F32) + norm_back(second[here, :] * gain2[...], u, scaled)
        second[here, :] = gm
        low[here, :] = gm.astype(BF16)
    done = [pltpu.make_async_copy(second, gmid_o, io_sems.at[5])]
    done[-1].start()
    for row in range(rows):
        here = slice(row * length, (row + 1) * length)
        gmix[here, :] = dot_nt(low[here, :], ov[...]).astype(BF16)
    done.append(pltpu.make_async_copy(gmix, gmix_o, io_sems.at[6]))
    done[-1].start()
    for n in range(0, width, 512):
        cols = slice(n, n + 512)
        value = middle[:, cols] + down_b[:, cols]
        for term in ahead:
            value = value + term(cols)
        result[:, cols] = value.astype(BF16)
    done.append(pltpu.make_async_copy(result, result_o, io_sems.at[7]))
    done[-1].start()
    keys = 0.0
    values = 0.0
    for row in range(rows):
        here = slice(row * length, (row + 1) * length)
        up = gmix[here, :]
        product = up.astype(F32) * mix[here, :].astype(F32)
        high = product.astype(BF16)
        small = (product - high.astype(F32)).astype(BF16)
        delta = dot_nt(ones[...], high) + dot_nt(ones[...], small)
        delta_o[row] = delta
        each = jnp.broadcast_to(delta[:, None, :], (heads, PAD, length)).reshape(-1, length)
        p = pre[row]
        ds = (p.astype(F32) * (dot_nt(bdv[...], up) - each)).astype(BF16)
        dspre_o[row] = ds
        keys = keys + dot(ds, q[here, :])
        values = values + dot(p, up)
    row = lax.broadcasted_iota(jnp.int32, keys.shape, 0)
    col = lax.broadcasted_iota(jnp.int32, keys.shape, 1)
    inside = (row // PAD) == (col // HEAD)
    keys = jnp.where(inside, keys * scale, 0.0).reshape(heads, PAD, width)
    values = jnp.where(inside, values, 0.0).reshape(heads, PAD, width)
    pairs_o[0] = jnp.sum(keys, axis=0)
    pairs_o[1] = jnp.sum(values, axis=0)
    wait(done)


def attend_back_body(row, length, heads, triple, gmix, prob, delta, dspre_i, bdk_i, *refs):
    out_o, tri, up, p, before, out, dspre, bdk, sems = refs
    width = heads * HEAD
    scale = HEAD ** (-0.5)
    here = pl.ds(row * length, length)
    groups = 4
    span = heads // groups
    inward = []
    for n in range(groups):
        cols = pl.ds(n * span * HEAD, span * HEAD)
        copies = [
            pltpu.make_async_copy(
                triple.at[here, pl.ds(m * width + n * span * HEAD, span * HEAD)],
                tri.at[:, pl.ds(m * width + n * span * HEAD, span * HEAD)],
                sems.at[5 * n + m],
            )
            for m in range(3)
        ]
        copies.append(pltpu.make_async_copy(gmix.at[here, cols], up.at[:, cols], sems.at[5 * n + 3]))
        copies.append(
            pltpu.make_async_copy(
                prob.at[pl.ds(row * heads + n * span, span)],
                p.at[pl.ds(n * span, span)],
                sems.at[5 * n + 4],
            )
        )
        start(copies)
        inward.append(copies)
        if n == 0:
            side = [
                pltpu.make_async_copy(dspre_i.at[row], dspre, sems.at[32]),
                pltpu.make_async_copy(bdk_i, bdk, sems.at[33]),
            ]
            start(side)
    low_lane = lax.broadcasted_iota(jnp.int32, (length, 2 * HEAD), 1) < HEAD
    wait(side)
    before[...] = dot_tn(dspre[...], bdk[...])
    done = []

    def columns(m, h):
        low = m * width + h // 2 * 2 * HEAD
        return slice(low, low + 2 * HEAD)

    def own(value, h):
        return jnp.where(low_lane if h % 2 == 0 else ~low_lane, value, jnp.zeros_like(value))

    lead = 2
    upstream, scores, half = {}, {}, {}
    for turn in range(heads + 2 * lead):
        h = turn
        if h < heads:
            if h % span == 0:
                wait(inward[h // span])
            upstream[h] = dot_nt(tri[:, columns(2, h)], own(up[:, columns(0, h)], h))
        h = turn - lead
        if 0 <= h < heads:
            d = delta[row, h : h + 1, :]
            scores[h] = (p[h].astype(F32) * (upstream.pop(h) - d)).astype(BF16)
        h = turn - 2 * lead
        if 0 <= h < heads:
            ds = scores.pop(h)
            found = (
                dot_tn(ds, own(tri[:, columns(1, h)], h)),
                dot(ds, own(tri[:, columns(0, h)], h)),
                dot(p[h], own(up[:, columns(0, h)], h)),
            )
            if h % 2 == 0:
                half[h] = found
                continue
            queries, keys, values = (a + b for a, b in zip(half.pop(h - 1), found))
            out[:, columns(0, h)] = ((queries + before[:, columns(0, h)]) * scale).astype(BF16)
            out[:, columns(1, h)] = (keys * scale).astype(BF16)
            out[:, columns(2, h)] = values.astype(BF16)
            if (h + 1) % span == 0:
                for m in range(3):
                    at = pl.ds(m * width + (h + 1 - span) * HEAD, span * HEAD)
                    done.append(
                        pltpu.make_async_copy(
                            out.at[:, at], out_o.at[:, at], sems.at[5 * groups + len(done)]
                        )
                    )
                    done[-1].start()
    wait(done)


def input_body(rows, *refs):
    grads = refs[:rows]
    triple_w, x_i, gain1, gmid_i, result_o, tv, gv, first, gmid, x, result, sems = refs[rows:]
    tokens, width = x.shape
    length = tokens // rows
    inward = []
    cuts = [(0, width // 2), (width // 2, width), (width, 2 * width), (2 * width, 3 * width)]
    for n, (low, high) in enumerate(cuts):
        cols = pl.ds(low, high - low)
        copies = [
            pltpu.make_async_copy(triple_w.at[:, cols], tv.at[:, cols], sems.at[n * (rows + 1)])
        ]
        for row in range(rows):
            copies.append(
                pltpu.make_async_copy(
                    grads[row].at[:, cols],
                    gv.at[pl.ds(row * length, length), cols],
                    sems.at[n * (rows + 1) + 1 + row],
                )
            )
        start(copies)
        inward.append(copies)
    late = [
        pltpu.make_async_copy(x_i, x, sems.at[4 * (rows + 1)]),
        pltpu.make_async_copy(gmid_i, gmid, sems.at[4 * (rows + 1) + 1]),
    ]
    start(late)
    for n in range(3):
        wait(inward[n])
        cols = slice(*cuts[n])
        for m in range(0, width, 512):
            value = dot_nt(gv[:, cols], tv[m : m + 512, cols])
            first[:, m : m + 512] = value if n == 0 else first[:, m : m + 512] + value
    wait(inward[3])
    wait(late)
    step = 128
    done = []
    last = slice(2 * width, 3 * width)
    for row in range(rows):
        here = slice(row * length, (row + 1) * length)
        first[here, :] = first[here, :] + dot_nt(gv[here, last], tv[:, last])
        for t in range(row * length, (row + 1) * length, step):
            now = slice(t, t + step)
            u, scaled = unit(x[now, :].astype(F32))
            back = norm_back(first[now, :] * gain1[...], u, scaled)
            result[now, :] = (gmid[now, :] + back).astype(BF16)
        at = pl.ds(row * length, length)
        done.append(pltpu.make_async_copy(result.at[at, :], result_o.at[at, :], sems.at[4 * (rows + 1) + 2 + row]))
        done[-1].start()
    wait(done)


def split3(value):
    high = value.astype(BF16)
    rest = value - high.astype(F32)
    mid = rest.astype(BF16)
    return high, mid, (rest - mid.astype(F32)).astype(BF16)


def reparam_body(prefix, pairs, hidden_r, table, inner_w, outer_w, *refs):
    table_o, inner_wo, inner_bo, outer_wo, outer_bo, outer_g, inner_g, sems = refs
    width = pairs.shape[2]
    hidden = hidden_r[...]
    low = jnp.concatenate([hidden.astype(BF16)] * 3, axis=0)
    row = lax.broadcasted_iota(jnp.int32, (PAD, hidden.shape[1]), 0)
    grads = []
    done = []
    for k in (0, 1):
        value = pairs[k]
        parts = jnp.concatenate(split3(value), axis=0)
        cols = slice(k * width, (k + 1) * width)
        outer_g[:, cols] = dot_tn(low, parts)
        at = pl.ds(k * width, width)
        done.append(pltpu.make_async_copy(outer_g.at[:, at], outer_wo.at[:, at], sems.at[k]))
        done[-1].start()
        outer_bo[:, cols] = jnp.sum(value, axis=0, keepdims=True)
        grads.append(dot_nt(parts, outer_w[:, cols]))
    total = grads[0] + grads[1]
    hidden_grad = total[:PAD] + total[PAD : 2 * PAD] + total[2 * PAD :]
    before = jnp.where(row < prefix, hidden_grad * (1.0 - hidden * hidden), 0.0)
    inner_bo[...] = jnp.sum(before, axis=0, keepdims=True)
    stacked = jnp.concatenate(split3(before), axis=0)
    inner_g[...] = dot_tn(jnp.concatenate([table[...]] * 3, axis=0), stacked)
    done.append(pltpu.make_async_copy(inner_g, inner_wo, sems.at[2]))
    done[-1].start()
    back = dot_nt(stacked, inner_w[...])
    table_o[...] = back[:PAD] + back[PAD : 2 * PAD] + back[2 * PAD :]
    wait(done)


def total_pairs(pairs, fsdp, dp):
    if fsdp == 8 and dp == 4:
        rounds = [("fsdp", (1,)), ("fsdp", (2, 4, 6)), ("dp", (1, 2, 3))]
    else:
        rounds = [("fsdp", (1 << k,)) for k in range(fsdp.bit_length() - 1)]
        rounds += [("dp", (1 << k,)) for k in range(dp.bit_length() - 1)]
    sizes = {"fsdp": fsdp, "dp": dp}
    for axis, masks in rounds:
        size = sizes[axis]
        terms = {0: pairs}
        for mask in masks:
            terms[mask] = lax.ppermute(pairs, axis, [(i, i ^ mask) for i in range(size)])
        if len(masks) == 1:
            pairs = terms[0] + terms[masks[0]]
        else:
            low = min(masks)
            pairs = (terms[0] + terms[low]) + (terms[2 * low] + terms[3 * low])
    return pairs


def body(
    fsdp,
    dp,
    activations,
    lengths,
    cotangent,
    gain_first,
    shift_first,
    triple_weight,
    output_weight,
    output_bias,
    gain_second,
    shift_second,
    upward_weight,
    upward_bias,
    downward_weight,
    downward_bias,
    prefix_table,
    inner_weight,
    inner_bias,
    outer_weight,
    outer_bias,
):
    rows, length, width = activations.shape
    tokens = rows * length
    heads = width // HEAD
    wide = upward_bias.shape[0]
    prefix, _ = prefix_table.shape
    mid = inner_bias.shape[0]
    chunk = wide // 4
    x = activations.reshape(tokens, width)
    g = cotangent.reshape(tokens, width)
    flat = lambda v: v.reshape(1, -1)
    dma = lambda n: pltpu.SemaphoreType.DMA((n,))
    vm = pltpu.VMEM

    table = jnp.pad(prefix_table, ((0, PAD - prefix), (0, 0)))
    bias, hidden, bdk, bdv, ones = call(
        partial(prefix_body, prefix),
        "prefix",
        [(shaped((rows, length, length), F32), VMEM), (shaped((PAD, mid), F32), VMEM)]
        + [(shaped((heads * PAD, width), BF16), VMEM)] * 2
        + [(shaped((heads, width), BF16), VMEM)],
        [SMEM] + [VMEM] * 5,
        [],
        3.7,
    )(lengths, table, inner_weight, flat(inner_bias), outer_weight, flat(outer_bias))

    arrays = {}
    quick = fsdp == 8 and dp > 1
    triple_parts = Pieces(dp, triple_weight)
    output_parts = Pieces(dp, output_weight)
    up_parts = Pieces(dp, upward_weight)
    down_parts = Pieces(dp, packed(downward_weight, triple_weight.shape[0]))
    if quick:
        cut_rows, triple_c = triple_weight.shape
        blocks = downward_weight.shape[0] // cut_rows
        far = list(range(1, dp))
        layout = halves(far, cut_rows)
        near_rows = cut_rows + cut_rows // 2
        far_rows = cut_rows * (dp - 1) // 2
        half = cut_rows // 2
        triple_parts.add("near", [(0, 0, 0, cut_rows, 0, 0)], near_rows)
        triple_parts.add("first", [part + (0,) for part in layout], far_rows)
        output_parts.add("near", [(0, 0, 0, cut_rows, 0, triple_c)], near_rows)
        output_parts.add("first", [part + (triple_c,) for part in layout], far_rows)
        up_parts.add("near", [(1, 0, 0, cut_rows, 0, 0)], near_rows)
        up_parts.add("up", [part + (0,) for part in layout], far_rows)
        down_parts.add("near", [(side, cut_rows, side * half, half, 0, 0) for side in (0, 1)], near_rows)
        down_parts.add("down", [part + (0,) for part in layout], far_rows)

        head = jnp.concatenate([triple_weight, output_weight], axis=1)
        beside = packed(downward_weight, cut_rows)
        near = Spread(
            jnp.concatenate([head, beside[:half]], axis=0),
            jnp.concatenate([upward_weight, beside[half:]], axis=0),
            fsdp,
        )
        near.second(bdk)
        near.put(arrays, "near", range(4))
        first = Spread(*cut(from_planes(head, dp, *near.arrays[2:]), layout), fsdp)
        first.second()
        first.put(arrays, "first", (0, 1))
        up_far = from_planes(after(upward_weight, head), dp, *first.arrays[:2])
        up = Spread(*cut(up_far, layout), fsdp)
        first.put(arrays, "first", (2, 3), *up.first)
        up.second()
        up.put(arrays, "up", (0, 1))
        x = after(x, *up.arrays[:2])
    else:
        whole = (
            (triple_weight, triple_parts),
            (output_weight, output_parts),
            (upward_weight, up_parts),
            (downward_weight, down_parts),
        )
        for k, (weight, parts) in enumerate(whole):
            gathered = lax.all_gather(weight, "fsdp", axis=0, tiled=True)
            arrays["whole", k] = lax.all_gather(gathered, "dp", axis=1, tiled=True)
            parts.whole(("whole", k))

    keys = triple_parts.keys()
    triple, triple_full = call(
        partial(triple_body, triple_parts, keys),
        "triple",
        [(shaped((tokens, 3 * width), BF16), ANY), (shaped((width, 3 * width), BF16), ANY)],
        [VMEM] * 3 + [ANY] * len(keys),
        [
            vm((width, 3 * width), BF16),
            vm((tokens, width), BF16),
            vm((tokens, 3 * width), BF16),
            dma(len(triple_parts.parts)),
            dma(2 * len(triple_parts.planes()) + 4),
        ],
        0.1,
    )(x, flat(gain_first), flat(shift_first), *[arrays[key] for key in keys])
    if quick:
        down_far = from_planes(after(beside, upward_weight), dp, triple)
        down = Spread(*cut(down_far, layout), fsdp)
        triple = after(triple, *down.halves)
    keys = output_parts.keys()
    prob, pre, mix, middle, norm_two, output_full = call(
        partial(attend_body, rows, prefix, output_parts, keys),
        "attend",
        [
            (shaped((rows * heads, length, length), BF16), ANY),
            (shaped((rows, heads * PAD, length), BF16), ANY),
            (shaped((tokens, width), BF16), ANY),
            (shaped((tokens, width), F32), ANY),
            (shaped((tokens, width), BF16), ANY),
            (shaped((width, width), BF16), ANY),
        ],
        [VMEM] * 7 + [ANY] * (1 + len(keys)),
        [
            vm((tokens, 3 * width), BF16),
            vm((width, width), BF16),
            vm((tokens, width), BF16),
            vm((rows * heads, length, length), BF16),
            vm((heads * PAD, length), F32),
            vm((rows, heads * PAD, length), BF16),
            vm((length, width), F32),
            vm((tokens, width), BF16),
            vm((tokens, width), F32),
            dma(rows + len(output_parts.parts)),
            dma(3 + 3 * rows),
        ],
        10,
    )(
        bias,
        x,
        flat(output_bias),
        flat(gain_second),
        flat(shift_second),
        bdk,
        bdv,
        triple,
        *[arrays[key] for key in keys],
    )

    if quick:
        up.put(arrays, "up", (2, 3), norm_two)
        down.second(norm_two)
        down.put(arrays, "down", (0, 1))
        norm_two = after(norm_two, *down.arrays[:2])
    keys = up_parts.keys()
    state = []
    planes = up_parts.planes()
    cuts = [planes]
    for k, some in enumerate(cuts):
        state = call(
            partial(upward_body, some, up_parts, keys, len(state)),
            "upward_%d" % k,
            [
                (shaped((tokens, wide), BF16), ANY),
                (shaped((tokens, wide), BF16), ANY),
                (shaped((width, wide), BF16), ANY),
            ],
            [VMEM] * 2 + [ANY] * (len(keys) + len(state)),
            [
                vm((width, wide), BF16),
                vm((tokens, wide), BF16),
                vm((tokens, wide), BF16),
                dma(len(up_parts.parts)),
                dma(3 * wide // 512),
            ],
            16 / len(cuts),
            aliases={2 + len(keys) + n: n for n in range(len(state))},
        )(norm_two, flat(upward_bias), *[arrays[key] for key in keys], *state)
    active, slope, up_full = state

    down_shape = (chunk, width)
    if quick:
        down_shape = (2 * cut_rows, dp * blocks * width // dp)

    def chunk_scratch(count):
        return [
            vm((count, *down_shape), BF16),
            vm((count, width, chunk), BF16),
            vm((count, tokens, chunk), BF16),
            vm((count, tokens, chunk), BF16),
            vm((count, tokens, chunk), BF16),
            vm((tokens, width), F32),
        ]

    n_sems = len(down_parts.parts) + 16

    if quick:
        down.put(arrays, "down", (2, 3), active)
    keys = down_parts.keys()
    result, g_middle, g_mix, delta, d_pre, pairs = call(
        partial(middle_body, rows, (0, 1, 2, 3), down_parts, keys),
        "middle",
        [
            (shaped((tokens, width), BF16), ANY),
            (shaped((tokens, width), F32), ANY),
            (shaped((tokens, width), BF16), ANY),
            (shaped((rows, heads, length), F32), VMEM),
            (shaped((rows, heads * PAD, length), BF16), VMEM),
            (shaped((2, PAD, width), F32), VMEM),
        ],
        [ANY] * (4 + len(keys)) + [ANY] + [VMEM] * 2 + [ANY] * 6,
        chunk_scratch(4)
        + [
            vm((tokens, width), F32),
            vm((width, width), BF16),
            vm((tokens, width), BF16),
            vm((tokens, width), BF16),
            vm((tokens, width), BF16),
            vm((tokens, width), BF16),
            vm((tokens, width), BF16),
            vm((rows, heads * PAD, length), BF16),
            vm((heads * PAD, width), BF16),
            vm((heads, width), BF16),
            vm((tokens, width), BF16),
            dma(n_sems),
            dma(13),
        ],
        28,
    )(
        g,
        active,
        slope,
        up_full,
        *[arrays[key] for key in keys],
        middle,
        flat(gain_second),
        flat(downward_bias),
        output_full,
        mix,
        triple,
        pre,
        bdv,
        ones,
    )

    grads = []
    for row in range(rows):
        grads += call(
            partial(attend_back_body, row, length, heads),
            "attend_back_%d" % row,
            [(shaped((length, 3 * width), BF16), ANY)],
            [ANY] * 3 + [VMEM] + [ANY] * 2,
            [
                vm((length, 3 * width), BF16),
                vm((length, width), BF16),
                vm((heads, length, length), BF16),
                vm((length, width), F32),
                vm((length, 3 * width), BF16),
                vm((heads * PAD, length), BF16),
                vm((heads * PAD, width), BF16),
                dma(34),
            ],
            8.5,
            room=12,
        )(triple, g_mix, prob, delta, d_pre, bdk)

    (input_grad,) = call(
        partial(input_body, rows),
        "input",
        [(shaped((tokens, width), BF16), ANY)],
        [ANY] * rows + [ANY] * 2 + [VMEM] + [ANY],
        [
            vm((width, 3 * width), BF16),
            vm((tokens, 3 * width), BF16),
            vm((tokens, width), F32),
            vm((tokens, width), F32),
            vm((tokens, width), BF16),
            vm((tokens, width), BF16),
            dma(4 * (rows + 1) + 2 + rows),
        ],
        9,
        room=12,
    )(*grads, triple_full, x, flat(gain_first), g_middle)

    pairs = total_pairs(pairs, fsdp, dp)
    table_grad, inner_w_grad, inner_b_grad, outer_w_grad, outer_b_grad = call(
        partial(reparam_body, prefix),
        "reparam",
        [
            (shaped((PAD, width), F32), VMEM),
            (shaped((width, mid), F32), ANY),
            (shaped((1, mid), F32), VMEM),
            (shaped((mid, 2 * width), F32), ANY),
            (shaped((1, 2 * width), F32), VMEM),
        ],
        [VMEM] * 5,
        [vm((mid, 2 * width), F32), vm((width, mid), F32), dma(3)],
        6,
        room=10,
    )(pairs, hidden, table, inner_weight, outer_weight)
    return (
        result.reshape(rows, length, width),
        input_grad.reshape(rows, length, width),
        table_grad[:prefix],
        inner_w_grad,
        inner_b_grad.reshape(-1),
        outer_w_grad,
        outer_b_grad.reshape(-1),
    )


def solution(mesh):
    in_specs = (
        P(("dp", "fsdp"), None, None),
        P(("dp", "fsdp"), None),
        P(("dp", "fsdp"), None, None),
        P(),
        P(),
        P("fsdp", "dp"),
        P("fsdp", "dp"),
        P(),
        P(),
        P(),
        P("fsdp", "dp"),
        P(),
        P("fsdp", "dp"),
        P(),
        P(),
        P(),
        P(),
        P(),
        P(),
    )
    out_specs = (
        P(("dp", "fsdp"), None, None),
        P(("dp", "fsdp"), None, None),
        P(),
        P(),
        P(),
        P(),
        P(),
    )
    return jax.shard_map(
        partial(body, mesh.shape["fsdp"], mesh.shape["dp"]),
        mesh=mesh,
        in_specs=in_specs,
        out_specs=out_specs,
        check_vma=False,
    )
```

```python
import math
from functools import partial

import jax
import jax.numpy as jnp
from jax import lax
from jax.experimental import pallas as pl
from jax.experimental.pallas import tpu as pltpu
from jax.sharding import PartitionSpec as P

HEAD = 64
PAD = 16
MASKED = -1e30
F32 = jnp.float32
BF16 = jnp.bfloat16
GELU_C = 0.7978845608028654
GELU_A = 0.044715
PEAK = 1.15e9

ANY = pl.BlockSpec(memory_space=pl.ANY)
VMEM = pl.BlockSpec(memory_space=pltpu.VMEM)
SMEM = pl.BlockSpec(memory_space=pltpu.SMEM)


def dot(a, b):
    return lax.dot_general(a, b, (((1,), (0,)), ((), ())), preferred_element_type=F32)


def dot_nt(a, b):
    return lax.dot_general(a, b, (((1,), (1,)), ((), ())), preferred_element_type=F32)


def dot_tn(a, b):
    return lax.dot_general(a, b, (((0,), (0,)), ((), ())), preferred_element_type=F32)


def unit(values):
    center = values - jnp.mean(values, axis=-1, keepdims=True)
    scaled = lax.rsqrt(jnp.mean(center * center, axis=-1, keepdims=True) + 1e-05)
    return center * scaled, scaled


def norm_back(upstream, unit_rows, scaled):
    return scaled * (
        upstream
        - jnp.mean(upstream, axis=-1, keepdims=True)
        - unit_rows * jnp.mean(upstream * unit_rows, axis=-1, keepdims=True)
    )


def call(body, name, outs, ins, scratch, micros, room=None, aliases={}):
    held = sum(
        math.prod(s.shape) * jnp.dtype(s.dtype).itemsize
        for s in scratch
        if jnp.issubdtype(s.dtype, jnp.floating)
    )
    limit = 50 * 1024 * 1024 if room is None else held + room * 1024 * 1024
    return pl.pallas_call(
        body,
        name=name,
        out_shape=[o[0] for o in outs],
        out_specs=[o[1] for o in outs],
        in_specs=ins,
        scratch_shapes=scratch,
        input_output_aliases=aliases,
        compiler_params=pltpu.CompilerParams(vmem_limit_bytes=limit),
        cost_estimate=pl.CostEstimate(
            flops=int(micros * PEAK), bytes_accessed=0, transcendentals=0
        ),
    )


def shaped(shape, dtype):
    return jax.ShapeDtypeStruct(shape, dtype)


class Pieces:
    def __init__(self, dp, shard):
        self.dp = dp
        self.shard_rows, self.shard_cols = shard.shape
        self.parts = []
        self.split = True

    def whole(self, key):
        self.split = False
        self.parts.append((key, None, None, None, 0, None, None))
        return self

    def add(self, stage, layout, rows):
        where = {(0, 0): (0, 0), (1, 0): (0, 1), (0, 1): (1, 0), (2, 1): (1, 1)}
        where.update({(2, 0): (2, 0), (3, 0): (2, 1), (1, 1): (3, 0), (3, 1): (3, 1)})
        for core in (0, 1):
            for way in range(4):
                for side, src_row, low, count, plane, col in layout:
                    array, second = where[way, side]
                    key = (stage, array, core)
                    src = src_row + second * rows
                    self.parts.append((key, src, low, count, plane, 2 * way | core, col))
        return self

    def of(self, picks):
        out = Pieces.__new__(Pieces)
        out.__dict__.update(self.__dict__)
        out.parts = [p for p in self.parts if not self.split or p[5] >> 1 in picks]
        return out

    def keys(self):
        return sorted({part[0] for part in self.parts})

    def planes(self):
        return sorted({part[4] for part in self.parts})

    def columns(self, place, plane):
        if not self.split:
            return 0, self.shard_cols * self.dp
        across = lax.rem(place[0] + plane, self.dp)
        return pl.multiple_of(across * self.shard_cols, 128), self.shard_cols

    def copies(self, refs, dst, sems, base, place, plane=None, paired=False):
        out = []
        for key, src_row, low, count, at, flip, col in self.parts:
            if plane is not None and at != plane:
                continue
            if not self.split:
                out.append(pltpu.make_async_copy(refs[key], dst, sems.at[base + len(out)]))
                continue
            owner = jnp.bitwise_xor(place[1], flip)
            if paired:
                owner = jnp.bitwise_and(owner, 1)
            row = pl.multiple_of(owner * self.shard_rows + low, 16)
            column, cols = self.columns(place, at)
            out.append(
                pltpu.make_async_copy(
                    refs[key].at[pl.ds(src_row, count), pl.ds(col, cols)],
                    dst.at[pl.ds(row, count), pl.ds(column, cols)],
                    sems.at[base + len(out)],
                )
            )
        return out


def position():
    return lax.axis_index("dp"), lax.axis_index("fsdp")


def start(copies):
    for c in copies:
        c.start()


def wait(copies):
    for c in copies:
        c.wait()


def after(value, *others):
    return lax.optimization_barrier((value, *others))[0]


def flip(value, mask, size):
    return lax.ppermute(value, "fsdp", [(i, i ^ mask) for i in range(size)])


class Spread:
    def __init__(self, low, high, size):
        self.size = size
        self.halves = low, high
        self.first = flip(low, 2, size), flip(high, 4, size)

    def second(self, *others):
        self.arrays = [
            jnp.concatenate([half, after(came, *others)], axis=0)
            for half, came in zip(self.halves, self.first)
        ]
        self.arrays.append(flip(self.arrays[0], 4, self.size))
        self.arrays.append(flip(self.arrays[1], 2, self.size))

    def put(self, arrays, stage, which, *others):
        for k in which:
            arrays[stage, k, 0] = self.arrays[k]
            arrays[stage, k, 1] = flip(after(self.arrays[k], *others), 1, self.size)


def packed(value, rows):
    return jnp.concatenate(
        [value[k : k + rows] for k in range(0, value.shape[0], rows)], axis=1
    )


def halves(planes, shard_rows):
    total = shard_rows * len(planes)
    middle = total // 2
    out = []
    for k, plane in enumerate(planes):
        for side, (first, last) in enumerate(((0, middle), (middle, total))):
            low, high = max(first, k * shard_rows), min(last, (k + 1) * shard_rows)
            if low < high:
                out.append((side, low - first, low - k * shard_rows, high - low, plane))
    return out


def cut(shards, layout):
    return [
        jnp.concatenate(
            [shards[p][low : low + count] for s, _, low, count, p in layout if s == side], axis=0
        )
        for side in (0, 1)
    ]


def from_planes(value, dp, *others):
    planes = after(lax.all_gather(value, "dp", axis=0, tiled=False), *others)
    here = lax.axis_index("dp")
    return {
        j: lax.dynamic_index_in_dim(planes, lax.rem(here + j, dp), 0, keepdims=False)
        for j in range(1, dp)
    }


def prefix_body(
    prefix, lengths, table, inner_w, inner_b, outer_w, outer_b, bias_o, hidden_o, keys_o, values_o, ones_o
):
    rows, length, _ = bias_o.shape
    for row in range(rows):
        key = lax.broadcasted_iota(jnp.int32, (length, length), 0)
        query = lax.broadcasted_iota(jnp.int32, (length, length), 1)
        key_seg = jnp.zeros((length, length), jnp.int32)
        query_seg = jnp.zeros((length, length), jnp.int32)
        bound = 0
        for s in range(lengths.shape[1]):
            bound = bound + lengths[row, s]
            key_seg = key_seg + jnp.where(key >= bound, 1, 0)
            query_seg = query_seg + jnp.where(query >= bound, 1, 0)
        seen = (key_seg == query_seg) & (key <= query)
        bias_o[row] = jnp.where(seen, 0.0, MASKED)
    width = keys_o.shape[1]
    hidden = jnp.tanh(dot(table[...], inner_w[...]) + inner_b[...])
    hidden_o[...] = hidden
    pairs = (dot(hidden.astype(BF16), outer_w[...]) + outer_b[...]).astype(BF16).astype(F32)
    shape = keys_o.shape
    row = lax.broadcasted_iota(jnp.int32, shape, 0)
    col = lax.broadcasted_iota(jnp.int32, shape, 1)
    inside = (row // PAD) == (col // HEAD)
    real = inside & (lax.rem(row, PAD) < prefix)
    heads = shape[0] // PAD
    keys_o[...] = jnp.where(real, jnp.tile(pairs[:, :width], (heads, 1)), 0.0).astype(BF16)
    values_o[...] = jnp.where(real, jnp.tile(pairs[:, width:], (heads, 1)), 0.0).astype(BF16)
    head = lax.broadcasted_iota(jnp.int32, ones_o.shape, 0)
    lane = lax.broadcasted_iota(jnp.int32, ones_o.shape, 1)
    ones_o[...] = jnp.where(head == lane // HEAD, 1.0, 0.0).astype(BF16)


def triple_body(parts, keys, *refs):
    n_arrays = len(keys)
    place = position()
    x, gain, shift = refs[:3]
    arrays = dict(zip(keys, refs[3 : 3 + n_arrays]))
    triple_o, t_o, tv, normed, tri, sems, out_sems = refs[3 + n_arrays :]
    tokens, _ = x.shape
    inward = []
    base = 0
    for plane in parts.planes():
        inward.append((plane, parts.copies(arrays, tv, sems, base, place, plane)))
        base += len(inward[-1][1])
        start(inward[-1][1])
    outs = []

    def send(src, dst):
        outs.append(pltpu.make_async_copy(src, dst, out_sems.at[len(outs)]))
        outs[-1].start()

    step = 128
    for t in range(0, tokens, step):
        u, _ = unit(x[t : t + step, :].astype(F32))
        normed[t : t + step, :] = (u * gain[...] + shift[...]).astype(BF16)
    for plane, copies in inward:
        wait(copies)
        column, count = parts.columns(place, plane)
        block = count if count <= 1024 else 1024
        for n in range(0, count, block):
            cols = pl.ds(column + n, block)
            if not isinstance(column, int):
                cols = pl.ds(pl.multiple_of(column + n, 128), block)
            tri[:, cols] = dot(normed[...], tv[:, cols]).astype(BF16)
            send(tri.at[:, cols], triple_o.at[:, cols])
            send(tv.at[:, cols], t_o.at[:, cols])
    wait(outs)


def attend_body(rows, prefix, parts, keys, *refs):
    n_arrays = len(keys)
    place = position()
    bias, x, out_b, gain, shift, bdk, bdv, triple = refs[:8]
    arrays = dict(zip(keys, refs[8 : 8 + n_arrays]))
    prob_o, pre_o, mix_o, middle_o, norm_o, o_o = refs[8 + n_arrays : 14 + n_arrays]
    (tri, ov, normed, prob, spre, pre, main, mix, middle, sems, out_sems) = refs[14 + n_arrays :]
    tokens, width = x.shape
    length = tokens // rows
    heads = width // HEAD
    scale = HEAD ** (-0.5)
    step = 128
    inward = [
        pltpu.make_async_copy(
            triple.at[pl.ds(row * length, length), :],
            tri.at[pl.ds(row * length, length), :],
            sems.at[row],
        )
        for row in range(rows)
    ]
    start(inward)
    in_o = parts.copies(arrays, ov, sems, rows, place)
    start(in_o)
    outs = []

    def send(src, dst):
        outs.append(pltpu.make_async_copy(src, dst, out_sems.at[len(outs)]))
        outs[-1].start()

    lane = lax.broadcasted_iota(jnp.int32, (length, 2 * HEAD), 1)
    low_lane = lane < HEAD
    for row in range(rows):
        here = slice(row * length, (row + 1) * length)
        inward[row].wait()
        raw = dot_nt(bdk[...], tri[here, :width]) * scale
        pre_row = lax.broadcasted_iota(jnp.int32, raw.shape, 0)
        spre[...] = jnp.where(lax.rem(pre_row, PAD) < prefix, raw, MASKED)
        for i in range(heads // 2):
            cols = i * 2 * HEAD
            q = tri[here, cols : cols + 2 * HEAD]
            k = tri[here, width + cols : width + cols + 2 * HEAD]
            v = tri[here, 2 * width + cols : 2 * width + cols + 2 * HEAD]
            found = []
            for sub in (0, 1):
                qm = jnp.where(low_lane if sub == 0 else ~low_lane, q, jnp.zeros_like(q))
                s = dot_nt(k, qm) * scale + bias[row]
                at = (2 * i + sub) * PAD
                sp = spre[at : at + PAD, :]
                top = jnp.maximum(
                    jnp.max(s, axis=0, keepdims=True), jnp.max(sp, axis=0, keepdims=True)
                )
                e = jnp.exp(s - top)
                ep = jnp.exp(sp - top)
                inverse = 1.0 / (
                    jnp.sum(e, axis=0, keepdims=True) + jnp.sum(ep, axis=0, keepdims=True)
                )
                p = (e * inverse).astype(BF16)
                prob[row * heads + 2 * i + sub] = p
                pre[row, at : at + PAD, :] = (ep * inverse).astype(BF16)
                found.append(dot_tn(p, v))
            main[:, cols : cols + 2 * HEAD] = jnp.where(low_lane, found[0], found[1])
            if i % 2 == 1:
                some = pl.ds(row * heads + 2 * i - 2, 4)
                send(prob.at[some], prob_o.at[some])
        if row == 0:
            wait(in_o)
            send(ov, o_o)
        mix[here, :] = (main[...] + dot_tn(pre[row], bdv[...])).astype(BF16)
        middle[here, :] = x[here, :].astype(F32) + dot(mix[here, :], ov[...]) + out_b[...]
        for t in range(row * length, (row + 1) * length, step):
            u, _ = unit(middle[t : t + step, :])
            normed[t : t + step, :] = (u * gain[...] + shift[...]).astype(BF16)
        send(middle.at[pl.ds(row * length, length), :], middle_o.at[pl.ds(row * length, length), :])
        send(normed.at[pl.ds(row * length, length), :], norm_o.at[pl.ds(row * length, length), :])
    send(pre, pre_o)
    send(mix, mix_o)
    wait(outs)


def upward_body(planes, parts, keys, carried, *refs):
    n_arrays = len(keys)
    place = position()
    norm, bias = refs[:2]
    arrays = dict(zip(keys, refs[2 : 2 + n_arrays]))
    n_arrays += carried
    active_o, slope_o, up_o = refs[2 + n_arrays : 5 + n_arrays]
    uv, active, slope, sems, out_sems = refs[5 + n_arrays :]
    inward = []
    base = 0
    for plane in planes:
        inward.append((plane, parts.copies(arrays, uv, sems, base, place, plane)))
        base += len(inward[-1][1])
        start(inward[-1][1])
    outs = []

    def send(src, dst):
        outs.append(pltpu.make_async_copy(src, dst, out_sems.at[len(outs)]))
        outs[-1].start()

    for plane, copies in inward:
        wait(copies)
        column, count = parts.columns(place, plane)
        block = 512
        for n in range(0, count, block):
            cols = pl.ds(column + n, block)
            if not isinstance(column, int):
                cols = pl.ds(pl.multiple_of(column + n, 128), block)
            u = dot(norm[...], uv[:, cols]) + bias[:, cols]
            square = u * u
            half = 0.5 + 0.5 * jnp.tanh(u * (GELU_C + GELU_C * GELU_A * square))
            active[:, cols] = (u * half).astype(BF16)
            slope[:, cols] = (
                half
                + (u * (half - half * half)) * (2.0 * GELU_C + 6.0 * GELU_C * GELU_A * square)
            ).astype(BF16)
            send(active.at[:, cols], active_o.at[:, cols])
            send(slope.at[:, cols], slope_o.at[:, cols])
            send(uv.at[:, cols], up_o.at[:, cols])
    wait(outs)


class Chunk:
    def __init__(self, place, pick, parts, arrays, full, held, slot, sems, base):
        active, slope, upward = full
        self.dv, self.uc, self.ac, self.sc, self.gu = (h.at[slot] for h in held)
        size = self.uc.shape[1]
        self.split = parts.split
        if not parts.split:
            cols = rows = pl.ds(pick * size, size)
            (whole,) = arrays.values()
            self.down = [pltpu.make_async_copy(whole.at[rows, :], self.dv, sems.at[base])]
        else:
            at = jnp.bitwise_xor(lax.shift_right_logical(place[1], 1), pick)
            self.down = parts.of((pick,)).copies(
                arrays, self.dv, sems, base, place, paired=True
            )
            self.planes, self.shard_rows = parts.dp, parts.shard_rows
            cols = pl.ds(pl.multiple_of(at * size, size), size)
        base += len(self.down)
        self.sems = len(self.down) + 3
        self.rest = [
            pltpu.make_async_copy(slope.at[:, cols], self.sc, sems.at[base]),
            pltpu.make_async_copy(upward.at[:, cols], self.uc, sems.at[base + 1]),
            pltpu.make_async_copy(active.at[:, cols], self.ac, sems.at[base + 2]),
        ]

    def blocks(self):
        rows = self.shard_rows
        size = self.uc.shape[1]
        count = size // (2 * rows)
        return [(k, (k * rows, size // 2 + k * rows)) for k in range(count)]

    def upstream(self, g):
        wait(self.down)
        self.rest[0].wait()
        size = self.uc.shape[1]
        if not self.split:
            for n in range(0, size, 512):
                cols = slice(n, n + 512)
                value = dot_nt(g[...], self.dv[cols, :])
                self.gu[:, cols] = (value * self.sc[:, cols].astype(F32)).astype(BF16)
            return
        width = g.shape[1] // self.planes
        rows = self.shard_rows
        for k, places in self.blocks():
            value = 0.0
            for z in range(self.planes):
                at = z * self.dv.shape[1] // self.planes + k * width
                value = value + dot_nt(g[:, z * width : (z + 1) * width], self.dv[:, at : at + width])
            for n, low in enumerate(places):
                cols = slice(low, low + rows)
                part = value[:, n * rows : (n + 1) * rows]
                self.gu[:, cols] = (part * self.sc[:, cols].astype(F32)).astype(BF16)

    def back(self):
        self.rest[1].wait()
        return lambda cols: dot_nt(self.gu[...], self.uc[cols, :])

    def ahead(self):
        self.rest[2].wait()
        if not self.split:
            return lambda cols: dot(self.ac[...], self.dv[:, cols])
        rows = self.shard_rows

        def term(cols):
            width = self.uc.shape[0] // self.planes
            found = []
            for z in range(cols.start // width, cols.stop // width):
                value = 0.0
                for k, places in self.blocks():
                    at = z * self.dv.shape[1] // self.planes + k * width
                    left = jnp.concatenate([self.ac[:, low : low + rows] for low in places], axis=1)
                    value = value + dot(left, self.dv[:, at : at + width])
                found.append(value)
            return jnp.concatenate(found, axis=1)

        return term


def middle_body(rows, picks, parts, keys, *refs):
    n_arrays = len(keys)
    place = position()
    g, active, slope, upward = refs[:4]
    arrays = dict(zip(keys, refs[4 : 4 + n_arrays]))
    middle_i, gain2, down_b, output_w, mix, triple, pre, bdv, ones = refs[
        4 + n_arrays : 13 + n_arrays
    ]
    result_o, gmid_o, gmix_o, delta_o, dspre_o, pairs_o = refs[13 + n_arrays : 19 + n_arrays]
    mix_i, pre_i, bdv_i, ones_i, g_i = mix, pre, bdv, ones, g
    (dv, uc, ac, sc, gu, second, middle, ov, low, gmix, q, result) = refs[
        19 + n_arrays : 31 + n_arrays
    ]
    mix, pre, bdv, ones, g, sems, io_sems = refs[31 + n_arrays :]
    tokens, width = g.shape
    g_copy = pltpu.make_async_copy(g_i, g, io_sems.at[12])
    g_copy.start()
    length = tokens // rows
    heads = width // HEAD
    scale = HEAD ** (-0.5)
    chunks = []
    base = 0
    for k, pick in enumerate(picks):
        chunks.append(
            Chunk(
                place, pick, parts, arrays, (active, slope, upward), (dv, uc, ac, sc, gu), k, sems, base
            )
        )
        base += chunks[-1].sems
    for chunk in chunks:
        start(chunk.down)
        start(chunk.rest[:1])
    for k in (1, 2):
        for chunk in chunks:
            start(chunk.rest[k : k + 1])
    carried = [
        pltpu.make_async_copy(middle_i, middle, io_sems.at[2]),
        pltpu.make_async_copy(output_w, ov, io_sems.at[3]),
        pltpu.make_async_copy(triple.at[:, pl.ds(0, width)], q, io_sems.at[4]),
        pltpu.make_async_copy(mix_i, mix, io_sems.at[8]),
        pltpu.make_async_copy(pre_i, pre, io_sems.at[9]),
        pltpu.make_async_copy(bdv_i, bdv, io_sems.at[10]),
        pltpu.make_async_copy(ones_i, ones, io_sems.at[11]),
    ]
    start(carried)
    g_copy.wait()
    for chunk in chunks:
        chunk.upstream(g)
    back = [chunk.back() for chunk in chunks]
    ahead = [chunk.ahead() for chunk in chunks]
    wait(carried)
    for n in range(0, width, 512):
        cols = slice(n, n + 512)
        value = back[0](cols)
        for term in back[1:]:
            value = value + term(cols)
        second[:, cols] = value
    step = 128
    for t in range(0, tokens, step):
        here = slice(t, t + step)
        u, scaled = unit(middle[here, :])
        gm = g[here, :].astype(F32) + norm_back(second[here, :] * gain2[...], u, scaled)
        second[here, :] = gm
        low[here, :] = gm.astype(BF16)
    done = [pltpu.make_async_copy(second, gmid_o, io_sems.at[5])]
    done[-1].start()
    for row in range(rows):
        here = slice(row * length, (row + 1) * length)
        gmix[here, :] = dot_nt(low[here, :], ov[...]).astype(BF16)
    done.append(pltpu.make_async_copy(gmix, gmix_o, io_sems.at[6]))
    done[-1].start()
    for n in range(0, width, 512):
        cols = slice(n, n + 512)
        value = middle[:, cols] + down_b[:, cols]
        for term in ahead:
            value = value + term(cols)
        result[:, cols] = value.astype(BF16)
    done.append(pltpu.make_async_copy(result, result_o, io_sems.at[7]))
    done[-1].start()
    keys = 0.0
    values = 0.0
    for row in range(rows):
        here = slice(row * length, (row + 1) * length)
        up = gmix[here, :]
        product = up.astype(F32) * mix[here, :].astype(F32)
        high = product.astype(BF16)
        small = (product - high.astype(F32)).astype(BF16)
        delta = dot_nt(ones[...], high) + dot_nt(ones[...], small)
        delta_o[row] = delta
        each = jnp.broadcast_to(delta[:, None, :], (heads, PAD, length)).reshape(-1, length)
        p = pre[row]
        ds = (p.astype(F32) * (dot_nt(bdv[...], up) - each)).astype(BF16)
        dspre_o[row] = ds
        keys = keys + dot(ds, q[here, :])
        values = values + dot(p, up)
    row = lax.broadcasted_iota(jnp.int32, keys.shape, 0)
    col = lax.broadcasted_iota(jnp.int32, keys.shape, 1)
    inside = (row // PAD) == (col // HEAD)
    keys = jnp.where(inside, keys * scale, 0.0).reshape(heads, PAD, width)
    values = jnp.where(inside, values, 0.0).reshape(heads, PAD, width)
    prefix = pairs_o.shape[0] // 4
    for k, value in enumerate((jnp.sum(keys, axis=0), jnp.sum(values, axis=0))):
        for n in (0, 1):
            part = value[:prefix, n * width // 2 : (n + 1) * width // 2]
            pairs_o[(2 * k + n) * prefix : (2 * k + n + 1) * prefix, :] = part
    wait(done)


def attend_back_body(row, length, heads, triple, gmix, prob, delta, dspre_i, bdk_i, *refs):
    out_o, tri, up, p, before, out, dspre, bdk, sems = refs
    width = heads * HEAD
    scale = HEAD ** (-0.5)
    here = pl.ds(row * length, length)
    groups = 4
    span = heads // groups
    inward = []
    for n in range(groups):
        cols = pl.ds(n * span * HEAD, span * HEAD)
        copies = [
            pltpu.make_async_copy(
                triple.at[here, pl.ds(m * width + n * span * HEAD, span * HEAD)],
                tri.at[:, pl.ds(m * width + n * span * HEAD, span * HEAD)],
                sems.at[5 * n + m],
            )
            for m in range(3)
        ]
        copies.append(pltpu.make_async_copy(gmix.at[here, cols], up.at[:, cols], sems.at[5 * n + 3]))
        copies.append(
            pltpu.make_async_copy(
                prob.at[pl.ds(row * heads + n * span, span)],
                p.at[pl.ds(n * span, span)],
                sems.at[5 * n + 4],
            )
        )
        start(copies)
        inward.append(copies)
        if n == 0:
            side = [
                pltpu.make_async_copy(dspre_i.at[row], dspre, sems.at[32]),
                pltpu.make_async_copy(bdk_i, bdk, sems.at[33]),
            ]
            start(side)
    low_lane = lax.broadcasted_iota(jnp.int32, (length, 2 * HEAD), 1) < HEAD
    wait(side)
    before[...] = dot_tn(dspre[...], bdk[...])
    done = []

    def columns(m, h):
        low = m * width + h // 2 * 2 * HEAD
        return slice(low, low + 2 * HEAD)

    def own(value, h):
        return jnp.where(low_lane if h % 2 == 0 else ~low_lane, value, jnp.zeros_like(value))

    lead = 2
    upstream, scores, half = {}, {}, {}
    for turn in range(heads + 2 * lead):
        h = turn
        if h < heads:
            if h % span == 0:
                wait(inward[h // span])
            upstream[h] = dot_nt(tri[:, columns(2, h)], own(up[:, columns(0, h)], h))
        h = turn - lead
        if 0 <= h < heads:
            d = delta[row, h : h + 1, :]
            scores[h] = (p[h].astype(F32) * (upstream.pop(h) - d)).astype(BF16)
        h = turn - 2 * lead
        if 0 <= h < heads:
            ds = scores.pop(h)
            found = (
                dot_tn(ds, own(tri[:, columns(1, h)], h)),
                dot(ds, own(tri[:, columns(0, h)], h)),
                dot(p[h], own(up[:, columns(0, h)], h)),
            )
            if h % 2 == 0:
                half[h] = found
                continue
            queries, keys, values = (a + b for a, b in zip(half.pop(h - 1), found))
            out[:, columns(0, h)] = ((queries + before[:, columns(0, h)]) * scale).astype(BF16)
            out[:, columns(1, h)] = (keys * scale).astype(BF16)
            out[:, columns(2, h)] = values.astype(BF16)
            if (h + 1) % span == 0:
                for m in range(3):
                    at = pl.ds(m * width + (h + 1 - span) * HEAD, span * HEAD)
                    done.append(
                        pltpu.make_async_copy(
                            out.at[:, at], out_o.at[:, at], sems.at[5 * groups + len(done)]
                        )
                    )
                    done[-1].start()
    wait(done)


def input_body(rows, *refs):
    grads = refs[:rows]
    triple_w, x_i, gain1, gmid_i, result_o, tv, gv, first, gmid, x, result, sems = refs[rows:]
    tokens, width = x.shape
    length = tokens // rows
    inward = []
    cuts = [(0, width // 2), (width // 2, width), (width, 2 * width), (2 * width, 3 * width)]
    for n, (low, high) in enumerate(cuts):
        cols = pl.ds(low, high - low)
        copies = [
            pltpu.make_async_copy(triple_w.at[:, cols], tv.at[:, cols], sems.at[n * (rows + 1)])
        ]
        for row in range(rows):
            copies.append(
                pltpu.make_async_copy(
                    grads[row].at[:, cols],
                    gv.at[pl.ds(row * length, length), cols],
                    sems.at[n * (rows + 1) + 1 + row],
                )
            )
        start(copies)
        inward.append(copies)
    late = [
        pltpu.make_async_copy(x_i, x, sems.at[4 * (rows + 1)]),
        pltpu.make_async_copy(gmid_i, gmid, sems.at[4 * (rows + 1) + 1]),
    ]
    start(late)
    for n in range(3):
        wait(inward[n])
        cols = slice(*cuts[n])
        for m in range(0, width, 512):
            value = dot_nt(gv[:, cols], tv[m : m + 512, cols])
            first[:, m : m + 512] = value if n == 0 else first[:, m : m + 512] + value
    wait(inward[3])
    wait(late)
    step = 128
    done = []
    last = slice(2 * width, 3 * width)
    for row in range(rows):
        here = slice(row * length, (row + 1) * length)
        first[here, :] = first[here, :] + dot_nt(gv[here, last], tv[:, last])
        for t in range(row * length, (row + 1) * length, step):
            now = slice(t, t + step)
            u, scaled = unit(x[now, :].astype(F32))
            back = norm_back(first[now, :] * gain1[...], u, scaled)
            result[now, :] = (gmid[now, :] + back).astype(BF16)
        at = pl.ds(row * length, length)
        done.append(pltpu.make_async_copy(result.at[at, :], result_o.at[at, :], sems.at[4 * (rows + 1) + 2 + row]))
        done[-1].start()
    wait(done)


def split3(value):
    high = value.astype(BF16)
    rest = value - high.astype(F32)
    mid = rest.astype(BF16)
    return high, mid, (rest - mid.astype(F32)).astype(BF16)


def reparam_body(prefix, pairs, hidden_r, table, inner_w, outer_w, *refs):
    table_o, inner_wo, inner_bo, outer_wo, outer_bo, outer_g, inner_g, sems = refs
    width = 2 * pairs.shape[1]
    hidden = hidden_r[...]
    low = jnp.concatenate([hidden.astype(BF16)] * 3, axis=0)
    row = lax.broadcasted_iota(jnp.int32, (PAD, hidden.shape[1]), 0)
    grads = []
    done = []
    for k in (0, 1):
        value = jnp.concatenate(
            [pairs[(2 * k + n) * prefix : (2 * k + n + 1) * prefix, :] for n in (0, 1)], axis=1
        )
        value = jnp.concatenate([value, jnp.zeros((PAD - prefix, width), F32)], axis=0)
        parts = jnp.concatenate(split3(value), axis=0)
        cols = slice(k * width, (k + 1) * width)
        outer_g[:, cols] = dot_tn(low, parts)
        at = pl.ds(k * width, width)
        done.append(pltpu.make_async_copy(outer_g.at[:, at], outer_wo.at[:, at], sems.at[k]))
        done[-1].start()
        outer_bo[:, cols] = jnp.sum(value, axis=0, keepdims=True)
        grads.append(dot_nt(parts, outer_w[:, cols]))
    total = grads[0] + grads[1]
    hidden_grad = total[:PAD] + total[PAD : 2 * PAD] + total[2 * PAD :]
    before = jnp.where(row < prefix, hidden_grad * (1.0 - hidden * hidden), 0.0)
    inner_bo[...] = jnp.sum(before, axis=0, keepdims=True)
    stacked = jnp.concatenate(split3(before), axis=0)
    inner_g[...] = dot_tn(jnp.concatenate([table[...]] * 3, axis=0), stacked)
    done.append(pltpu.make_async_copy(inner_g, inner_wo, sems.at[2]))
    done[-1].start()
    back = dot_nt(stacked, inner_w[...])
    table_o[...] = back[:PAD] + back[PAD : 2 * PAD] + back[2 * PAD :]
    wait(done)


def total_pairs(pairs, fsdp, dp):
    if fsdp == 8 and dp == 4:
        rounds = [("fsdp", (1,)), ("fsdp", (2, 4, 6)), ("dp", (1, 2, 3))]
    else:
        rounds = [("fsdp", (1 << k,)) for k in range(fsdp.bit_length() - 1)]
        rounds += [("dp", (1 << k,)) for k in range(dp.bit_length() - 1)]
    sizes = {"fsdp": fsdp, "dp": dp}
    for axis, masks in rounds:
        size = sizes[axis]
        terms = {0: pairs}
        for mask in masks:
            terms[mask] = lax.ppermute(pairs, axis, [(i, i ^ mask) for i in range(size)])
        if len(masks) == 1:
            pairs = terms[0] + terms[masks[0]]
        else:
            low = min(masks)
            pairs = (terms[0] + terms[low]) + (terms[2 * low] + terms[3 * low])
    return pairs


def body(
    fsdp,
    dp,
    activations,
    lengths,
    cotangent,
    gain_first,
    shift_first,
    triple_weight,
    output_weight,
    output_bias,
    gain_second,
    shift_second,
    upward_weight,
    upward_bias,
    downward_weight,
    downward_bias,
    prefix_table,
    inner_weight,
    inner_bias,
    outer_weight,
    outer_bias,
):
    rows, length, width = activations.shape
    tokens = rows * length
    heads = width // HEAD
    wide = upward_bias.shape[0]
    prefix, _ = prefix_table.shape
    mid = inner_bias.shape[0]
    chunk = wide // 4
    x = activations.reshape(tokens, width)
    g = cotangent.reshape(tokens, width)
    flat = lambda v: v.reshape(1, -1)
    dma = lambda n: pltpu.SemaphoreType.DMA((n,))
    vm = pltpu.VMEM

    table = jnp.pad(prefix_table, ((0, PAD - prefix), (0, 0)))
    bias, hidden, bdk, bdv, ones = call(
        partial(prefix_body, prefix),
        "prefix",
        [(shaped((rows, length, length), F32), VMEM), (shaped((PAD, mid), F32), VMEM)]
        + [(shaped((heads * PAD, width), BF16), VMEM)] * 2
        + [(shaped((heads, width), BF16), VMEM)],
        [SMEM] + [VMEM] * 5,
        [],
        3.7,
    )(lengths, table, inner_weight, flat(inner_bias), outer_weight, flat(outer_bias))

    arrays = {}
    quick = fsdp == 8 and dp > 1
    triple_parts = Pieces(dp, triple_weight)
    output_parts = Pieces(dp, output_weight)
    up_parts = Pieces(dp, upward_weight)
    down_parts = Pieces(dp, packed(downward_weight, triple_weight.shape[0]))
    if quick:
        cut_rows, triple_c = triple_weight.shape
        blocks = downward_weight.shape[0] // cut_rows
        far = list(range(1, dp))
        layout = halves(far, cut_rows)
        near_rows = cut_rows + cut_rows // 2
        far_rows = cut_rows * (dp - 1) // 2
        half = cut_rows // 2
        triple_parts.add("near", [(0, 0, 0, cut_rows, 0, 0)], near_rows)
        triple_parts.add("first", [part + (0,) for part in layout], far_rows)
        output_parts.add("near", [(0, 0, 0, cut_rows, 0, triple_c)], near_rows)
        output_parts.add("first", [part + (triple_c,) for part in layout], far_rows)
        up_parts.add("near", [(1, 0, 0, cut_rows, 0, 0)], near_rows)
        up_parts.add("up", [part + (0,) for part in layout], far_rows)
        down_parts.add("near", [(side, cut_rows, side * half, half, 0, 0) for side in (0, 1)], near_rows)
        down_parts.add("down", [part + (0,) for part in layout], far_rows)

        head = jnp.concatenate([triple_weight, output_weight], axis=1)
        beside = packed(downward_weight, cut_rows)
        near = Spread(
            jnp.concatenate([head, beside[:half]], axis=0),
            jnp.concatenate([upward_weight, beside[half:]], axis=0),
            fsdp,
        )
        near.second(bdk)
        near.put(arrays, "near", range(4))
        first = Spread(*cut(from_planes(head, dp, *near.arrays[2:]), layout), fsdp)
        first.second()
        first.put(arrays, "first", (0, 1))
        up_far = from_planes(after(upward_weight, head), dp, *first.arrays[:2])
        up = Spread(*cut(up_far, layout), fsdp)
        first.put(arrays, "first", (2, 3), *up.first)
        up.second()
        up.put(arrays, "up", (0, 1))
        x = after(x, *up.arrays[:2])
    else:
        whole = (
            (triple_weight, triple_parts),
            (output_weight, output_parts),
            (upward_weight, up_parts),
            (downward_weight, down_parts),
        )
        for k, (weight, parts) in enumerate(whole):
            gathered = lax.all_gather(weight, "fsdp", axis=0, tiled=True)
            arrays["whole", k] = lax.all_gather(gathered, "dp", axis=1, tiled=True)
            parts.whole(("whole", k))

    keys = triple_parts.keys()
    triple, triple_full = call(
        partial(triple_body, triple_parts, keys),
        "triple",
        [(shaped((tokens, 3 * width), BF16), ANY), (shaped((width, 3 * width), BF16), ANY)],
        [VMEM] * 3 + [ANY] * len(keys),
        [
            vm((width, 3 * width), BF16),
            vm((tokens, width), BF16),
            vm((tokens, 3 * width), BF16),
            dma(len(triple_parts.parts)),
            dma(2 * len(triple_parts.planes()) + 4),
        ],
        0.1,
    )(x, flat(gain_first), flat(shift_first), *[arrays[key] for key in keys])
    if quick:
        down_far = from_planes(after(beside, upward_weight), dp, triple)
        down = Spread(*cut(down_far, layout), fsdp)
        triple = after(triple, *down.halves)
    keys = output_parts.keys()
    prob, pre, mix, middle, norm_two, output_full = call(
        partial(attend_body, rows, prefix, output_parts, keys),
        "attend",
        [
            (shaped((rows * heads, length, length), BF16), ANY),
            (shaped((rows, heads * PAD, length), BF16), ANY),
            (shaped((tokens, width), BF16), ANY),
            (shaped((tokens, width), F32), ANY),
            (shaped((tokens, width), BF16), ANY),
            (shaped((width, width), BF16), ANY),
        ],
        [VMEM] * 7 + [ANY] * (1 + len(keys)),
        [
            vm((tokens, 3 * width), BF16),
            vm((width, width), BF16),
            vm((tokens, width), BF16),
            vm((rows * heads, length, length), BF16),
            vm((heads * PAD, length), F32),
            vm((rows, heads * PAD, length), BF16),
            vm((length, width), F32),
            vm((tokens, width), BF16),
            vm((tokens, width), F32),
            dma(rows + len(output_parts.parts)),
            dma(3 + rows * (2 + heads // 4)),
        ],
        10,
    )(
        bias,
        x,
        flat(output_bias),
        flat(gain_second),
        flat(shift_second),
        bdk,
        bdv,
        triple,
        *[arrays[key] for key in keys],
    )

    if quick:
        up.put(arrays, "up", (2, 3), norm_two)
        down.second(norm_two)
        down.put(arrays, "down", (0, 1))
        norm_two = after(norm_two, *down.arrays[:2])
    keys = up_parts.keys()
    state = []
    planes = up_parts.planes()
    cuts = [planes]
    for k, some in enumerate(cuts):
        state = call(
            partial(upward_body, some, up_parts, keys, len(state)),
            "upward_%d" % k,
            [
                (shaped((tokens, wide), BF16), ANY),
                (shaped((tokens, wide), BF16), ANY),
                (shaped((width, wide), BF16), ANY),
            ],
            [VMEM] * 2 + [ANY] * (len(keys) + len(state)),
            [
                vm((width, wide), BF16),
                vm((tokens, wide), BF16),
                vm((tokens, wide), BF16),
                dma(len(up_parts.parts)),
                dma(3 * wide // 512),
            ],
            16 / len(cuts),
            aliases={2 + len(keys) + n: n for n in range(len(state))},
        )(norm_two, flat(upward_bias), *[arrays[key] for key in keys], *state)
    active, slope, up_full = state

    down_shape = (chunk, width)
    if quick:
        down_shape = (2 * cut_rows, dp * blocks * width // dp)

    def chunk_scratch(count):
        return [
            vm((count, *down_shape), BF16),
            vm((count, width, chunk), BF16),
            vm((count, tokens, chunk), BF16),
            vm((count, tokens, chunk), BF16),
            vm((count, tokens, chunk), BF16),
            vm((tokens, width), F32),
        ]

    n_sems = len(down_parts.parts) + 16

    if quick:
        down.put(arrays, "down", (2, 3), active)
    keys = down_parts.keys()
    result, g_middle, g_mix, delta, d_pre, pairs = call(
        partial(middle_body, rows, (0, 1, 2, 3), down_parts, keys),
        "middle",
        [
            (shaped((tokens, width), BF16), ANY),
            (shaped((tokens, width), F32), ANY),
            (shaped((tokens, width), BF16), ANY),
            (shaped((rows, heads, length), F32), VMEM),
            (shaped((rows, heads * PAD, length), BF16), VMEM),
            (shaped((4 * prefix, width // 2), F32), VMEM),
        ],
        [ANY] * (4 + len(keys)) + [ANY] + [VMEM] * 2 + [ANY] * 6,
        chunk_scratch(4)
        + [
            vm((tokens, width), F32),
            vm((width, width), BF16),
            vm((tokens, width), BF16),
            vm((tokens, width), BF16),
            vm((tokens, width), BF16),
            vm((tokens, width), BF16),
            vm((tokens, width), BF16),
            vm((rows, heads * PAD, length), BF16),
            vm((heads * PAD, width), BF16),
            vm((heads, width), BF16),
            vm((tokens, width), BF16),
            dma(n_sems),
            dma(13),
        ],
        28,
    )(
        g,
        active,
        slope,
        up_full,
        *[arrays[key] for key in keys],
        middle,
        flat(gain_second),
        flat(downward_bias),
        output_full,
        mix,
        triple,
        pre,
        bdv,
        ones,
    )

    grads = []
    for row in range(rows):
        grads += call(
            partial(attend_back_body, row, length, heads),
            "attend_back_%d" % row,
            [(shaped((length, 3 * width), BF16), ANY)],
            [ANY] * 3 + [VMEM] + [ANY] * 2,
            [
                vm((length, 3 * width), BF16),
                vm((length, width), BF16),
                vm((heads, length, length), BF16),
                vm((length, width), F32),
                vm((length, 3 * width), BF16),
                vm((heads * PAD, length), BF16),
                vm((heads * PAD, width), BF16),
                dma(34),
            ],
            8.5,
            room=12,
        )(triple, g_mix, prob, delta, d_pre, bdk)

    (input_grad,) = call(
        partial(input_body, rows),
        "input",
        [(shaped((tokens, width), BF16), ANY)],
        [ANY] * rows + [ANY] * 2 + [VMEM] + [ANY],
        [
            vm((width, 3 * width), BF16),
            vm((tokens, 3 * width), BF16),
            vm((tokens, width), F32),
            vm((tokens, width), F32),
            vm((tokens, width), BF16),
            vm((tokens, width), BF16),
            dma(4 * (rows + 1) + 2 + rows),
        ],
        9,
        room=12,
    )(*grads, triple_full, x, flat(gain_first), g_middle)

    pairs = total_pairs(pairs, fsdp, dp)
    table_grad, inner_w_grad, inner_b_grad, outer_w_grad, outer_b_grad = call(
        partial(reparam_body, prefix),
        "reparam",
        [
            (shaped((PAD, width), F32), VMEM),
            (shaped((width, mid), F32), ANY),
            (shaped((1, mid), F32), VMEM),
            (shaped((mid, 2 * width), F32), ANY),
            (shaped((1, 2 * width), F32), VMEM),
        ],
        [VMEM] * 5,
        [vm((mid, 2 * width), F32), vm((width, mid), F32), dma(3)],
        6,
        room=10,
    )(pairs, hidden, table, inner_weight, outer_weight)
    return (
        result.reshape(rows, length, width),
        input_grad.reshape(rows, length, width),
        table_grad[:prefix],
        inner_w_grad,
        inner_b_grad.reshape(-1),
        outer_w_grad,
        outer_b_grad.reshape(-1),
    )


def solution(mesh):
    in_specs = (
        P(("dp", "fsdp"), None, None),
        P(("dp", "fsdp"), None),
        P(("dp", "fsdp"), None, None),
        P(),
        P(),
        P("fsdp", "dp"),
        P("fsdp", "dp"),
        P(),
        P(),
        P(),
        P("fsdp", "dp"),
        P(),
        P("fsdp", "dp"),
        P(),
        P(),
        P(),
        P(),
        P(),
        P(),
    )
    out_specs = (
        P(("dp", "fsdp"), None, None),
        P(("dp", "fsdp"), None, None),
        P(),
        P(),
        P(),
        P(),
        P(),
    )
    return jax.shard_map(
        partial(body, mesh.shape["fsdp"], mesh.shape["dp"]),
        mesh=mesh,
        in_specs=in_specs,
        out_specs=out_specs,
        check_vma=False,
    )
```

```python
import math
from functools import partial

import jax
import jax.numpy as jnp
from jax import lax
from jax.experimental import pallas as pl
from jax.experimental.pallas import tpu as pltpu
from jax.sharding import PartitionSpec as P

HEAD = 64
PAD = 16
MASKED = -1e30
F32 = jnp.float32
BF16 = jnp.bfloat16
GELU_C = 0.7978845608028654
GELU_A = 0.044715
PEAK = 1.15e9

ANY = pl.BlockSpec(memory_space=pl.ANY)
VMEM = pl.BlockSpec(memory_space=pltpu.VMEM)
SMEM = pl.BlockSpec(memory_space=pltpu.SMEM)


def dot(a, b):
    return lax.dot_general(a, b, (((1,), (0,)), ((), ())), preferred_element_type=F32)


def dot_nt(a, b):
    return lax.dot_general(a, b, (((1,), (1,)), ((), ())), preferred_element_type=F32)


def dot_tn(a, b):
    return lax.dot_general(a, b, (((0,), (0,)), ((), ())), preferred_element_type=F32)


def unit(values):
    center = values - jnp.mean(values, axis=-1, keepdims=True)
    scaled = lax.rsqrt(jnp.mean(center * center, axis=-1, keepdims=True) + 1e-05)
    return center * scaled, scaled


def norm_back(upstream, unit_rows, scaled):
    return scaled * (
        upstream
        - jnp.mean(upstream, axis=-1, keepdims=True)
        - unit_rows * jnp.mean(upstream * unit_rows, axis=-1, keepdims=True)
    )


def call(body, name, outs, ins, scratch, micros, room=None, aliases={}):
    held = sum(
        math.prod(s.shape) * jnp.dtype(s.dtype).itemsize
        for s in scratch
        if jnp.issubdtype(s.dtype, jnp.floating)
    )
    limit = 50 * 1024 * 1024 if room is None else held + room * 1024 * 1024
    return pl.pallas_call(
        body,
        name=name,
        out_shape=[o[0] for o in outs],
        out_specs=[o[1] for o in outs],
        in_specs=ins,
        scratch_shapes=scratch,
        input_output_aliases=aliases,
        compiler_params=pltpu.CompilerParams(vmem_limit_bytes=limit),
        cost_estimate=pl.CostEstimate(
            flops=int(micros * PEAK), bytes_accessed=0, transcendentals=0
        ),
    )


def shaped(shape, dtype):
    return jax.ShapeDtypeStruct(shape, dtype)


class Pieces:
    def __init__(self, dp, shard):
        self.dp = dp
        self.shard_rows, self.shard_cols = shard.shape
        self.parts = []
        self.split = True

    def whole(self, key):
        self.split = False
        self.parts.append((key, None, None, None, 0, None, None))
        return self

    def add(self, stage, layout, rows):
        where = {(0, 0): (0, 0), (1, 0): (0, 1), (0, 1): (1, 0), (2, 1): (1, 1)}
        where.update({(2, 0): (2, 0), (3, 0): (2, 1), (1, 1): (3, 0), (3, 1): (3, 1)})
        for core in (0, 1):
            for way in range(4):
                for side, src_row, low, count, plane, col in layout:
                    array, second = where[way, side]
                    key = (stage, array, core)
                    src = src_row + second * rows
                    self.parts.append((key, src, low, count, plane, 2 * way | core, col))
        return self

    def of(self, picks):
        out = Pieces.__new__(Pieces)
        out.__dict__.update(self.__dict__)
        out.parts = [p for p in self.parts if not self.split or p[5] >> 1 in picks]
        return out

    def keys(self):
        return sorted({part[0] for part in self.parts})

    def planes(self):
        return sorted({part[4] for part in self.parts})

    def columns(self, place, plane):
        if not self.split:
            return 0, self.shard_cols * self.dp
        across = lax.rem(place[0] + plane, self.dp)
        return pl.multiple_of(across * self.shard_cols, 128), self.shard_cols

    def copies(self, refs, dst, sems, base, place, plane=None, paired=False):
        out = []
        for key, src_row, low, count, at, flip, col in self.parts:
            if plane is not None and at != plane:
                continue
            if not self.split:
                out.append(pltpu.make_async_copy(refs[key], dst, sems.at[base + len(out)]))
                continue
            owner = jnp.bitwise_xor(place[1], flip)
            if paired:
                owner = jnp.bitwise_and(owner, 1)
            row = pl.multiple_of(owner * self.shard_rows + low, 16)
            column, cols = self.columns(place, at)
            out.append(
                pltpu.make_async_copy(
                    refs[key].at[pl.ds(src_row, count), pl.ds(col, cols)],
                    dst.at[pl.ds(row, count), pl.ds(column, cols)],
                    sems.at[base + len(out)],
                )
            )
        return out


def position():
    return lax.axis_index("dp"), lax.axis_index("fsdp")


def start(copies):
    for c in copies:
        c.start()


def wait(copies):
    for c in copies:
        c.wait()


def after(value, *others):
    return lax.optimization_barrier((value, *others))[0]


def flip(value, mask, size):
    return lax.ppermute(value, "fsdp", [(i, i ^ mask) for i in range(size)])


class Spread:
    def __init__(self, low, high, size):
        self.size = size
        self.halves = low, high
        self.first = flip(low, 2, size), flip(high, 4, size)

    def second(self, *others):
        self.arrays = [
            jnp.concatenate([half, after(came, *others)], axis=0)
            for half, came in zip(self.halves, self.first)
        ]
        self.arrays.append(flip(self.arrays[0], 4, self.size))
        self.arrays.append(flip(self.arrays[1], 2, self.size))

    def put(self, arrays, stage, which, *others):
        for k in which:
            arrays[stage, k, 0] = self.arrays[k]
            arrays[stage, k, 1] = flip(after(self.arrays[k], *others), 1, self.size)


def packed(value, rows):
    return jnp.concatenate(
        [value[k : k + rows] for k in range(0, value.shape[0], rows)], axis=1
    )


def halves(planes, shard_rows):
    total = shard_rows * len(planes)
    middle = total // 2
    out = []
    for k, plane in enumerate(planes):
        for side, (first, last) in enumerate(((0, middle), (middle, total))):
            low, high = max(first, k * shard_rows), min(last, (k + 1) * shard_rows)
            if low < high:
                out.append((side, low - first, low - k * shard_rows, high - low, plane))
    return out


def cut(shards, layout):
    return [
        jnp.concatenate(
            [shards[p][low : low + count] for s, _, low, count, p in layout if s == side], axis=0
        )
        for side in (0, 1)
    ]


def from_planes(value, dp, *others):
    planes = after(lax.all_gather(value, "dp", axis=0, tiled=False), *others)
    here = lax.axis_index("dp")
    return {
        j: lax.dynamic_index_in_dim(planes, lax.rem(here + j, dp), 0, keepdims=False)
        for j in range(1, dp)
    }


def prefix_body(
    prefix, lengths, table, inner_w, inner_b, outer_w, outer_b, bias_o, hidden_o, keys_o, values_o, ones_o
):
    rows, length, _ = bias_o.shape
    for row in range(rows):
        key = lax.broadcasted_iota(jnp.int32, (length, length), 0)
        query = lax.broadcasted_iota(jnp.int32, (length, length), 1)
        key_seg = jnp.zeros((length, length), jnp.int32)
        query_seg = jnp.zeros((length, length), jnp.int32)
        bound = 0
        for s in range(lengths.shape[1]):
            bound = bound + lengths[row, s]
            key_seg = key_seg + jnp.where(key >= bound, 1, 0)
            query_seg = query_seg + jnp.where(query >= bound, 1, 0)
        seen = (key_seg == query_seg) & (key <= query)
        bias_o[row] = jnp.where(seen, 0.0, MASKED)
    width = keys_o.shape[1]
    hidden = jnp.tanh(dot(table[...], inner_w[...]) + inner_b[...])
    hidden_o[...] = hidden
    pairs = (dot(hidden.astype(BF16), outer_w[...]) + outer_b[...]).astype(BF16).astype(F32)
    shape = keys_o.shape
    row = lax.broadcasted_iota(jnp.int32, shape, 0)
    col = lax.broadcasted_iota(jnp.int32, shape, 1)
    inside = (row // PAD) == (col // HEAD)
    real = inside & (lax.rem(row, PAD) < prefix)
    heads = shape[0] // PAD
    keys_o[...] = jnp.where(real, jnp.tile(pairs[:, :width], (heads, 1)), 0.0).astype(BF16)
    values_o[...] = jnp.where(real, jnp.tile(pairs[:, width:], (heads, 1)), 0.0).astype(BF16)
    head = lax.broadcasted_iota(jnp.int32, ones_o.shape, 0)
    lane = lax.broadcasted_iota(jnp.int32, ones_o.shape, 1)
    ones_o[...] = jnp.where(head == lane // HEAD, 1.0, 0.0).astype(BF16)


def triple_body(parts, keys, *refs):
    n_arrays = len(keys)
    place = position()
    x, gain, shift = refs[:3]
    arrays = dict(zip(keys, refs[3 : 3 + n_arrays]))
    triple_o, t_o, tv, normed, tri, sems, out_sems = refs[3 + n_arrays :]
    tokens, _ = x.shape
    inward = []
    base = 0
    for plane in parts.planes():
        inward.append((plane, parts.copies(arrays, tv, sems, base, place, plane)))
        base += len(inward[-1][1])
        start(inward[-1][1])
    outs = []

    def send(src, dst):
        outs.append(pltpu.make_async_copy(src, dst, out_sems.at[len(outs)]))
        outs[-1].start()

    step = 128
    for t in range(0, tokens, step):
        u, _ = unit(x[t : t + step, :].astype(F32))
        normed[t : t + step, :] = (u * gain[...] + shift[...]).astype(BF16)
    for plane, copies in inward:
        wait(copies)
        column, count = parts.columns(place, plane)
        block = count if count <= 1024 else 1024
        for n in range(0, count, block):
            cols = pl.ds(column + n, block)
            if not isinstance(column, int):
                cols = pl.ds(pl.multiple_of(column + n, 128), block)
            tri[:, cols] = dot(normed[...], tv[:, cols]).astype(BF16)
            send(tri.at[:, cols], triple_o.at[:, cols])
            send(tv.at[:, cols], t_o.at[:, cols])
    wait(outs)


def attend_body(rows, prefix, parts, keys, *refs):
    n_arrays = len(keys)
    place = position()
    bias, x, out_b, gain, shift, bdk, bdv, triple = refs[:8]
    arrays = dict(zip(keys, refs[8 : 8 + n_arrays]))
    prob_o, pre_o, mix_o, middle_o, norm_o, o_o = refs[8 + n_arrays : 14 + n_arrays]
    (tri, ov, normed, prob, spre, pre, main, mix, middle, sems, out_sems) = refs[14 + n_arrays :]
    tokens, width = x.shape
    length = tokens // rows
    heads = width // HEAD
    scale = HEAD ** (-0.5)
    step = 128
    inward = [
        pltpu.make_async_copy(
            triple.at[pl.ds(row * length, length), :],
            tri.at[pl.ds(row * length, length), :],
            sems.at[row],
        )
        for row in range(rows)
    ]
    start(inward)
    in_o = parts.copies(arrays, ov, sems, rows, place)
    start(in_o)
    outs = []

    def send(src, dst):
        outs.append(pltpu.make_async_copy(src, dst, out_sems.at[len(outs)]))
        outs[-1].start()

    lane = lax.broadcasted_iota(jnp.int32, (length, 2 * HEAD), 1)
    low_lane = lane < HEAD
    for row in range(rows):
        here = slice(row * length, (row + 1) * length)
        inward[row].wait()
        raw = dot_nt(bdk[...], tri[here, :width]) * scale
        pre_row = lax.broadcasted_iota(jnp.int32, raw.shape, 0)
        spre[...] = jnp.where(lax.rem(pre_row, PAD) < prefix, raw, MASKED)
        for i in range(heads // 2):
            cols = i * 2 * HEAD
            q = tri[here, cols : cols + 2 * HEAD]
            k = tri[here, width + cols : width + cols + 2 * HEAD]
            v = tri[here, 2 * width + cols : 2 * width + cols + 2 * HEAD]
            found = []
            for sub in (0, 1):
                qm = jnp.where(low_lane if sub == 0 else ~low_lane, q, jnp.zeros_like(q))
                s = dot_nt(k, qm) * scale + bias[row]
                at = (2 * i + sub) * PAD
                sp = spre[at : at + PAD, :]
                top = jnp.maximum(
                    jnp.max(s, axis=0, keepdims=True), jnp.max(sp, axis=0, keepdims=True)
                )
                e = jnp.exp(s - top)
                ep = jnp.exp(sp - top)
                inverse = 1.0 / (
                    jnp.sum(e, axis=0, keepdims=True) + jnp.sum(ep, axis=0, keepdims=True)
                )
                p = (e * inverse).astype(BF16)
                prob[row * heads + 2 * i + sub] = p
                pre[row, at : at + PAD, :] = (ep * inverse).astype(BF16)
                found.append(dot_tn(p, v))
            main[:, cols : cols + 2 * HEAD] = jnp.where(low_lane, found[0], found[1])
            if i % 2 == 1:
                some = pl.ds(row * heads + 2 * i - 2, 4)
                send(prob.at[some], prob_o.at[some])
        if row == 0:
            wait(in_o)
            send(ov, o_o)
        mix[here, :] = (main[...] + dot_tn(pre[row], bdv[...])).astype(BF16)
        middle[here, :] = x[here, :].astype(F32) + dot(mix[here, :], ov[...]) + out_b[...]
        for t in range(row * length, (row + 1) * length, step):
            u, _ = unit(middle[t : t + step, :])
            normed[t : t + step, :] = (u * gain[...] + shift[...]).astype(BF16)
        send(middle.at[pl.ds(row * length, length), :], middle_o.at[pl.ds(row * length, length), :])
        send(normed.at[pl.ds(row * length, length), :], norm_o.at[pl.ds(row * length, length), :])
    send(pre, pre_o)
    send(mix, mix_o)
    wait(outs)


def upward_body(planes, parts, keys, carried, *refs):
    n_arrays = len(keys)
    place = position()
    norm, bias = refs[:2]
    arrays = dict(zip(keys, refs[2 : 2 + n_arrays]))
    n_arrays += carried
    active_o, slope_o, up_o = refs[2 + n_arrays : 5 + n_arrays]
    uv, active, slope, sems, out_sems = refs[5 + n_arrays :]
    inward = []
    base = 0
    for plane in planes:
        inward.append((plane, parts.copies(arrays, uv, sems, base, place, plane)))
        base += len(inward[-1][1])
        start(inward[-1][1])
    outs = []

    def send(src, dst):
        outs.append(pltpu.make_async_copy(src, dst, out_sems.at[len(outs)]))
        outs[-1].start()

    for plane, copies in inward:
        wait(copies)
        column, count = parts.columns(place, plane)
        block = 512
        for n in range(0, count, block):
            cols = pl.ds(column + n, block)
            if not isinstance(column, int):
                cols = pl.ds(pl.multiple_of(column + n, 128), block)
            u = dot(norm[...], uv[:, cols]) + bias[:, cols]
            square = u * u
            half = 0.5 + 0.5 * jnp.tanh(u * (GELU_C + GELU_C * GELU_A * square))
            active[:, cols] = (u * half).astype(BF16)
            slope[:, cols] = (
                half
                + (u * (half - half * half)) * (2.0 * GELU_C + 6.0 * GELU_C * GELU_A * square)
            ).astype(BF16)
            send(active.at[:, cols], active_o.at[:, cols])
            send(slope.at[:, cols], slope_o.at[:, cols])
            send(uv.at[:, cols], up_o.at[:, cols])
    wait(outs)


class Chunk:
    def __init__(self, place, pick, parts, arrays, full, held, slot, sems, base):
        active, slope, upward = full
        self.dv, self.uc, self.ac, self.sc, self.gu = (h.at[slot] for h in held)
        size = self.uc.shape[1]
        self.split = parts.split
        if not parts.split:
            cols = rows = pl.ds(pick * size, size)
            (whole,) = arrays.values()
            self.down = [pltpu.make_async_copy(whole.at[rows, :], self.dv, sems.at[base])]
        else:
            at = jnp.bitwise_xor(lax.shift_right_logical(place[1], 1), pick)
            self.down = parts.of((pick,)).copies(
                arrays, self.dv, sems, base, place, paired=True
            )
            self.planes, self.shard_rows = parts.dp, parts.shard_rows
            cols = pl.ds(pl.multiple_of(at * size, size), size)
        base += len(self.down)
        self.sems = len(self.down) + 3
        self.rest = [
            pltpu.make_async_copy(slope.at[:, cols], self.sc, sems.at[base]),
            pltpu.make_async_copy(upward.at[:, cols], self.uc, sems.at[base + 1]),
            pltpu.make_async_copy(active.at[:, cols], self.ac, sems.at[base + 2]),
        ]

    def blocks(self):
        rows = self.shard_rows
        size = self.uc.shape[1]
        count = size // (2 * rows)
        return [(k, (k * rows, size // 2 + k * rows)) for k in range(count)]

    def upstream(self, g):
        wait(self.down)
        self.rest[0].wait()
        size = self.uc.shape[1]
        if not self.split:
            for n in range(0, size, 512):
                cols = slice(n, n + 512)
                value = dot_nt(g[...], self.dv[cols, :])
                self.gu[:, cols] = (value * self.sc[:, cols].astype(F32)).astype(BF16)
            return
        width = g.shape[1] // self.planes
        rows = self.shard_rows
        for k, places in self.blocks():
            value = 0.0
            for z in range(self.planes):
                at = z * self.dv.shape[1] // self.planes + k * width
                value = value + dot_nt(g[:, z * width : (z + 1) * width], self.dv[:, at : at + width])
            for n, low in enumerate(places):
                cols = slice(low, low + rows)
                part = value[:, n * rows : (n + 1) * rows]
                self.gu[:, cols] = (part * self.sc[:, cols].astype(F32)).astype(BF16)

    def back(self):
        self.rest[1].wait()
        return lambda cols: dot_nt(self.gu[...], self.uc[cols, :])

    def ahead(self):
        self.rest[2].wait()
        if not self.split:
            return lambda cols: dot(self.ac[...], self.dv[:, cols])
        rows = self.shard_rows

        def term(cols):
            width = self.uc.shape[0] // self.planes
            found = []
            for z in range(cols.start // width, cols.stop // width):
                value = 0.0
                for k, places in self.blocks():
                    at = z * self.dv.shape[1] // self.planes + k * width
                    left = jnp.concatenate([self.ac[:, low : low + rows] for low in places], axis=1)
                    value = value + dot(left, self.dv[:, at : at + width])
                found.append(value)
            return jnp.concatenate(found, axis=1)

        return term


def middle_body(rows, picks, parts, keys, *refs):
    n_arrays = len(keys)
    place = position()
    g, active, slope, upward = refs[:4]
    arrays = dict(zip(keys, refs[4 : 4 + n_arrays]))
    middle_i, gain2, down_b, output_w, mix, triple, pre, bdv, ones = refs[
        4 + n_arrays : 13 + n_arrays
    ]
    result_o, gmid_o, gmix_o, delta_o, dspre_o, pairs_o = refs[13 + n_arrays : 19 + n_arrays]
    mix_i, pre_i, bdv_i, ones_i, g_i = mix, pre, bdv, ones, g
    (dv, uc, ac, sc, gu, second, middle, ov, low, gmix, q, result) = refs[
        19 + n_arrays : 31 + n_arrays
    ]
    mix, pre, bdv, ones, g, sems, io_sems = refs[31 + n_arrays :]
    tokens, width = g.shape
    g_copy = pltpu.make_async_copy(g_i, g, io_sems.at[12])
    g_copy.start()
    length = tokens // rows
    heads = width // HEAD
    scale = HEAD ** (-0.5)
    chunks = []
    base = 0
    for k, pick in enumerate(picks):
        chunks.append(
            Chunk(
                place, pick, parts, arrays, (active, slope, upward), (dv, uc, ac, sc, gu), k, sems, base
            )
        )
        base += chunks[-1].sems
    for chunk in chunks:
        start(chunk.down)
        start(chunk.rest[:1])
    for k in (1, 2):
        for chunk in chunks:
            start(chunk.rest[k : k + 1])
    carried = [
        pltpu.make_async_copy(middle_i, middle, io_sems.at[2]),
        pltpu.make_async_copy(output_w, ov, io_sems.at[3]),
        pltpu.make_async_copy(triple.at[:, pl.ds(0, width)], q, io_sems.at[4]),
        pltpu.make_async_copy(mix_i, mix, io_sems.at[8]),
        pltpu.make_async_copy(pre_i, pre, io_sems.at[9]),
        pltpu.make_async_copy(bdv_i, bdv, io_sems.at[10]),
        pltpu.make_async_copy(ones_i, ones, io_sems.at[11]),
    ]
    start(carried)
    g_copy.wait()
    for chunk in chunks:
        chunk.upstream(g)
    back = [chunk.back() for chunk in chunks]
    ahead = [chunk.ahead() for chunk in chunks]
    wait(carried)
    for n in range(0, width, 512):
        cols = slice(n, n + 512)
        value = back[0](cols)
        for term in back[1:]:
            value = value + term(cols)
        second[:, cols] = value
    done = []

    def send(src, dst):
        done.append(pltpu.make_async_copy(src, dst, io_sems.at[5 + len(done)]))
        done[-1].start()

    step = length // 2
    block = width // (2 * rows)
    for n, t in enumerate(range(0, tokens, step)):
        cols = slice(n * block, (n + 1) * block)
        value = middle[:, cols] + down_b[:, cols]
        for term in ahead:
            value = value + term(cols)
        result[:, cols] = value.astype(BF16)
        here = slice(t, t + step)
        u, scaled = unit(middle[here, :])
        gm = g[here, :].astype(F32) + norm_back(second[here, :] * gain2[...], u, scaled)
        second[here, :] = gm
        low[here, :] = gm.astype(BF16)
        if n % 2 == 1:
            here = slice(n // 2 * length, (n // 2 + 1) * length)
            gmix[here, :] = dot_nt(low[here, :], ov[...]).astype(BF16)
    send(result, result_o)
    send(second, gmid_o)
    send(gmix, gmix_o)
    keys = 0.0
    values = 0.0
    for row in range(rows):
        here = slice(row * length, (row + 1) * length)
        up = gmix[here, :]
        product = up.astype(F32) * mix[here, :].astype(F32)
        high = product.astype(BF16)
        small = (product - high.astype(F32)).astype(BF16)
        delta = dot_nt(ones[...], high) + dot_nt(ones[...], small)
        delta_o[row] = delta
        each = jnp.broadcast_to(delta[:, None, :], (heads, PAD, length)).reshape(-1, length)
        p = pre[row]
        ds = (p.astype(F32) * (dot_nt(bdv[...], up) - each)).astype(BF16)
        dspre_o[row] = ds
        keys = keys + dot(ds, q[here, :])
        values = values + dot(p, up)
    row = lax.broadcasted_iota(jnp.int32, keys.shape, 0)
    col = lax.broadcasted_iota(jnp.int32, keys.shape, 1)
    inside = (row // PAD) == (col // HEAD)
    keys = jnp.where(inside, keys * scale, 0.0).reshape(heads, PAD, width)
    values = jnp.where(inside, values, 0.0).reshape(heads, PAD, width)
    prefix = pairs_o.shape[0] // 4
    for k, value in enumerate((jnp.sum(keys, axis=0), jnp.sum(values, axis=0))):
        for n in (0, 1):
            part = value[:prefix, n * width // 2 : (n + 1) * width // 2]
            pairs_o[(2 * k + n) * prefix : (2 * k + n + 1) * prefix, :] = part
    wait(done)


def attend_back_body(row, length, heads, triple, gmix, prob, delta, dspre_i, bdk_i, *refs):
    out_o, tri, up, p, before, out, dspre, bdk, sems = refs
    width = heads * HEAD
    scale = HEAD ** (-0.5)
    here = pl.ds(row * length, length)
    groups = 4
    span = heads // groups
    inward = []
    for n in range(groups):
        cols = pl.ds(n * span * HEAD, span * HEAD)
        copies = [
            pltpu.make_async_copy(
                triple.at[here, pl.ds(m * width + n * span * HEAD, span * HEAD)],
                tri.at[:, pl.ds(m * width + n * span * HEAD, span * HEAD)],
                sems.at[5 * n + m],
            )
            for m in range(3)
        ]
        copies.append(pltpu.make_async_copy(gmix.at[here, cols], up.at[:, cols], sems.at[5 * n + 3]))
        copies.append(
            pltpu.make_async_copy(
                prob.at[pl.ds(row * heads + n * span, span)],
                p.at[pl.ds(n * span, span)],
                sems.at[5 * n + 4],
            )
        )
        start(copies)
        inward.append(copies)
        if n == 0:
            side = [
                pltpu.make_async_copy(dspre_i.at[row], dspre, sems.at[32]),
                pltpu.make_async_copy(bdk_i, bdk, sems.at[33]),
            ]
            start(side)
    low_lane = lax.broadcasted_iota(jnp.int32, (length, 2 * HEAD), 1) < HEAD
    wait(side)
    before[...] = dot_tn(dspre[...], bdk[...])
    done = []

    def columns(m, h):
        low = m * width + h // 2 * 2 * HEAD
        return slice(low, low + 2 * HEAD)

    def own(value, h):
        return jnp.where(low_lane if h % 2 == 0 else ~low_lane, value, jnp.zeros_like(value))

    lead = 2
    upstream, scores, half = {}, {}, {}
    for turn in range(heads + 2 * lead):
        h = turn
        if h < heads:
            if h % span == 0:
                wait(inward[h // span])
            upstream[h] = dot_nt(tri[:, columns(2, h)], own(up[:, columns(0, h)], h))
        h = turn - lead
        if 0 <= h < heads:
            d = delta[row, h : h + 1, :]
            scores[h] = (p[h].astype(F32) * (upstream.pop(h) - d)).astype(BF16)
        h = turn - 2 * lead
        if 0 <= h < heads:
            ds = scores.pop(h)
            found = (
                dot_tn(ds, own(tri[:, columns(1, h)], h)),
                dot(ds, own(tri[:, columns(0, h)], h)),
                dot(p[h], own(up[:, columns(0, h)], h)),
            )
            if h % 2 == 0:
                half[h] = found
                continue
            queries, keys, values = (a + b for a, b in zip(half.pop(h - 1), found))
            out[:, columns(0, h)] = ((queries + before[:, columns(0, h)]) * scale).astype(BF16)
            out[:, columns(1, h)] = (keys * scale).astype(BF16)
            out[:, columns(2, h)] = values.astype(BF16)
            if (h + 1) % span == 0:
                for m in range(3):
                    at = pl.ds(m * width + (h + 1 - span) * HEAD, span * HEAD)
                    done.append(
                        pltpu.make_async_copy(
                            out.at[:, at], out_o.at[:, at], sems.at[5 * groups + len(done)]
                        )
                    )
                    done[-1].start()
    wait(done)


def input_body(rows, *refs):
    grads = refs[:rows]
    triple_w, x_i, gain1, gmid_i, result_o, tv, gv, first, gmid, x, result, sems = refs[rows:]
    tokens, width = x.shape
    length = tokens // rows
    inward = []
    cuts = [(0, width // 2), (width // 2, width), (width, 2 * width), (2 * width, 3 * width)]
    for n, (low, high) in enumerate(cuts):
        cols = pl.ds(low, high - low)
        copies = [
            pltpu.make_async_copy(triple_w.at[:, cols], tv.at[:, cols], sems.at[n * (rows + 1)])
        ]
        for row in range(rows):
            copies.append(
                pltpu.make_async_copy(
                    grads[row].at[:, cols],
                    gv.at[pl.ds(row * length, length), cols],
                    sems.at[n * (rows + 1) + 1 + row],
                )
            )
        start(copies)
        inward.append(copies)
    late = [
        pltpu.make_async_copy(x_i, x, sems.at[4 * (rows + 1)]),
        pltpu.make_async_copy(gmid_i, gmid, sems.at[4 * (rows + 1) + 1]),
    ]
    start(late)
    for n in range(3):
        wait(inward[n])
        cols = slice(*cuts[n])
        for m in range(0, width, 512):
            value = dot_nt(gv[:, cols], tv[m : m + 512, cols])
            first[:, m : m + 512] = value if n == 0 else first[:, m : m + 512] + value
    wait(inward[3])
    wait(late)
    step = 128
    done = []
    last = slice(2 * width, 3 * width)
    for row in range(rows):
        here = slice(row * length, (row + 1) * length)
        first[here, :] = first[here, :] + dot_nt(gv[here, last], tv[:, last])
        for t in range(row * length, (row + 1) * length, step):
            now = slice(t, t + step)
            u, scaled = unit(x[now, :].astype(F32))
            back = norm_back(first[now, :] * gain1[...], u, scaled)
            result[now, :] = (gmid[now, :] + back).astype(BF16)
        at = pl.ds(row * length, length)
        done.append(pltpu.make_async_copy(result.at[at, :], result_o.at[at, :], sems.at[4 * (rows + 1) + 2 + row]))
        done[-1].start()
    wait(done)


def split3(value):
    high = value.astype(BF16)
    rest = value - high.astype(F32)
    mid = rest.astype(BF16)
    return high, mid, (rest - mid.astype(F32)).astype(BF16)


def reparam_body(prefix, pairs, hidden_r, table, inner_w, outer_w, *refs):
    table_o, inner_wo, inner_bo, outer_wo, outer_bo, outer_g, inner_g, sems = refs
    width = 2 * pairs.shape[1]
    hidden = hidden_r[...]
    low = jnp.concatenate([hidden.astype(BF16)] * 3, axis=0)
    row = lax.broadcasted_iota(jnp.int32, (PAD, hidden.shape[1]), 0)
    grads = []
    done = []
    for k in (0, 1):
        value = jnp.concatenate(
            [pairs[(2 * k + n) * prefix : (2 * k + n + 1) * prefix, :] for n in (0, 1)], axis=1
        )
        value = jnp.concatenate([value, jnp.zeros((PAD - prefix, width), F32)], axis=0)
        parts = jnp.concatenate(split3(value), axis=0)
        cols = slice(k * width, (k + 1) * width)
        outer_g[:, cols] = dot_tn(low, parts)
        at = pl.ds(k * width, width)
        done.append(pltpu.make_async_copy(outer_g.at[:, at], outer_wo.at[:, at], sems.at[k]))
        done[-1].start()
        outer_bo[:, cols] = jnp.sum(value, axis=0, keepdims=True)
        grads.append(dot_nt(parts, outer_w[:, cols]))
    total = grads[0] + grads[1]
    hidden_grad = total[:PAD] + total[PAD : 2 * PAD] + total[2 * PAD :]
    before = jnp.where(row < prefix, hidden_grad * (1.0 - hidden * hidden), 0.0)
    inner_bo[...] = jnp.sum(before, axis=0, keepdims=True)
    stacked = jnp.concatenate(split3(before), axis=0)
    inner_g[...] = dot_tn(jnp.concatenate([table[...]] * 3, axis=0), stacked)
    done.append(pltpu.make_async_copy(inner_g, inner_wo, sems.at[2]))
    done[-1].start()
    back = dot_nt(stacked, inner_w[...])
    table_o[...] = back[:PAD] + back[PAD : 2 * PAD] + back[2 * PAD :]
    wait(done)


def total_pairs(pairs, fsdp, dp):
    if fsdp == 8 and dp == 4:
        rounds = [("fsdp", (1,)), ("fsdp", (2, 4, 6)), ("dp", (1, 2, 3))]
    else:
        rounds = [("fsdp", (1 << k,)) for k in range(fsdp.bit_length() - 1)]
        rounds += [("dp", (1 << k,)) for k in range(dp.bit_length() - 1)]
    sizes = {"fsdp": fsdp, "dp": dp}
    for axis, masks in rounds:
        size = sizes[axis]
        terms = {0: pairs}
        for mask in masks:
            terms[mask] = lax.ppermute(pairs, axis, [(i, i ^ mask) for i in range(size)])
        if len(masks) == 1:
            pairs = terms[0] + terms[masks[0]]
        else:
            low = min(masks)
            pairs = (terms[0] + terms[low]) + (terms[2 * low] + terms[3 * low])
    return pairs


def body(
    fsdp,
    dp,
    activations,
    lengths,
    cotangent,
    gain_first,
    shift_first,
    triple_weight,
    output_weight,
    output_bias,
    gain_second,
    shift_second,
    upward_weight,
    upward_bias,
    downward_weight,
    downward_bias,
    prefix_table,
    inner_weight,
    inner_bias,
    outer_weight,
    outer_bias,
):
    rows, length, width = activations.shape
    tokens = rows * length
    heads = width // HEAD
    wide = upward_bias.shape[0]
    prefix, _ = prefix_table.shape
    mid = inner_bias.shape[0]
    chunk = wide // 4
    x = activations.reshape(tokens, width)
    g = cotangent.reshape(tokens, width)
    flat = lambda v: v.reshape(1, -1)
    dma = lambda n: pltpu.SemaphoreType.DMA((n,))
    vm = pltpu.VMEM

    table = jnp.pad(prefix_table, ((0, PAD - prefix), (0, 0)))
    bias, hidden, bdk, bdv, ones = call(
        partial(prefix_body, prefix),
        "prefix",
        [(shaped((rows, length, length), F32), VMEM), (shaped((PAD, mid), F32), VMEM)]
        + [(shaped((heads * PAD, width), BF16), VMEM)] * 2
        + [(shaped((heads, width), BF16), VMEM)],
        [SMEM] + [VMEM] * 5,
        [],
        3.7,
    )(lengths, table, inner_weight, flat(inner_bias), outer_weight, flat(outer_bias))

    arrays = {}
    quick = fsdp == 8 and dp > 1
    triple_parts = Pieces(dp, triple_weight)
    output_parts = Pieces(dp, output_weight)
    up_parts = Pieces(dp, upward_weight)
    down_parts = Pieces(dp, packed(downward_weight, triple_weight.shape[0]))
    if quick:
        cut_rows, triple_c = triple_weight.shape
        blocks = downward_weight.shape[0] // cut_rows
        far = list(range(1, dp))
        layout = halves(far, cut_rows)
        near_rows = cut_rows + cut_rows // 2
        far_rows = cut_rows * (dp - 1) // 2
        half = cut_rows // 2
        triple_parts.add("near", [(0, 0, 0, cut_rows, 0, 0)], near_rows)
        triple_parts.add("first", [part + (0,) for part in layout], far_rows)
        output_parts.add("near", [(0, 0, 0, cut_rows, 0, triple_c)], near_rows)
        output_parts.add("first", [part + (triple_c,) for part in layout], far_rows)
        up_parts.add("near", [(1, 0, 0, cut_rows, 0, 0)], near_rows)
        up_parts.add("up", [part + (0,) for part in layout], far_rows)
        down_parts.add("near", [(side, cut_rows, side * half, half, 0, 0) for side in (0, 1)], near_rows)
        down_parts.add("down", [part + (0,) for part in layout], far_rows)

        head = jnp.concatenate([triple_weight, output_weight], axis=1)
        beside = packed(downward_weight, cut_rows)
        near = Spread(
            jnp.concatenate([head, beside[:half]], axis=0),
            jnp.concatenate([upward_weight, beside[half:]], axis=0),
            fsdp,
        )
        near.second(bdk)
        near.put(arrays, "near", range(4))
        first_cut = tuple(cut(from_planes(head, dp), layout))
        first = Spread(*after(first_cut, *near.arrays[2:]), fsdp)
        first.second()
        first.put(arrays, "first", (0, 1))
        up_far = from_planes(after(upward_weight, head), dp, *first.arrays[:2])
        up = Spread(*cut(up_far, layout), fsdp)
        first.put(arrays, "first", (2, 3), *up.first)
        up.second()
        up.put(arrays, "up", (0, 1))
        x = after(x, *up.arrays[:2])
    else:
        whole = (
            (triple_weight, triple_parts),
            (output_weight, output_parts),
            (upward_weight, up_parts),
            (downward_weight, down_parts),
        )
        for k, (weight, parts) in enumerate(whole):
            gathered = lax.all_gather(weight, "fsdp", axis=0, tiled=True)
            arrays["whole", k] = lax.all_gather(gathered, "dp", axis=1, tiled=True)
            parts.whole(("whole", k))

    keys = triple_parts.keys()
    triple, triple_full = call(
        partial(triple_body, triple_parts, keys),
        "triple",
        [(shaped((tokens, 3 * width), BF16), ANY), (shaped((width, 3 * width), BF16), ANY)],
        [VMEM] * 3 + [ANY] * len(keys),
        [
            vm((width, 3 * width), BF16),
            vm((tokens, width), BF16),
            vm((tokens, 3 * width), BF16),
            dma(len(triple_parts.parts)),
            dma(2 * len(triple_parts.planes()) + 4),
        ],
        0.1,
    )(x, flat(gain_first), flat(shift_first), *[arrays[key] for key in keys])
    if quick:
        down_far = from_planes(after(beside, upward_weight), dp, triple)
        down = Spread(*cut(down_far, layout), fsdp)
        triple = after(triple, *down.halves)
    keys = output_parts.keys()
    prob, pre, mix, middle, norm_two, output_full = call(
        partial(attend_body, rows, prefix, output_parts, keys),
        "attend",
        [
            (shaped((rows * heads, length, length), BF16), ANY),
            (shaped((rows, heads * PAD, length), BF16), ANY),
            (shaped((tokens, width), BF16), ANY),
            (shaped((tokens, width), F32), ANY),
            (shaped((tokens, width), BF16), ANY),
            (shaped((width, width), BF16), ANY),
        ],
        [VMEM] * 7 + [ANY] * (1 + len(keys)),
        [
            vm((tokens, 3 * width), BF16),
            vm((width, width), BF16),
            vm((tokens, width), BF16),
            vm((rows * heads, length, length), BF16),
            vm((heads * PAD, length), F32),
            vm((rows, heads * PAD, length), BF16),
            vm((length, width), F32),
            vm((tokens, width), BF16),
            vm((tokens, width), F32),
            dma(rows + len(output_parts.parts)),
            dma(3 + rows * (2 + heads // 4)),
        ],
        10,
    )(
        bias,
        x,
        flat(output_bias),
        flat(gain_second),
        flat(shift_second),
        bdk,
        bdv,
        triple,
        *[arrays[key] for key in keys],
    )

    if quick:
        up.put(arrays, "up", (2, 3), norm_two)
        down.second(norm_two)
        down.put(arrays, "down", (0, 1))
        norm_two = after(norm_two, *down.arrays[:2])
    keys = up_parts.keys()
    state = []
    planes = up_parts.planes()
    cuts = [planes]
    for k, some in enumerate(cuts):
        state = call(
            partial(upward_body, some, up_parts, keys, len(state)),
            "upward_%d" % k,
            [
                (shaped((tokens, wide), BF16), ANY),
                (shaped((tokens, wide), BF16), ANY),
                (shaped((width, wide), BF16), ANY),
            ],
            [VMEM] * 2 + [ANY] * (len(keys) + len(state)),
            [
                vm((width, wide), BF16),
                vm((tokens, wide), BF16),
                vm((tokens, wide), BF16),
                dma(len(up_parts.parts)),
                dma(3 * wide // 512),
            ],
            16 / len(cuts),
            aliases={2 + len(keys) + n: n for n in range(len(state))},
        )(norm_two, flat(upward_bias), *[arrays[key] for key in keys], *state)
    active, slope, up_full = state

    down_shape = (chunk, width)
    if quick:
        down_shape = (2 * cut_rows, dp * blocks * width // dp)

    def chunk_scratch(count):
        return [
            vm((count, *down_shape), BF16),
            vm((count, width, chunk), BF16),
            vm((count, tokens, chunk), BF16),
            vm((count, tokens, chunk), BF16),
            vm((count, tokens, chunk), BF16),
            vm((tokens, width), F32),
        ]

    n_sems = len(down_parts.parts) + 16

    if quick:
        down.put(arrays, "down", (2, 3), active)
    keys = down_parts.keys()
    result, g_middle, g_mix, delta, d_pre, pairs = call(
        partial(middle_body, rows, (0, 1, 2, 3), down_parts, keys),
        "middle",
        [
            (shaped((tokens, width), BF16), ANY),
            (shaped((tokens, width), F32), ANY),
            (shaped((tokens, width), BF16), ANY),
            (shaped((rows, heads, length), F32), VMEM),
            (shaped((rows, heads * PAD, length), BF16), VMEM),
            (shaped((4 * prefix, width // 2), F32), VMEM),
        ],
        [ANY] * (4 + len(keys)) + [ANY] + [VMEM] * 2 + [ANY] * 6,
        chunk_scratch(4)
        + [
            vm((tokens, width), F32),
            vm((width, width), BF16),
            vm((tokens, width), BF16),
            vm((tokens, width), BF16),
            vm((tokens, width), BF16),
            vm((tokens, width), BF16),
            vm((tokens, width), BF16),
            vm((rows, heads * PAD, length), BF16),
            vm((heads * PAD, width), BF16),
            vm((heads, width), BF16),
            vm((tokens, width), BF16),
            dma(n_sems),
            dma(13),
        ],
        28,
    )(
        g,
        active,
        slope,
        up_full,
        *[arrays[key] for key in keys],
        middle,
        flat(gain_second),
        flat(downward_bias),
        output_full,
        mix,
        triple,
        pre,
        bdv,
        ones,
    )

    grads = []
    for row in range(rows):
        grads += call(
            partial(attend_back_body, row, length, heads),
            "attend_back_%d" % row,
            [(shaped((length, 3 * width), BF16), ANY)],
            [ANY] * 3 + [VMEM] + [ANY] * 2,
            [
                vm((length, 3 * width), BF16),
                vm((length, width), BF16),
                vm((heads, length, length), BF16),
                vm((length, width), F32),
                vm((length, 3 * width), BF16),
                vm((heads * PAD, length), BF16),
                vm((heads * PAD, width), BF16),
                dma(34),
            ],
            8.5,
            room=12,
        )(triple, g_mix, prob, delta, d_pre, bdk)

    (input_grad,) = call(
        partial(input_body, rows),
        "input",
        [(shaped((tokens, width), BF16), ANY)],
        [ANY] * rows + [ANY] * 2 + [VMEM] + [ANY],
        [
            vm((width, 3 * width), BF16),
            vm((tokens, 3 * width), BF16),
            vm((tokens, width), F32),
            vm((tokens, width), F32),
            vm((tokens, width), BF16),
            vm((tokens, width), BF16),
            dma(4 * (rows + 1) + 2 + rows),
        ],
        9,
        room=12,
    )(*grads, triple_full, x, flat(gain_first), g_middle)

    pairs = total_pairs(pairs, fsdp, dp)
    table_grad, inner_w_grad, inner_b_grad, outer_w_grad, outer_b_grad = call(
        partial(reparam_body, prefix),
        "reparam",
        [
            (shaped((PAD, width), F32), VMEM),
            (shaped((width, mid), F32), ANY),
            (shaped((1, mid), F32), VMEM),
            (shaped((mid, 2 * width), F32), ANY),
            (shaped((1, 2 * width), F32), VMEM),
        ],
        [VMEM] * 5,
        [vm((mid, 2 * width), F32), vm((width, mid), F32), dma(3)],
        6,
        room=10,
    )(pairs, hidden, table, inner_weight, outer_weight)
    return (
        result.reshape(rows, length, width),
        input_grad.reshape(rows, length, width),
        table_grad[:prefix],
        inner_w_grad,
        inner_b_grad.reshape(-1),
        outer_w_grad,
        outer_b_grad.reshape(-1),
    )


def solution(mesh):
    in_specs = (
        P(("dp", "fsdp"), None, None),
        P(("dp", "fsdp"), None),
        P(("dp", "fsdp"), None, None),
        P(),
        P(),
        P("fsdp", "dp"),
        P("fsdp", "dp"),
        P(),
        P(),
        P(),
        P("fsdp", "dp"),
        P(),
        P("fsdp", "dp"),
        P(),
        P(),
        P(),
        P(),
        P(),
        P(),
    )
    out_specs = (
        P(("dp", "fsdp"), None, None),
        P(("dp", "fsdp"), None, None),
        P(),
        P(),
        P(),
        P(),
        P(),
    )
    return jax.shard_map(
        partial(body, mesh.shape["fsdp"], mesh.shape["dp"]),
        mesh=mesh,
        in_specs=in_specs,
        out_specs=out_specs,
        check_vma=False,
    )
```

```python
import math
from functools import partial

import jax
import jax.numpy as jnp
from jax import lax
from jax.experimental import pallas as pl
from jax.experimental.pallas import tpu as pltpu
from jax.sharding import PartitionSpec as P

HEAD = 64
PAD = 16
MASKED = -1e30
F32 = jnp.float32
BF16 = jnp.bfloat16
GELU_C = 0.7978845608028654
GELU_A = 0.044715
PEAK = 1.15e9

ANY = pl.BlockSpec(memory_space=pl.ANY)
VMEM = pl.BlockSpec(memory_space=pltpu.VMEM)
SMEM = pl.BlockSpec(memory_space=pltpu.SMEM)


def dot(a, b):
    return lax.dot_general(a, b, (((1,), (0,)), ((), ())), preferred_element_type=F32)


def dot_nt(a, b):
    return lax.dot_general(a, b, (((1,), (1,)), ((), ())), preferred_element_type=F32)


def dot_tn(a, b):
    return lax.dot_general(a, b, (((0,), (0,)), ((), ())), preferred_element_type=F32)


def unit(values):
    center = values - jnp.mean(values, axis=-1, keepdims=True)
    scaled = lax.rsqrt(jnp.mean(center * center, axis=-1, keepdims=True) + 1e-05)
    return center * scaled, scaled


def norm_back(upstream, unit_rows, scaled):
    return scaled * (
        upstream
        - jnp.mean(upstream, axis=-1, keepdims=True)
        - unit_rows * jnp.mean(upstream * unit_rows, axis=-1, keepdims=True)
    )


def call(body, name, outs, ins, scratch, micros, room=None, aliases={}):
    held = sum(
        math.prod(s.shape) * jnp.dtype(s.dtype).itemsize
        for s in scratch
        if jnp.issubdtype(s.dtype, jnp.floating)
    )
    limit = 50 * 1024 * 1024 if room is None else held + room * 1024 * 1024
    return pl.pallas_call(
        body,
        name=name,
        out_shape=[o[0] for o in outs],
        out_specs=[o[1] for o in outs],
        in_specs=ins,
        scratch_shapes=scratch,
        input_output_aliases=aliases,
        compiler_params=pltpu.CompilerParams(vmem_limit_bytes=limit),
        cost_estimate=pl.CostEstimate(
            flops=int(micros * PEAK), bytes_accessed=0, transcendentals=0
        ),
    )


def shaped(shape, dtype):
    return jax.ShapeDtypeStruct(shape, dtype)


class Pieces:
    def __init__(self, dp, shard):
        self.dp = dp
        self.shard_rows, self.shard_cols = shard.shape
        self.parts = []
        self.split = True

    def whole(self, key):
        self.split = False
        self.parts.append((key, None, None, None, 0, None, None))
        return self

    def add(self, stage, layout, rows):
        where = {(0, 0): (0, 0), (1, 0): (0, 1), (0, 1): (1, 0), (2, 1): (1, 1)}
        where.update({(2, 0): (2, 0), (3, 0): (2, 1), (1, 1): (3, 0), (3, 1): (3, 1)})
        for core in (0, 1):
            for way in range(4):
                for side, src_row, low, count, plane, col in layout:
                    array, second = where[way, side]
                    key = (stage, array, core)
                    src = src_row + second * rows
                    self.parts.append((key, src, low, count, plane, 2 * way | core, col))
        return self

    def of(self, picks):
        out = Pieces.__new__(Pieces)
        out.__dict__.update(self.__dict__)
        out.parts = [p for p in self.parts if not self.split or p[5] >> 1 in picks]
        return out

    def keys(self):
        return sorted({part[0] for part in self.parts})

    def planes(self):
        return sorted({part[4] for part in self.parts})

    def columns(self, place, plane):
        if not self.split:
            return 0, self.shard_cols * self.dp
        across = lax.rem(place[0] + plane, self.dp)
        return pl.multiple_of(across * self.shard_cols, 128), self.shard_cols

    def copies(self, refs, dst, sems, base, place, plane=None, paired=False):
        out = []
        for key, src_row, low, count, at, flip, col in self.parts:
            if plane is not None and at != plane:
                continue
            if not self.split:
                out.append(pltpu.make_async_copy(refs[key], dst, sems.at[base + len(out)]))
                continue
            owner = jnp.bitwise_xor(place[1], flip)
            if paired:
                owner = jnp.bitwise_and(owner, 1)
            row = pl.multiple_of(owner * self.shard_rows + low, 16)
            column, cols = self.columns(place, at)
            out.append(
                pltpu.make_async_copy(
                    refs[key].at[pl.ds(src_row, count), pl.ds(col, cols)],
                    dst.at[pl.ds(row, count), pl.ds(column, cols)],
                    sems.at[base + len(out)],
                )
            )
        return out


def position():
    return lax.axis_index("dp"), lax.axis_index("fsdp")


def start(copies):
    for c in copies:
        c.start()


def wait(copies):
    for c in copies:
        c.wait()


def after(value, *others):
    return lax.optimization_barrier((value, *others))[0]


def flip(value, mask, size):
    return lax.ppermute(value, "fsdp", [(i, i ^ mask) for i in range(size)])


class Spread:
    def __init__(self, low, high, size):
        self.size = size
        self.halves = low, high
        self.first = flip(low, 2, size), flip(high, 4, size)

    def second(self, *others):
        self.arrays = [
            jnp.concatenate([half, after(came, *others)], axis=0)
            for half, came in zip(self.halves, self.first)
        ]
        self.arrays.append(flip(self.arrays[0], 4, self.size))
        self.arrays.append(flip(self.arrays[1], 2, self.size))

    def put(self, arrays, stage, which, *others):
        for k in which:
            arrays[stage, k, 0] = self.arrays[k]
            arrays[stage, k, 1] = flip(after(self.arrays[k], *others), 1, self.size)


def packed(value, rows):
    return jnp.concatenate(
        [value[k : k + rows] for k in range(0, value.shape[0], rows)], axis=1
    )


def halves(planes, shard_rows):
    total = shard_rows * len(planes)
    middle = total // 2
    out = []
    for k, plane in enumerate(planes):
        for side, (first, last) in enumerate(((0, middle), (middle, total))):
            low, high = max(first, k * shard_rows), min(last, (k + 1) * shard_rows)
            if low < high:
                out.append((side, low - first, low - k * shard_rows, high - low, plane))
    return out


def cut(shards, layout):
    return [
        jnp.concatenate(
            [shards[p][low : low + count] for s, _, low, count, p in layout if s == side], axis=0
        )
        for side in (0, 1)
    ]


def from_planes(value, dp, *others):
    planes = after(lax.all_gather(value, "dp", axis=0, tiled=False), *others)
    here = lax.axis_index("dp")
    return {
        j: lax.dynamic_index_in_dim(planes, lax.rem(here + j, dp), 0, keepdims=False)
        for j in range(1, dp)
    }


def prefix_body(
    prefix, lengths, table, inner_w, inner_b, outer_w, outer_b, bias_o, hidden_o, keys_o, values_o, ones_o
):
    rows, length, _ = bias_o.shape
    for row in range(rows):
        key = lax.broadcasted_iota(jnp.int32, (length, length), 0)
        query = lax.broadcasted_iota(jnp.int32, (length, length), 1)
        key_seg = jnp.zeros((length, length), jnp.int32)
        query_seg = jnp.zeros((length, length), jnp.int32)
        bound = 0
        for s in range(lengths.shape[1]):
            bound = bound + lengths[row, s]
            key_seg = key_seg + jnp.where(key >= bound, 1, 0)
            query_seg = query_seg + jnp.where(query >= bound, 1, 0)
        seen = (key_seg == query_seg) & (key <= query)
        bias_o[row] = jnp.where(seen, 0.0, MASKED)
    width = keys_o.shape[1]
    hidden = jnp.tanh(dot(table[...], inner_w[...]) + inner_b[...])
    hidden_o[...] = hidden
    pairs = (dot(hidden.astype(BF16), outer_w[...]) + outer_b[...]).astype(BF16).astype(F32)
    shape = keys_o.shape
    row = lax.broadcasted_iota(jnp.int32, shape, 0)
    col = lax.broadcasted_iota(jnp.int32, shape, 1)
    inside = (row // PAD) == (col // HEAD)
    real = inside & (lax.rem(row, PAD) < prefix)
    heads = shape[0] // PAD
    keys_o[...] = jnp.where(real, jnp.tile(pairs[:, :width], (heads, 1)), 0.0).astype(BF16)
    values_o[...] = jnp.where(real, jnp.tile(pairs[:, width:], (heads, 1)), 0.0).astype(BF16)
    head = lax.broadcasted_iota(jnp.int32, ones_o.shape, 0)
    lane = lax.broadcasted_iota(jnp.int32, ones_o.shape, 1)
    ones_o[...] = jnp.where(head == lane // HEAD, 1.0, 0.0).astype(BF16)


def triple_body(parts, keys, *refs):
    n_arrays = len(keys)
    place = position()
    x, gain, shift = refs[:3]
    arrays = dict(zip(keys, refs[3 : 3 + n_arrays]))
    triple_o, t_o, tv, normed, tri, sems, out_sems = refs[3 + n_arrays :]
    tokens, _ = x.shape
    inward = []
    base = 0
    for plane in parts.planes():
        inward.append((plane, parts.copies(arrays, tv, sems, base, place, plane)))
        base += len(inward[-1][1])
        start(inward[-1][1])
    outs = []

    def send(src, dst):
        outs.append(pltpu.make_async_copy(src, dst, out_sems.at[len(outs)]))
        outs[-1].start()

    step = 128
    for t in range(0, tokens, step):
        u, _ = unit(x[t : t + step, :].astype(F32))
        normed[t : t + step, :] = (u * gain[...] + shift[...]).astype(BF16)
    for plane, copies in inward:
        wait(copies)
        column, count = parts.columns(place, plane)
        block = count if count <= 1024 else 1024
        for n in range(0, count, block):
            cols = pl.ds(column + n, block)
            if not isinstance(column, int):
                cols = pl.ds(pl.multiple_of(column + n, 128), block)
            tri[:, cols] = dot(normed[...], tv[:, cols]).astype(BF16)
            send(tri.at[:, cols], triple_o.at[:, cols])
            send(tv.at[:, cols], t_o.at[:, cols])
    wait(outs)


def attend_body(rows, prefix, parts, keys, *refs):
    n_arrays = len(keys)
    place = position()
    bias, x, out_b, gain, shift, bdk, bdv, triple = refs[:8]
    arrays = dict(zip(keys, refs[8 : 8 + n_arrays]))
    prob_o, pre_o, mix_o, middle_o, norm_o, o_o = refs[8 + n_arrays : 14 + n_arrays]
    (tri, ov, normed, prob, spre, pre, main, mix, middle, sems, out_sems) = refs[14 + n_arrays :]
    tokens, width = x.shape
    length = tokens // rows
    heads = width // HEAD
    scale = HEAD ** (-0.5)
    step = 128
    inward = [
        pltpu.make_async_copy(
            triple.at[pl.ds(row * length, length), :],
            tri.at[pl.ds(row * length, length), :],
            sems.at[row],
        )
        for row in range(rows)
    ]
    start(inward)
    in_o = parts.copies(arrays, ov, sems, rows, place)
    start(in_o)
    outs = []

    def send(src, dst):
        outs.append(pltpu.make_async_copy(src, dst, out_sems.at[len(outs)]))
        outs[-1].start()

    lane = lax.broadcasted_iota(jnp.int32, (length, 2 * HEAD), 1)
    low_lane = lane < HEAD
    for row in range(rows):
        here = slice(row * length, (row + 1) * length)
        inward[row].wait()
        raw = dot_nt(bdk[...], tri[here, :width]) * scale
        pre_row = lax.broadcasted_iota(jnp.int32, raw.shape, 0)
        spre[...] = jnp.where(lax.rem(pre_row, PAD) < prefix, raw, MASKED)
        def columns(m, h):
            low = m * width + h // 2 * 2 * HEAD
            return slice(low, low + 2 * HEAD)

        products, shares, half = {}, {}, {}
        for turn in range(heads + 2):
            h = turn
            if h < heads:
                q = tri[here, columns(0, h)]
                q = jnp.where(low_lane if h % 2 == 0 else ~low_lane, q, jnp.zeros_like(q))
                products[h] = dot_nt(tri[here, columns(1, h)], q)
            h = turn - 1
            if 0 <= h < heads:
                s = products.pop(h) * scale + bias[row]
                sp = spre[h * PAD : (h + 1) * PAD, :]
                top = jnp.maximum(
                    jnp.max(s, axis=0, keepdims=True), jnp.max(sp, axis=0, keepdims=True)
                )
                e = jnp.exp(s - top)
                ep = jnp.exp(sp - top)
                inverse = 1.0 / (
                    jnp.sum(e, axis=0, keepdims=True) + jnp.sum(ep, axis=0, keepdims=True)
                )
                shares[h] = (e * inverse).astype(BF16)
                prob[row * heads + h] = shares[h]
                pre[row, h * PAD : (h + 1) * PAD, :] = (ep * inverse).astype(BF16)
            h = turn - 2
            if h >= 0:
                found = dot_tn(shares.pop(h), tri[here, columns(2, h)])
                if h % 2 == 0:
                    half[h] = found
                    continue
                main[:, columns(0, h)] = jnp.where(low_lane, half.pop(h - 1), found)
                if h % 4 == 3:
                    some = pl.ds(row * heads + h - 3, 4)
                    send(prob.at[some], prob_o.at[some])
        if row == 0:
            wait(in_o)
            send(ov, o_o)
        mix[here, :] = (main[...] + dot_tn(pre[row], bdv[...])).astype(BF16)
        middle[here, :] = x[here, :].astype(F32) + dot(mix[here, :], ov[...]) + out_b[...]
        for t in range(row * length, (row + 1) * length, step):
            u, _ = unit(middle[t : t + step, :])
            normed[t : t + step, :] = (u * gain[...] + shift[...]).astype(BF16)
        send(middle.at[pl.ds(row * length, length), :], middle_o.at[pl.ds(row * length, length), :])
        send(normed.at[pl.ds(row * length, length), :], norm_o.at[pl.ds(row * length, length), :])
    send(pre, pre_o)
    send(mix, mix_o)
    wait(outs)


def upward_body(planes, parts, keys, carried, *refs):
    n_arrays = len(keys)
    place = position()
    norm, bias = refs[:2]
    arrays = dict(zip(keys, refs[2 : 2 + n_arrays]))
    n_arrays += carried
    active_o, slope_o, up_o = refs[2 + n_arrays : 5 + n_arrays]
    uv, active, slope, sems, out_sems = refs[5 + n_arrays :]
    inward = []
    base = 0
    for plane in planes:
        inward.append((plane, parts.copies(arrays, uv, sems, base, place, plane)))
        base += len(inward[-1][1])
        start(inward[-1][1])
    outs = []

    def send(src, dst):
        outs.append(pltpu.make_async_copy(src, dst, out_sems.at[len(outs)]))
        outs[-1].start()

    for plane, copies in inward:
        wait(copies)
        column, count = parts.columns(place, plane)
        block = 512
        for n in range(0, count, block):
            cols = pl.ds(column + n, block)
            if not isinstance(column, int):
                cols = pl.ds(pl.multiple_of(column + n, 128), block)
            u = dot(norm[...], uv[:, cols]) + bias[:, cols]
            square = u * u
            half = 0.5 + 0.5 * jnp.tanh(u * (GELU_C + GELU_C * GELU_A * square))
            active[:, cols] = (u * half).astype(BF16)
            slope[:, cols] = (
                half
                + (u * (half - half * half)) * (2.0 * GELU_C + 6.0 * GELU_C * GELU_A * square)
            ).astype(BF16)
            send(active.at[:, cols], active_o.at[:, cols])
            send(slope.at[:, cols], slope_o.at[:, cols])
            send(uv.at[:, cols], up_o.at[:, cols])
    wait(outs)


class Chunk:
    def __init__(self, place, pick, parts, arrays, full, held, slot, sems, base):
        active, slope, upward = full
        self.dv, self.uc, self.ac, self.sc, self.gu = (h.at[slot] for h in held)
        size = self.uc.shape[1]
        self.split = parts.split
        if not parts.split:
            cols = rows = pl.ds(pick * size, size)
            (whole,) = arrays.values()
            self.down = [pltpu.make_async_copy(whole.at[rows, :], self.dv, sems.at[base])]
        else:
            at = jnp.bitwise_xor(lax.shift_right_logical(place[1], 1), pick)
            self.down = parts.of((pick,)).copies(
                arrays, self.dv, sems, base, place, paired=True
            )
            self.planes, self.shard_rows = parts.dp, parts.shard_rows
            cols = pl.ds(pl.multiple_of(at * size, size), size)
        base += len(self.down)
        self.sems = len(self.down) + 3
        self.rest = [
            pltpu.make_async_copy(slope.at[:, cols], self.sc, sems.at[base]),
            pltpu.make_async_copy(upward.at[:, cols], self.uc, sems.at[base + 1]),
            pltpu.make_async_copy(active.at[:, cols], self.ac, sems.at[base + 2]),
        ]

    def blocks(self):
        rows = self.shard_rows
        size = self.uc.shape[1]
        count = size // (2 * rows)
        return [(k, (k * rows, size // 2 + k * rows)) for k in range(count)]

    def upstream(self, g):
        wait(self.down)
        self.rest[0].wait()
        size = self.uc.shape[1]
        if not self.split:
            for n in range(0, size, 512):
                cols = slice(n, n + 512)
                value = dot_nt(g[...], self.dv[cols, :])
                self.gu[:, cols] = (value * self.sc[:, cols].astype(F32)).astype(BF16)
            return
        width = g.shape[1] // self.planes
        rows = self.shard_rows
        for k, places in self.blocks():
            value = 0.0
            for z in range(self.planes):
                at = z * self.dv.shape[1] // self.planes + k * width
                value = value + dot_nt(g[:, z * width : (z + 1) * width], self.dv[:, at : at + width])
            for n, low in enumerate(places):
                cols = slice(low, low + rows)
                part = value[:, n * rows : (n + 1) * rows]
                self.gu[:, cols] = (part * self.sc[:, cols].astype(F32)).astype(BF16)

    def back(self):
        self.rest[1].wait()
        return lambda cols: dot_nt(self.gu[...], self.uc[cols, :])

    def ahead(self):
        self.rest[2].wait()
        if not self.split:
            return lambda cols: dot(self.ac[...], self.dv[:, cols])
        rows = self.shard_rows

        def term(cols):
            width = self.uc.shape[0] // self.planes
            found = []
            for z in range(cols.start // width, cols.stop // width):
                value = 0.0
                for k, places in self.blocks():
                    at = z * self.dv.shape[1] // self.planes + k * width
                    left = jnp.concatenate([self.ac[:, low : low + rows] for low in places], axis=1)
                    value = value + dot(left, self.dv[:, at : at + width])
                found.append(value)
            return jnp.concatenate(found, axis=1)

        return term


def middle_body(rows, picks, parts, keys, *refs):
    n_arrays = len(keys)
    place = position()
    g, active, slope, upward = refs[:4]
    arrays = dict(zip(keys, refs[4 : 4 + n_arrays]))
    middle_i, gain2, down_b, output_w, mix, triple, pre, bdv, ones = refs[
        4 + n_arrays : 13 + n_arrays
    ]
    result_o, gmid_o, gmix_o, delta_o, dspre_o, pairs_o = refs[13 + n_arrays : 19 + n_arrays]
    mix_i, pre_i, bdv_i, ones_i, g_i = mix, pre, bdv, ones, g
    (dv, uc, ac, sc, gu, second, middle, ov, low, gmix, q, result) = refs[
        19 + n_arrays : 31 + n_arrays
    ]
    mix, pre, bdv, ones, g, sems, io_sems = refs[31 + n_arrays :]
    tokens, width = g.shape
    g_copy = pltpu.make_async_copy(g_i, g, io_sems.at[12])
    g_copy.start()
    length = tokens // rows
    heads = width // HEAD
    scale = HEAD ** (-0.5)
    chunks = []
    base = 0
    for k, pick in enumerate(picks):
        chunks.append(
            Chunk(
                place, pick, parts, arrays, (active, slope, upward), (dv, uc, ac, sc, gu), k, sems, base
            )
        )
        base += chunks[-1].sems
    for chunk in chunks:
        start(chunk.down)
        start(chunk.rest[:1])
    for k in (1, 2):
        for chunk in chunks:
            start(chunk.rest[k : k + 1])
    carried = [
        pltpu.make_async_copy(middle_i, middle, io_sems.at[2]),
        pltpu.make_async_copy(output_w, ov, io_sems.at[3]),
        pltpu.make_async_copy(triple.at[:, pl.ds(0, width)], q, io_sems.at[4]),
        pltpu.make_async_copy(mix_i, mix, io_sems.at[8]),
        pltpu.make_async_copy(pre_i, pre, io_sems.at[9]),
        pltpu.make_async_copy(bdv_i, bdv, io_sems.at[10]),
        pltpu.make_async_copy(ones_i, ones, io_sems.at[11]),
    ]
    start(carried)
    g_copy.wait()
    for chunk in chunks:
        chunk.upstream(g)
    back = [chunk.back() for chunk in chunks]
    ahead = [chunk.ahead() for chunk in chunks]
    wait(carried)
    for n in range(0, width, 512):
        cols = slice(n, n + 512)
        value = back[0](cols)
        for term in back[1:]:
            value = value + term(cols)
        second[:, cols] = value
    done = []

    def send(src, dst):
        done.append(pltpu.make_async_copy(src, dst, io_sems.at[5 + len(done)]))
        done[-1].start()

    step = length // 2
    block = width // (2 * rows)
    for n, t in enumerate(range(0, tokens, step)):
        cols = slice(n * block, (n + 1) * block)
        value = middle[:, cols] + down_b[:, cols]
        for term in ahead:
            value = value + term(cols)
        result[:, cols] = value.astype(BF16)
        here = slice(t, t + step)
        u, scaled = unit(middle[here, :])
        gm = g[here, :].astype(F32) + norm_back(second[here, :] * gain2[...], u, scaled)
        second[here, :] = gm
        low[here, :] = gm.astype(BF16)
        if n % 2 == 1:
            here = slice(n // 2 * length, (n // 2 + 1) * length)
            gmix[here, :] = dot_nt(low[here, :], ov[...]).astype(BF16)
    send(result, result_o)
    send(second, gmid_o)
    send(gmix, gmix_o)
    keys = 0.0
    values = 0.0
    for row in range(rows):
        here = slice(row * length, (row + 1) * length)
        up = gmix[here, :]
        product = up.astype(F32) * mix[here, :].astype(F32)
        high = product.astype(BF16)
        small = (product - high.astype(F32)).astype(BF16)
        delta = dot_nt(ones[...], high) + dot_nt(ones[...], small)
        delta_o[row] = delta
        each = jnp.broadcast_to(delta[:, None, :], (heads, PAD, length)).reshape(-1, length)
        p = pre[row]
        ds = (p.astype(F32) * (dot_nt(bdv[...], up) - each)).astype(BF16)
        dspre_o[row] = ds
        keys = keys + dot(ds, q[here, :])
        values = values + dot(p, up)
    row = lax.broadcasted_iota(jnp.int32, keys.shape, 0)
    col = lax.broadcasted_iota(jnp.int32, keys.shape, 1)
    inside = (row // PAD) == (col // HEAD)
    keys = jnp.where(inside, keys * scale, 0.0).reshape(heads, PAD, width)
    values = jnp.where(inside, values, 0.0).reshape(heads, PAD, width)
    prefix = pairs_o.shape[0] // 4
    for k, value in enumerate((jnp.sum(keys, axis=0), jnp.sum(values, axis=0))):
        for n in (0, 1):
            part = value[:prefix, n * width // 2 : (n + 1) * width // 2]
            pairs_o[(2 * k + n) * prefix : (2 * k + n + 1) * prefix, :] = part
    wait(done)


def attend_back_body(row, length, heads, triple, gmix, prob, delta, dspre_i, bdk_i, *refs):
    out_o, tri, up, p, before, out, dspre, bdk, sems = refs
    width = heads * HEAD
    scale = HEAD ** (-0.5)
    here = pl.ds(row * length, length)
    groups = 4
    span = heads // groups
    inward = []
    for n in range(groups):
        cols = pl.ds(n * span * HEAD, span * HEAD)
        copies = [
            pltpu.make_async_copy(
                triple.at[here, pl.ds(m * width + n * span * HEAD, span * HEAD)],
                tri.at[:, pl.ds(m * width + n * span * HEAD, span * HEAD)],
                sems.at[5 * n + m],
            )
            for m in range(3)
        ]
        copies.append(pltpu.make_async_copy(gmix.at[here, cols], up.at[:, cols], sems.at[5 * n + 3]))
        copies.append(
            pltpu.make_async_copy(
                prob.at[pl.ds(row * heads + n * span, span)],
                p.at[pl.ds(n * span, span)],
                sems.at[5 * n + 4],
            )
        )
        start(copies)
        inward.append(copies)
        if n == 0:
            side = [
                pltpu.make_async_copy(dspre_i.at[row], dspre, sems.at[32]),
                pltpu.make_async_copy(bdk_i, bdk, sems.at[33]),
            ]
            start(side)
    low_lane = lax.broadcasted_iota(jnp.int32, (length, 2 * HEAD), 1) < HEAD
    wait(side)
    before[...] = dot_tn(dspre[...], bdk[...])
    done = []

    def columns(m, h):
        low = m * width + h // 2 * 2 * HEAD
        return slice(low, low + 2 * HEAD)

    def own(value, h):
        return jnp.where(low_lane if h % 2 == 0 else ~low_lane, value, jnp.zeros_like(value))

    lead = 2
    upstream, scores, half = {}, {}, {}
    for turn in range(heads + 2 * lead):
        h = turn
        if h < heads:
            if h % span == 0:
                wait(inward[h // span])
            upstream[h] = dot_nt(tri[:, columns(2, h)], own(up[:, columns(0, h)], h))
        h = turn - lead
        if 0 <= h < heads:
            d = delta[row, h : h + 1, :]
            scores[h] = (p[h].astype(F32) * (upstream.pop(h) - d)).astype(BF16)
        h = turn - 2 * lead
        if 0 <= h < heads:
            ds = scores.pop(h)
            found = (
                dot_tn(ds, own(tri[:, columns(1, h)], h)),
                dot(ds, own(tri[:, columns(0, h)], h)),
                dot(p[h], own(up[:, columns(0, h)], h)),
            )
            if h % 2 == 0:
                half[h] = found
                continue
            queries, keys, values = (a + b for a, b in zip(half.pop(h - 1), found))
            out[:, columns(0, h)] = ((queries + before[:, columns(0, h)]) * scale).astype(BF16)
            out[:, columns(1, h)] = (keys * scale).astype(BF16)
            out[:, columns(2, h)] = values.astype(BF16)
            if (h + 1) % span == 0:
                for m in range(3):
                    at = pl.ds(m * width + (h + 1 - span) * HEAD, span * HEAD)
                    done.append(
                        pltpu.make_async_copy(
                            out.at[:, at], out_o.at[:, at], sems.at[5 * groups + len(done)]
                        )
                    )
                    done[-1].start()
    wait(done)


def input_body(rows, *refs):
    grads = refs[:rows]
    triple_w, x_i, gain1, gmid_i, result_o, tv, gv, first, gmid, x, result, sems = refs[rows:]
    tokens, width = x.shape
    length = tokens // rows
    inward = []
    cuts = [(0, width // 2), (width // 2, width), (width, 2 * width), (2 * width, 3 * width)]
    for n, (low, high) in enumerate(cuts):
        cols = pl.ds(low, high - low)
        copies = [
            pltpu.make_async_copy(triple_w.at[:, cols], tv.at[:, cols], sems.at[n * (rows + 1)])
        ]
        for row in range(rows):
            copies.append(
                pltpu.make_async_copy(
                    grads[row].at[:, cols],
                    gv.at[pl.ds(row * length, length), cols],
                    sems.at[n * (rows + 1) + 1 + row],
                )
            )
        start(copies)
        inward.append(copies)
    late = [
        pltpu.make_async_copy(x_i, x, sems.at[4 * (rows + 1)]),
        pltpu.make_async_copy(gmid_i, gmid, sems.at[4 * (rows + 1) + 1]),
    ]
    start(late)
    for n in range(3):
        wait(inward[n])
        cols = slice(*cuts[n])
        for m in range(0, width, 512):
            value = dot_nt(gv[:, cols], tv[m : m + 512, cols])
            first[:, m : m + 512] = value if n == 0 else first[:, m : m + 512] + value
    wait(inward[3])
    wait(late)
    step = 128
    done = []
    last = slice(2 * width, 3 * width)
    for row in range(rows):
        here = slice(row * length, (row + 1) * length)
        first[here, :] = first[here, :] + dot_nt(gv[here, last], tv[:, last])
        for t in range(row * length, (row + 1) * length, step):
            now = slice(t, t + step)
            u, scaled = unit(x[now, :].astype(F32))
            back = norm_back(first[now, :] * gain1[...], u, scaled)
            result[now, :] = (gmid[now, :] + back).astype(BF16)
        at = pl.ds(row * length, length)
        done.append(pltpu.make_async_copy(result.at[at, :], result_o.at[at, :], sems.at[4 * (rows + 1) + 2 + row]))
        done[-1].start()
    wait(done)


def split3(value):
    high = value.astype(BF16)
    rest = value - high.astype(F32)
    mid = rest.astype(BF16)
    return high, mid, (rest - mid.astype(F32)).astype(BF16)


def reparam_body(prefix, pairs, hidden_r, table, inner_w, outer_w, *refs):
    table_o, inner_wo, inner_bo, outer_wo, outer_bo, outer_g, inner_g, sems = refs
    width = 2 * pairs.shape[1]
    hidden = hidden_r[...]
    low = jnp.concatenate([hidden.astype(BF16)] * 3, axis=0)
    row = lax.broadcasted_iota(jnp.int32, (PAD, hidden.shape[1]), 0)
    grads = []
    done = []
    for k in (0, 1):
        value = jnp.concatenate(
            [pairs[(2 * k + n) * prefix : (2 * k + n + 1) * prefix, :] for n in (0, 1)], axis=1
        )
        value = jnp.concatenate([value, jnp.zeros((PAD - prefix, width), F32)], axis=0)
        parts = jnp.concatenate(split3(value), axis=0)
        cols = slice(k * width, (k + 1) * width)
        outer_g[:, cols] = dot_tn(low, parts)
        at = pl.ds(k * width, width)
        done.append(pltpu.make_async_copy(outer_g.at[:, at], outer_wo.at[:, at], sems.at[k]))
        done[-1].start()
        outer_bo[:, cols] = jnp.sum(value, axis=0, keepdims=True)
        grads.append(dot_nt(parts, outer_w[:, cols]))
    total = grads[0] + grads[1]
    hidden_grad = total[:PAD] + total[PAD : 2 * PAD] + total[2 * PAD :]
    before = jnp.where(row < prefix, hidden_grad * (1.0 - hidden * hidden), 0.0)
    inner_bo[...] = jnp.sum(before, axis=0, keepdims=True)
    stacked = jnp.concatenate(split3(before), axis=0)
    inner_g[...] = dot_tn(jnp.concatenate([table[...]] * 3, axis=0), stacked)
    done.append(pltpu.make_async_copy(inner_g, inner_wo, sems.at[2]))
    done[-1].start()
    back = dot_nt(stacked, inner_w[...])
    table_o[...] = back[:PAD] + back[PAD : 2 * PAD] + back[2 * PAD :]
    wait(done)


def total_pairs(pairs, fsdp, dp):
    if fsdp == 8 and dp == 4:
        rounds = [("fsdp", (1,)), ("fsdp", (2, 4, 6)), ("dp", (1, 2, 3))]
    else:
        rounds = [("fsdp", (1 << k,)) for k in range(fsdp.bit_length() - 1)]
        rounds += [("dp", (1 << k,)) for k in range(dp.bit_length() - 1)]
    sizes = {"fsdp": fsdp, "dp": dp}
    for axis, masks in rounds:
        size = sizes[axis]
        terms = {0: pairs}
        for mask in masks:
            terms[mask] = lax.ppermute(pairs, axis, [(i, i ^ mask) for i in range(size)])
        if len(masks) == 1:
            pairs = terms[0] + terms[masks[0]]
        else:
            low = min(masks)
            pairs = (terms[0] + terms[low]) + (terms[2 * low] + terms[3 * low])
    return pairs


def body(
    fsdp,
    dp,
    activations,
    lengths,
    cotangent,
    gain_first,
    shift_first,
    triple_weight,
    output_weight,
    output_bias,
    gain_second,
    shift_second,
    upward_weight,
    upward_bias,
    downward_weight,
    downward_bias,
    prefix_table,
    inner_weight,
    inner_bias,
    outer_weight,
    outer_bias,
):
    rows, length, width = activations.shape
    tokens = rows * length
    heads = width // HEAD
    wide = upward_bias.shape[0]
    prefix, _ = prefix_table.shape
    mid = inner_bias.shape[0]
    chunk = wide // 4
    x = activations.reshape(tokens, width)
    g = cotangent.reshape(tokens, width)
    flat = lambda v: v.reshape(1, -1)
    dma = lambda n: pltpu.SemaphoreType.DMA((n,))
    vm = pltpu.VMEM

    table = jnp.pad(prefix_table, ((0, PAD - prefix), (0, 0)))
    bias, hidden, bdk, bdv, ones = call(
        partial(prefix_body, prefix),
        "prefix",
        [(shaped((rows, length, length), F32), VMEM), (shaped((PAD, mid), F32), VMEM)]
        + [(shaped((heads * PAD, width), BF16), VMEM)] * 2
        + [(shaped((heads, width), BF16), VMEM)],
        [SMEM] + [VMEM] * 5,
        [],
        3.7,
    )(lengths, table, inner_weight, flat(inner_bias), outer_weight, flat(outer_bias))

    arrays = {}
    quick = fsdp == 8 and dp > 1
    triple_parts = Pieces(dp, triple_weight)
    output_parts = Pieces(dp, output_weight)
    up_parts = Pieces(dp, upward_weight)
    down_parts = Pieces(dp, packed(downward_weight, triple_weight.shape[0]))
    if quick:
        cut_rows, triple_c = triple_weight.shape
        blocks = downward_weight.shape[0] // cut_rows
        far = list(range(1, dp))
        layout = halves(far, cut_rows)
        near_rows = cut_rows + cut_rows // 2
        far_rows = cut_rows * (dp - 1) // 2
        half = cut_rows // 2
        triple_parts.add("near", [(0, 0, 0, cut_rows, 0, 0)], near_rows)
        triple_parts.add("first", [part + (0,) for part in layout], far_rows)
        output_parts.add("near", [(0, 0, 0, cut_rows, 0, triple_c)], near_rows)
        output_parts.add("first", [part + (triple_c,) for part in layout], far_rows)
        up_parts.add("near", [(1, 0, 0, cut_rows, 0, 0)], near_rows)
        up_parts.add("up", [part + (0,) for part in layout], far_rows)
        down_parts.add("near", [(side, cut_rows, side * half, half, 0, 0) for side in (0, 1)], near_rows)
        down_parts.add("down", [part + (0,) for part in layout], far_rows)

        head = jnp.concatenate([triple_weight, output_weight], axis=1)
        beside = packed(downward_weight, cut_rows)
        near = Spread(
            jnp.concatenate([head, beside[:half]], axis=0),
            jnp.concatenate([upward_weight, beside[half:]], axis=0),
            fsdp,
        )
        near.second(bdk)
        near.put(arrays, "near", range(4))
        first_cut = tuple(cut(from_planes(head, dp), layout))
        first = Spread(*after(first_cut, *near.arrays[2:]), fsdp)
        first.second()
        first.put(arrays, "first", (0, 1))
        up_far = from_planes(after(upward_weight, head), dp, *first.arrays[:2])
        up = Spread(*cut(up_far, layout), fsdp)
        first.put(arrays, "first", (2, 3), *up.first)
        up.second()
        up.put(arrays, "up", (0, 1))
        x = after(x, *up.arrays[:2])
    else:
        whole = (
            (triple_weight, triple_parts),
            (output_weight, output_parts),
            (upward_weight, up_parts),
            (downward_weight, down_parts),
        )
        for k, (weight, parts) in enumerate(whole):
            gathered = lax.all_gather(weight, "fsdp", axis=0, tiled=True)
            arrays["whole", k] = lax.all_gather(gathered, "dp", axis=1, tiled=True)
            parts.whole(("whole", k))

    keys = triple_parts.keys()
    triple, triple_full = call(
        partial(triple_body, triple_parts, keys),
        "triple",
        [(shaped((tokens, 3 * width), BF16), ANY), (shaped((width, 3 * width), BF16), ANY)],
        [VMEM] * 3 + [ANY] * len(keys),
        [
            vm((width, 3 * width), BF16),
            vm((tokens, width), BF16),
            vm((tokens, 3 * width), BF16),
            dma(len(triple_parts.parts)),
            dma(2 * len(triple_parts.planes()) + 4),
        ],
        0.1,
    )(x, flat(gain_first), flat(shift_first), *[arrays[key] for key in keys])
    if quick:
        down_far = from_planes(after(beside, upward_weight), dp, triple)
        down = Spread(*cut(down_far, layout), fsdp)
        triple = after(triple, *down.halves)
    keys = output_parts.keys()
    prob, pre, mix, middle, norm_two, output_full = call(
        partial(attend_body, rows, prefix, output_parts, keys),
        "attend",
        [
            (shaped((rows * heads, length, length), BF16), ANY),
            (shaped((rows, heads * PAD, length), BF16), ANY),
            (shaped((tokens, width), BF16), ANY),
            (shaped((tokens, width), F32), ANY),
            (shaped((tokens, width), BF16), ANY),
            (shaped((width, width), BF16), ANY),
        ],
        [VMEM] * 7 + [ANY] * (1 + len(keys)),
        [
            vm((tokens, 3 * width), BF16),
            vm((width, width), BF16),
            vm((tokens, width), BF16),
            vm((rows * heads, length, length), BF16),
            vm((heads * PAD, length), F32),
            vm((rows, heads * PAD, length), BF16),
            vm((length, width), F32),
            vm((tokens, width), BF16),
            vm((tokens, width), F32),
            dma(rows + len(output_parts.parts)),
            dma(3 + rows * (2 + heads // 4)),
        ],
        10,
    )(
        bias,
        x,
        flat(output_bias),
        flat(gain_second),
        flat(shift_second),
        bdk,
        bdv,
        triple,
        *[arrays[key] for key in keys],
    )

    if quick:
        up.put(arrays, "up", (2, 3), norm_two)
        down.second(norm_two)
        down.put(arrays, "down", (0, 1))
        norm_two = after(norm_two, *down.arrays[:2])
    keys = up_parts.keys()
    state = []
    planes = up_parts.planes()
    cuts = [planes]
    for k, some in enumerate(cuts):
        state = call(
            partial(upward_body, some, up_parts, keys, len(state)),
            "upward_%d" % k,
            [
                (shaped((tokens, wide), BF16), ANY),
                (shaped((tokens, wide), BF16), ANY),
                (shaped((width, wide), BF16), ANY),
            ],
            [VMEM] * 2 + [ANY] * (len(keys) + len(state)),
            [
                vm((width, wide), BF16),
                vm((tokens, wide), BF16),
                vm((tokens, wide), BF16),
                dma(len(up_parts.parts)),
                dma(3 * wide // 512),
            ],
            16 / len(cuts),
            aliases={2 + len(keys) + n: n for n in range(len(state))},
        )(norm_two, flat(upward_bias), *[arrays[key] for key in keys], *state)
    active, slope, up_full = state

    down_shape = (chunk, width)
    if quick:
        down_shape = (2 * cut_rows, dp * blocks * width // dp)

    def chunk_scratch(count):
        return [
            vm((count, *down_shape), BF16),
            vm((count, width, chunk), BF16),
            vm((count, tokens, chunk), BF16),
            vm((count, tokens, chunk), BF16),
            vm((count, tokens, chunk), BF16),
            vm((tokens, width), F32),
        ]

    n_sems = len(down_parts.parts) + 16

    if quick:
        down.put(arrays, "down", (2, 3), active)
    keys = down_parts.keys()
    result, g_middle, g_mix, delta, d_pre, pairs = call(
        partial(middle_body, rows, (0, 1, 2, 3), down_parts, keys),
        "middle",
        [
            (shaped((tokens, width), BF16), ANY),
            (shaped((tokens, width), F32), ANY),
            (shaped((tokens, width), BF16), ANY),
            (shaped((rows, heads, length), F32), VMEM),
            (shaped((rows, heads * PAD, length), BF16), VMEM),
            (shaped((4 * prefix, width // 2), F32), VMEM),
        ],
        [ANY] * (4 + len(keys)) + [ANY] + [VMEM] * 2 + [ANY] * 6,
        chunk_scratch(4)
        + [
            vm((tokens, width), F32),
            vm((width, width), BF16),
            vm((tokens, width), BF16),
            vm((tokens, width), BF16),
            vm((tokens, width), BF16),
            vm((tokens, width), BF16),
            vm((tokens, width), BF16),
            vm((rows, heads * PAD, length), BF16),
            vm((heads * PAD, width), BF16),
            vm((heads, width), BF16),
            vm((tokens, width), BF16),
            dma(n_sems),
            dma(13),
        ],
        28,
    )(
        g,
        active,
        slope,
        up_full,
        *[arrays[key] for key in keys],
        middle,
        flat(gain_second),
        flat(downward_bias),
        output_full,
        mix,
        triple,
        pre,
        bdv,
        ones,
    )

    grads = []
    for row in range(rows):
        grads += call(
            partial(attend_back_body, row, length, heads),
            "attend_back_%d" % row,
            [(shaped((length, 3 * width), BF16), ANY)],
            [ANY] * 3 + [VMEM] + [ANY] * 2,
            [
                vm((length, 3 * width), BF16),
                vm((length, width), BF16),
                vm((heads, length, length), BF16),
                vm((length, width), F32),
                vm((length, 3 * width), BF16),
                vm((heads * PAD, length), BF16),
                vm((heads * PAD, width), BF16),
                dma(34),
            ],
            8.5,
            room=12,
        )(triple, g_mix, prob, delta, d_pre, bdk)

    (input_grad,) = call(
        partial(input_body, rows),
        "input",
        [(shaped((tokens, width), BF16), ANY)],
        [ANY] * rows + [ANY] * 2 + [VMEM] + [ANY],
        [
            vm((width, 3 * width), BF16),
            vm((tokens, 3 * width), BF16),
            vm((tokens, width), F32),
            vm((tokens, width), F32),
            vm((tokens, width), BF16),
            vm((tokens, width), BF16),
            dma(4 * (rows + 1) + 2 + rows),
        ],
        9,
        room=12,
    )(*grads, triple_full, x, flat(gain_first), g_middle)

    pairs = total_pairs(pairs, fsdp, dp)
    table_grad, inner_w_grad, inner_b_grad, outer_w_grad, outer_b_grad = call(
        partial(reparam_body, prefix),
        "reparam",
        [
            (shaped((PAD, width), F32), VMEM),
            (shaped((width, mid), F32), ANY),
            (shaped((1, mid), F32), VMEM),
            (shaped((mid, 2 * width), F32), ANY),
            (shaped((1, 2 * width), F32), VMEM),
        ],
        [VMEM] * 5,
        [vm((mid, 2 * width), F32), vm((width, mid), F32), dma(3)],
        6,
        room=10,
    )(pairs, hidden, table, inner_weight, outer_weight)
    return (
        result.reshape(rows, length, width),
        input_grad.reshape(rows, length, width),
        table_grad[:prefix],
        inner_w_grad,
        inner_b_grad.reshape(-1),
        outer_w_grad,
        outer_b_grad.reshape(-1),
    )


def solution(mesh):
    in_specs = (
        P(("dp", "fsdp"), None, None),
        P(("dp", "fsdp"), None),
        P(("dp", "fsdp"), None, None),
        P(),
        P(),
        P("fsdp", "dp"),
        P("fsdp", "dp"),
        P(),
        P(),
        P(),
        P("fsdp", "dp"),
        P(),
        P("fsdp", "dp"),
        P(),
        P(),
        P(),
        P(),
        P(),
        P(),
    )
    out_specs = (
        P(("dp", "fsdp"), None, None),
        P(("dp", "fsdp"), None, None),
        P(),
        P(),
        P(),
        P(),
        P(),
    )
    return jax.shard_map(
        partial(body, mesh.shape["fsdp"], mesh.shape["dp"]),
        mesh=mesh,
        in_specs=in_specs,
        out_specs=out_specs,
        check_vma=False,
    )
```
